128 devices in a mesh: dp: 8 (over x, core), ctx: 16 (over y, z).
Axes of the slice: x: 4, y: 4, z: 4, core: 2. Of those that a mesh axis runs over, the one named last changes fastest.
Arguments:
- tokens: bfloat16 [8, 2048, 576], P('dp', 'ctx'), may hold values from -6 to 6
- positions: int32 [8, 2048], P('dp', 'ctx'), may hold values from 0 to 2047, as said below
- cotangent: bfloat16 [8, 2048, 576], P('dp', 'ctx'), may hold values from -6 to 6
- w_square: float32 [2, 576, 576], P(None, 'ctx'), may hold values from -1 to 1
- w_kv: float32 [2, 576, 192], P(None, 'ctx'), may hold values from -1 to 1
- w_gate_up: float32 [2, 1536, 576], P(None, 'ctx'), may hold values from -0.25 to 0.25
- w_down: float32 [1536, 576], P('ctx'), may hold values from -0.15625 to 0.15625
- gains: float32 [2, 576], P(None, 'ctx'), may hold values from 0.5 to 1.5
- mom_square: float32 [2, 576, 576], P(None, 'ctx'), may hold values from -224 to 224
- mom_kv: float32 [2, 576, 192], P(None, 'ctx'), may hold values from -224 to 224
- mom_gate_up: float32 [2, 1536, 576], P(None, 'ctx'), may hold values from -224 to 224
- mom_down: float32 [1536, 576], P('ctx'), may hold values from -224 to 224
- mom_gains: float32 [2, 576], P(None, 'ctx')
Outputs:
- out: bfloat16 [8, 2048, 576], P('dp', 'ctx')
- grad_input: bfloat16 [8, 2048, 576], P('dp', 'ctx')
- grad_square: float32 [2, 576, 576], P(None, 'ctx')
- grad_kv: float32 [2, 576, 192], P(None, 'ctx')
- grad_gate_up: float32 [2, 1536, 576], P(None, 'ctx')
- grad_down: float32 [1536, 576], P('ctx')
- grad_gains: float32 [2, 576], P(None, 'ctx')
- next_square: float32 [2, 576, 576], P(None, 'ctx')
- next_kv: float32 [2, 576, 192], P(None, 'ctx')
- next_gate_up: float32 [2, 1536, 576], P(None, 'ctx')
- next_down: float32 [1536, 576], P('ctx')
- next_gains: float32 [2, 576], P(None, 'ctx')
- new_square: float32 [2, 576, 576], P(None, 'ctx')
- new_kv: float32 [2, 576, 192], P(None, 'ctx')
- new_gate_up: float32 [2, 1536, 576], P(None, 'ctx')
- new_down: float32 [1536, 576], P('ctx')
- new_gains: float32 [2, 576], P(None, 'ctx')
The draws below stay inside these ranges and needn't reach their ends.
Inputs may be any that keep to these rules, and one draw needn't show every extreme that they name: `positions`: in each row a position is 0 (a document begins) or one more than the position before it. Every row has a document that begins within its first 128 tokens and ends within its last 128.
All inputs are finite; a program needn't handle non-finite values.
Results may differ from the reference program's by a relative error of at most 0.029.
Values may be sent and summed in bfloat16 or wider, within the bound.
A program may use at most 192 MiB of HBM per device.

```python
import math
import jax
import jax.numpy as jnp
from jax import lax

D = 576
HEADS = 9
KV_HEADS = 3
HEAD_WIDTH = 64
FF = 1536
TOK_DEV = 128
NS_ITERS = 5
KVD = 192
LENGTH = 2048
SEQS = 8
TOKENS = 16384


def draw_positions(key, part):
    key = jax.random.fold_in(key, 11)
    first_key, second_key, third_key = jax.random.split(key, 3)
    head_length = jax.random.randint(first_key, (SEQS, 1), 1, TOK_DEV)
    tail_length = jax.random.randint(second_key, (SEQS, 1), 1, TOK_DEV)
    whole_row = jax.random.randint(third_key, (), 0, SEQS)
    places = jnp.arange(LENGTH, dtype=jnp.int32)[None, :]
    tail_start = LENGTH - tail_length
    packed = jnp.where(places < head_length, places, jnp.where(places < tail_start, places - head_length, places - tail_start))
    single = jnp.broadcast_to(places, (SEQS, LENGTH))
    row_index = jnp.arange(SEQS, dtype=jnp.int32)[:, None]
    return jnp.where(row_index == whole_row, single, packed).astype(jnp.int32)


def draw_mom_gains(key, part):
    key = jax.random.fold_in(key, 5)
    ramp_rows = jnp.arange(D, dtype=jnp.float32) / (D - 1)
    values = jnp.clip(jax.random.normal(key, (2, D), jnp.float32), -4.0, 4.0)
    ramp_rows = 1.0 + 2.0 * ramp_rows
    return values * ramp_rows[None, :] * (0.3 * TOKENS ** 0.5)


def level_of(rng, dims, cuts, low, top_value):
    def one(axis_at, parts):
        draws = jax.random.uniform(jax.random.fold_in(jax.random.fold_in(rng, 6), axis_at), (parts,), jnp.float32, low / len(cuts), top_value / len(cuts))
        return jnp.repeat(jnp.exp(draws), dims[axis_at] // parts).reshape((-1,) + (1,) * (len(dims) - axis_at - 1))

    factor_of = one(*cuts[0])
    for cut in cuts[1:]:
        factor_of = factor_of * one(*cut)
    return factor_of


def gaussian(key, shape, scale, most, shards=(), held_as=jnp.bfloat16):
    entries = jax.random.normal(key, shape, jnp.float32) * scale
    if len(shards) > 0:
        entries = level_of(key, shape, shards, -0.22, 0.18) * entries
    return jnp.clip(entries, min=-most, max=most).astype(held_as)


def setup_inputs(seed: int = 0) -> dict:
    streams_of = jax.random.split(jax.random.key(seed), 14)
    tokens = gaussian(streams_of[0], (SEQS, LENGTH, D), 1.0, 6.0, ((0, 8), (1, 16)))
    positions = draw_positions(jax.random.fold_in(streams_of[13], 71), 0)
    cotangent = gaussian(streams_of[2], (SEQS, LENGTH, D), 1.0, 6.0, ((0, 8), (1, 16)))
    w_square = gaussian(streams_of[3], (2, D, D), (1.5 / D ** 0.5), 1.0, ((1, 16),), jnp.float32)
    w_kv = gaussian(streams_of[4], (2, D, KVD), (1.5 / D ** 0.5), 1.0, ((1, 16),), jnp.float32)
    w_gate_up = gaussian(streams_of[5], (2, FF, D), D ** -0.5, 0.25, ((1, 16),), jnp.float32)
    w_down = gaussian(streams_of[6], (FF, D), FF ** -0.5, 0.15625, ((0, 16),), jnp.float32)
    gains = jnp.clip(1.0 + 0.1 * jax.random.normal(streams_of[7], (2, D), jnp.float32), 0.5, 1.5)
    mom_square = gaussian(streams_of[8], (2, D, D), (0.3 * TOKENS ** 0.5), 224.0, ((1, 16),), jnp.float32)
    mom_kv = gaussian(streams_of[9], (2, D, KVD), (0.3 * TOKENS ** 0.5), 224.0, ((1, 16),), jnp.float32)
    mom_gate_up = gaussian(streams_of[10], (2, FF, D), (0.3 * TOKENS ** 0.5), 224.0, ((1, 16),), jnp.float32)
    mom_down = gaussian(streams_of[11], (FF, D), (0.3 * TOKENS ** 0.5), 224.0, ((0, 16),), jnp.float32)
    mom_gains = draw_mom_gains(jax.random.fold_in(streams_of[13], 71), 0)
    return {"tokens": tokens, "positions": positions, "cotangent": cotangent, "w_square": w_square, "w_kv": w_kv, "w_gate_up": w_gate_up, "w_down": w_down, "gains": gains, "mom_square": mom_square, "mom_kv": mom_kv, "mom_gate_up": mom_gate_up, "mom_down": mom_down, "mom_gains": mom_gains}


@jax.custom_vjp
def low(v):
    return lax.optimization_barrier(v.astype(jnp.bfloat16)).astype(jnp.float32)

@jax.custom_vjp
def low_back(v):
    return v

def low_keep(v):
    return (low(v), None)

def low_pass(kept, grad):
    return (grad,)

def back_keep(v):
    return (v, None)

def back_low(kept, grad):
    return (low(grad),)
low.defvjp(low_keep, low_pass)
low_back.defvjp(back_keep, back_low)
highest_precision = lax.Precision.HIGHEST
norm_eps = 1e-05
rope_base = 100000.0
momentum_decay = 0.95
learn_rate = 0.2
weight_decay = 0.1
gain_rate = 0.25
poly_first = 3.4445
poly_second = -4.775
poly_third = 2.0315

def matmul(left, right):
    return jnp.dot(left, right, precision=highest_precision, preferred_element_type=jnp.float32)

def rms_scale(values, gain):
    factor = lax.rsqrt(lax.optimization_barrier(jnp.mean(values * values, -1, keepdims=True)) + norm_eps)
    return values * factor * gain

def angles(places, width):
    half_width = width // 2
    freqs = rope_base ** (-2.0 * jnp.arange(half_width, dtype=jnp.float32) / width)
    turned = places.astype(jnp.float32)[:, None] * freqs[None, :]
    turned = jnp.concatenate([turned, turned], axis=-1)
    return (jnp.cos(turned)[:, None, :], jnp.sin(turned)[:, None, :])

def rotate(values, cosine, sine):
    half_width = values.shape[-1] // 2
    swapped = jnp.concatenate([-values[..., half_width:], values[..., :half_width]], axis=-1)
    return values * cosine + swapped * sine

def attend_sequence(queries, key_collection, value_collection, places):
    repeat = HEADS // KV_HEADS
    block_rows = math.gcd(512, LENGTH)
    blocks = LENGTH // block_rows
    grouped_heads = queries.reshape(blocks, block_rows, KV_HEADS, repeat, HEAD_WIDTH)
    block_places = places.reshape(blocks, block_rows)
    block_starts = jnp.arange(blocks, dtype=jnp.int32) * block_rows
    key_index = jnp.arange(LENGTH, dtype=jnp.int32)

    def one_block(operands):
        query_tile_rows, query_places, block_start = operands
        query_index = block_start + jnp.arange(block_rows, dtype=jnp.int32)
        allowed = (key_index[None, :] <= query_index[:, None]) & (key_index[None, :] >= (query_index - query_places)[:, None])
        attention_scores = low_back(jnp.einsum('zqel,aql->qeza', query_tile_rows, key_collection, precision=highest_precision) * HEAD_WIDTH ** (-0.5))
        attention_scores = jnp.where(allowed[None, None], attention_scores, -jnp.inf)
        largest = lax.optimization_barrier(jnp.max(attention_scores, -1, keepdims=True))
        weight_tensors = jnp.exp(attention_scores - largest)
        weight_tensors = low(weight_tensors / lax.optimization_barrier(jnp.sum(weight_tensors, -1, keepdims=True)))
        mixed_heads = jnp.einsum('aump,pai->maui', weight_tensors, value_collection, precision=highest_precision)
        return mixed_heads.reshape(block_rows, HEADS * HEAD_WIDTH)
    result = lax.map(jax.checkpoint(one_block), (grouped_heads, block_places, block_starts))
    return result.reshape(LENGTH, HEADS * HEAD_WIDTH)

def forward(inputs, w_square, w_kv, w_gate_up, w_down, gains, positions):
    square_low = low(w_square)
    kv_low = low(w_kv)
    gate_low = low(w_gate_up)
    down_low = low(w_down)
    gain_low = low(gains)
    rows_in = inputs.reshape(SEQS * LENGTH, D)
    normed_one = low(rms_scale(rows_in, gain_low[0]))
    query_pre = low_back(matmul(normed_one, square_low[0]))
    key_pre = low_back(matmul(normed_one, kv_low[0]))
    value_rows = low(low_back(matmul(normed_one, kv_low[1])))
    cosine, sine = angles(positions.reshape(-1), HEAD_WIDTH)
    query_rows = low(rotate(query_pre.reshape(-1, HEADS, HEAD_WIDTH), cosine, sine))
    key_rows = low(rotate(key_pre.reshape(-1, KV_HEADS, HEAD_WIDTH), cosine, sine))
    mixed_heads = lax.map(lambda operands: attend_sequence(*operands), (query_rows.reshape(SEQS, LENGTH, HEADS, HEAD_WIDTH), key_rows.reshape(SEQS, LENGTH, KV_HEADS, HEAD_WIDTH), value_rows.reshape(SEQS, LENGTH, KV_HEADS, HEAD_WIDTH), positions))
    mixed_heads = low(low_back(mixed_heads.reshape(SEQS * LENGTH, D)))
    middle = rows_in + low_back(matmul(mixed_heads, square_low[1]))
    normed_two = low(rms_scale(middle, gain_low[1]))
    gate_rows = low_back(matmul(normed_two, gate_low[0].T))
    up_rows = low_back(matmul(normed_two, gate_low[1].T))
    hidden = low(jax.nn.silu(gate_rows) * up_rows)
    result = middle + low_back(matmul(hidden, down_low))
    return result.reshape(SEQS, LENGTH, D)

def orthogonal(update):
    if update.shape[0] > update.shape[1]:
        return orthogonal(update.T).T
    current = update / (jnp.sqrt(jnp.sum(update * update)) + 1e-07)
    for repeat_index in range(NS_ITERS):
        gram_matrix = matmul(current, current.T)
        poly = poly_second * gram_matrix + poly_third * matmul(gram_matrix, gram_matrix)
        current = poly_first * current + matmul(poly, current)
    return current

def muon_step(weight, momentum, gradient):
    new_momentum = momentum_decay * momentum + gradient
    update = gradient + momentum_decay * new_momentum
    spread = 0.2 * math.sqrt(max(weight.shape))
    new_weight = weight * (1.0 - learn_rate * weight_decay) - learn_rate * spread * orthogonal(update)
    return (new_momentum, new_weight)

def stacked_step(weight, momentum, gradient):
    results = [muon_step(weight[index], momentum[index], gradient[index]) for index in range(weight.shape[0])]
    return (jnp.stack([entry[0] for entry in results]), jnp.stack([entry[1] for entry in results]))

def reference(tokens, positions, cotangent, w_square, w_kv, w_gate_up, w_down, gains, mom_square, mom_kv, mom_gate_up, mom_down, mom_gains):

    def layer(inputs, square, pairs_kv, gate_up, down, gain_rows):
        return forward(inputs, square, pairs_kv, gate_up, down, gain_rows, positions)
    result, pullback = jax.vjp(layer, tokens.astype(jnp.float32), w_square, w_kv, w_gate_up, w_down, gains)
    grad_in, grad_square, grad_kv, grad_gate_up, grad_down, grad_gains = pullback(cotangent.astype(jnp.float32))
    next_square, new_square = stacked_step(w_square, mom_square, grad_square)
    next_kv, new_kv = stacked_step(w_kv, mom_kv, grad_kv)
    next_gate_up, new_gate_up = stacked_step(w_gate_up, mom_gate_up, grad_gate_up)
    next_down, new_down = muon_step(w_down, mom_down, grad_down)
    next_gains = momentum_decay * mom_gains + grad_gains
    gain_size = jnp.sqrt(lax.optimization_barrier(jnp.mean(next_gains * next_gains, -1, keepdims=True)) + 1e-06)
    new_gains = gains - gain_rate * next_gains / gain_size
    return (result.astype(jnp.bfloat16), grad_in.astype(jnp.bfloat16), grad_square, grad_kv, grad_gate_up, grad_down, grad_gains, next_square, next_kv, next_gate_up, next_down, next_gains, new_square, new_kv, new_gate_up, new_down, new_gains)
```

```python
import math

import jax
import jax.numpy as jnp
from jax import lax
from jax.experimental import pallas as pl
from jax.experimental.pallas import tpu as pltpu
from jax.sharding import PartitionSpec as P

HEAD_WIDTH = 64
NS_ITERS = 5


highest_precision = lax.Precision.HIGHEST
norm_eps = 1e-05
rope_base = 100000.0
momentum_decay = 0.95
learn_rate = 0.2
weight_decay = 0.1
gain_rate = 0.25
poly_first = 3.4445
poly_second = -4.775
poly_third = 2.0315
narrow_dtype = jnp.bfloat16
broad_dtype = jnp.float32


def spread(block, axis, holder):
    block = jnp.where(lax.axis_index(axis) == holder, block, jnp.zeros_like(block))
    return lax.psum(block, axis)


def side_by_side(arrays, axis, dim, along):
    ends, at = ([], 0)
    for a in arrays[:-1]:
        at += a.shape[along]
        ends.append(at)
    both = jnp.concatenate(arrays, axis=along)
    return tuple(jnp.split(lax.all_gather(both, axis, axis=dim, tiled=True), ends, axis=along))


def copy_for_each(shard, axis):
    copies = jnp.broadcast_to(shard, (lax.axis_size(axis), *shard.shape))
    return lax.all_to_all(copies, axis, split_axis=0, concat_axis=0, tiled=True)


def laid_out(tiles, dim):
    dims = list(tiles.shape[1:])
    dims[dim] *= tiles.shape[0]
    return jnp.moveaxis(tiles, 0, dim).reshape(dims)


def gathered_copies(shard, axis, dim):
    tiles = copy_for_each(shard, axis)
    return laid_out(tiles, dim)


def cut_along(shard, dim, length):
    before, after = (shard.shape[:dim], shard.shape[dim + 1 :])
    return jnp.moveaxis(shard.reshape(*before, length, -1, *after), dim, 0)


def summed_on_arrival(shard, axis, dim):
    length = lax.axis_size(axis)
    tiles = lax.all_to_all(cut_along(shard, dim, length), axis, 0, 0, tiled=True)
    return jnp.sum(tiles.astype(jnp.float32), axis=0)


def one_scatter(arrays, axis, dims):
    length = lax.axis_size(axis)
    tiles = [cut_along(a, dim, length) for a, dim in zip(arrays, dims)]
    lines = jnp.concatenate([b.reshape(length, -1) for b in tiles], axis=1)
    extent = max(16, -(-lines.shape[1] // 1024) * 8)
    lines = jnp.pad(lines, ((0, 0), (0, extent * 128 - lines.shape[1]))).reshape(-1, 128)
    flat, at, finished = (lax.psum_scatter(lines, axis, tiled=True).reshape(-1), 0, [])
    for b in tiles:
        part = b[0]
        finished.append(flat[at : at + part.size].reshape(part.shape))
        at += part.size
    return tuple(finished)


def in_one(arrays, axis):
    ends = [0]
    for a in arrays:
        ends.append(ends[-1] + a.size)
    total = lax.psum(jnp.concatenate([a.ravel() for a in arrays]), axis)
    return tuple((total[b:e].reshape(a.shape) for a, b, e in zip(arrays, ends, ends[1:])))


def angles(places, width):
    half_width = width // 2
    freqs = rope_base ** (-2.0 * jnp.arange(half_width, dtype=jnp.float32) / width)
    turned = places.astype(jnp.float32)[:, None] * freqs[None, :]
    turned = jnp.concatenate([turned, turned], axis=-1)
    return (jnp.cos(turned)[:, None, :], jnp.sin(turned)[:, None, :])


def rotate(values, cosine, sine):
    half_width = values.shape[-1] // 2
    swapped = jnp.concatenate([-values[..., half_width:], values[..., :half_width]], axis=-1)
    return values * cosine + swapped * sine


def norm_forward(values, gain):
    factor = lax.rsqrt(jnp.mean(values * values, -1, keepdims=True) + norm_eps)
    unit_rows = values * factor
    return (unit_rows * gain, unit_rows, factor)


def norm_backward(grad_rows, unit_rows, factor, gain):
    shaped = grad_rows * gain
    grad_values = factor * (shaped - unit_rows * jnp.mean(shaped * unit_rows, -1, keepdims=True))
    return (grad_values, jnp.sum(grad_rows * unit_rows, 0))


def score_block(grouped_heads, all_kv, block_start, block_rows, query_index, lowest_key, head_size):
    groups = grouped_heads.shape[1]
    kv_width = groups * head_size
    block_kv = lax.dynamic_slice_in_dim(all_kv, block_start, block_rows, 0)
    key_tile_rows = block_kv[:, :kv_width].reshape(block_rows, groups, head_size)
    value_tile_rows = block_kv[:, kv_width:].reshape(block_rows, groups, head_size)
    key_index = block_start + jnp.arange(block_rows, dtype=jnp.int32)
    allowed = (key_index[None, :] <= query_index[:, None]) & (
        key_index[None, :] >= lowest_key[:, None]
    )
    attention_scores = jnp.einsum(
        "zqel,aql->qeza", grouped_heads, key_tile_rows, preferred_element_type=broad_dtype
    ) * head_size ** (-0.5)
    return (jnp.where(allowed, attention_scores, -jnp.inf), key_tile_rows, value_tile_rows)


def attend_forward(
    grouped_heads, all_kv, query_index, lowest_key, block_rows, block_count, head_size
):
    token_count, groups, repeat, _ = grouped_heads.shape

    def advance(number, carry):
        running_max, running_sum, collected = carry
        attention_scores, key_tile_rows, value_tile_rows = score_block(
            grouped_heads,
            all_kv,
            number * block_rows,
            block_rows,
            query_index,
            lowest_key,
            head_size,
        )
        new_max = jnp.maximum(running_max, jnp.max(attention_scores, -1))
        damping = jnp.exp(running_max - new_max)
        weight_tensors = jnp.exp(attention_scores - new_max[..., None])
        running_sum = running_sum * damping + jnp.sum(weight_tensors, -1)
        collected = collected * damping[..., None] + jnp.einsum(
            "ovwk,koh->ovwh",
            weight_tensors.astype(narrow_dtype),
            value_tile_rows,
            preferred_element_type=broad_dtype,
        )
        return (new_max, running_sum, collected)

    start_state = (
        jnp.full((groups, repeat, token_count), -1e30, broad_dtype),
        jnp.zeros((groups, repeat, token_count), broad_dtype),
        jnp.zeros((groups, repeat, token_count, head_size), broad_dtype),
    )
    running_max, running_sum, collected = lax.fori_loop(0, block_count, advance, start_state)
    return (collected / running_sum[..., None], running_max + jnp.log(running_sum))


def attend_backward(
    grouped_heads,
    all_kv,
    query_index,
    lowest_key,
    block_rows,
    block_count,
    head_size,
    log_total,
    delta_rows,
    head_gradient,
):
    token_count, groups, repeat, _ = grouped_heads.shape
    length_all = all_kv.shape[0]
    factor = head_size ** (-0.5)

    def advance(number, carry):
        grad_query, grad_keys = carry
        block_start = number * block_rows
        attention_scores, key_tile_rows, value_tile_rows = score_block(
            grouped_heads, all_kv, block_start, block_rows, query_index, lowest_key, head_size
        )
        probabilities = jnp.exp(attention_scores - log_total[..., None])
        grad_probs = jnp.einsum(
            "jhai,uji->jhau", head_gradient, value_tile_rows, preferred_element_type=broad_dtype
        )
        score_gradient = (probabilities * (grad_probs - delta_rows[..., None])).astype(narrow_dtype)
        grad_query = (
            grad_query
            + jnp.einsum(
                "aump,pai->maui", score_gradient, key_tile_rows, preferred_element_type=broad_dtype
            )
            * factor
        )
        key_part = (
            jnp.einsum(
                "nkwv,wnkq->vnq", score_gradient, grouped_heads, preferred_element_type=broad_dtype
            )
            * factor
        )
        value_part = jnp.einsum(
            "yqki,yqkx->iyx",
            probabilities.astype(narrow_dtype),
            head_gradient,
            preferred_element_type=broad_dtype,
        )
        joined = jnp.concatenate(
            [key_part.reshape(block_rows, -1), value_part.reshape(block_rows, -1)], 1
        )
        current = lax.dynamic_slice_in_dim(grad_keys, block_start, block_rows, 0)
        grad_keys = lax.dynamic_update_slice_in_dim(grad_keys, current + joined, block_start, 0)
        return (grad_query, grad_keys)

    start_state = (
        jnp.zeros((token_count, groups, repeat, head_size), broad_dtype),
        jnp.zeros((length_all, all_kv.shape[1]), broad_dtype),
    )
    return lax.fori_loop(0, block_count, advance, start_state)


def orthogonal(update):
    if update.shape[0] > update.shape[1]:
        return orthogonal(update.T).T
    current = update / (jnp.sqrt(jnp.sum(update * update)) + 1e-07)
    for repeat_index in range(NS_ITERS):
        gram_matrix = jnp.dot(
            current, current.T, precision=highest_precision, preferred_element_type=broad_dtype
        )
        poly = poly_second * gram_matrix + poly_third * jnp.dot(
            gram_matrix,
            gram_matrix,
            precision=highest_precision,
            preferred_element_type=broad_dtype,
        )
        current = poly_first * current + jnp.dot(
            poly, current, precision=highest_precision, preferred_element_type=broad_dtype
        )
    return current


def publish(local_result, owner_rank):
    return spread(local_result.astype(jnp.bfloat16), "ctx", owner_rank).astype(local_result.dtype)


MESH = pl.DeviceIdType.MESH
bf16 = jnp.bfloat16
f32 = jnp.float32
NT = (((1,), (1,)), ((), ()))

OWNERS_FF = ((0, 5, 10), (15, 2, 8))
OWNERS_SQ = ((3, 12), (7, 13))
OWNERS_KV = ((6, 9), (4, 1))


def place():
    dp = lax.axis_index("dp")
    ctx = lax.axis_index("ctx")
    core = lax.rem(dp, 2)
    return dp, ctx, lax.div(dp, 2), core


def pick(core, first, second):
    return first + core * (second - first)


def remote(src, dst, send_sem, recv_sem, device):
    return pltpu.make_async_remote_copy(
        src_ref=src, dst_ref=dst, send_sem=send_sem, recv_sem=recv_sem, device_id=device, device_id_type=MESH
    )


def greet_all(dp, ctx):
    barrier = pltpu.get_barrier_semaphore()
    for d in range(1, 16):
        pl.semaphore_signal(
            barrier, inc=1, device_id={"dp": dp, "ctx": lax.rem(ctx + d, 16)}, device_id_type=MESH
        )
    for d in range(1, 4):
        pl.semaphore_signal(
            barrier, inc=1, device_id={"dp": lax.rem(dp + 2 * d, 8), "ctx": ctx}, device_id_type=MESH
        )
    pl.semaphore_signal(
        barrier, inc=1, device_id={"dp": dp + 1 - 2 * lax.rem(dp, 2), "ctx": ctx}, device_id_type=MESH
    )
    pl.semaphore_wait(barrier, 19)


class Reduce:
    names = ("g", "rx", "h", "r1", "h2", "r2", "x4", "fin", "s0", "v0", "s1", "v1", "s2", "v2", "s3", "v3", "s4", "v4")

    @staticmethod
    def scratch(rows, cols):
        return [
            pltpu.VMEM((16, rows, cols), bf16),
            pltpu.VMEM((4, 4, rows, cols), bf16),
            pltpu.VMEM((3, 4, rows, cols), bf16),
            pltpu.VMEM((4, rows, cols), bf16),
            pltpu.VMEM((3, rows, cols), bf16),
            pltpu.VMEM((4, rows, cols), bf16),
            pltpu.VMEM((2, rows, cols), bf16),
            pltpu.SemaphoreType.DMA((16,)),
            pltpu.SemaphoreType.DMA((16,)),
            pltpu.SemaphoreType.DMA((3,)),
            pltpu.SemaphoreType.DMA((3,)),
            pltpu.SemaphoreType.DMA((3,)),
            pltpu.SemaphoreType.DMA((3,)),
            pltpu.SemaphoreType.DMA((3,)),
            pltpu.SemaphoreType.DMA((3,)),
            pltpu.SemaphoreType.DMA((1,)),
            pltpu.SemaphoreType.DMA((1,)),
        ]

    def __init__(self, g, refs):
        (self.g, self.rx, self.h, self.r1, self.h2, self.r2, self.x4, self.fin) = (g, *refs[:7])
        (self.s0, self.v0, self.s1, self.v1, self.s2, self.v2, self.s3, self.v3, self.s4, self.v4) = refs[7:17]
        self.dp, self.ctx, self.x, self.core = place()
        y, z = lax.div(self.ctx, 4), lax.rem(self.ctx, 4)
        self.first = pick(self.core, z, y)
        self.second = pick(self.core, y, z)
        self.sa = pick(self.core, 1, 4)
        self.sb = pick(self.core, 4, 1)
        self.sibling = {"dp": self.dp + 1 - 2 * self.core, "ctx": self.ctx}

    def order(self, d):
        return jnp.where(d == 0, 2, jnp.where(d == 1, 1, jnp.where(d == 2, 3, 0)))

    def pair_copy(self, s):
        return remote(self.g.at[1 - self.core, s], self.rx.at[s], self.s0.at[s], self.v0.at[s], self.sibling)

    def first_copy(self, d):
        a = lax.rem(self.first + d, 4)
        peer = {"dp": self.dp, "ctx": self.ctx + (a - self.first) * self.sa}
        return remote(self.h.at[a], self.r1.at[d - 1], self.s1.at[d - 1], self.v1.at[d - 1], peer)

    def second_copy(self, d):
        b = lax.rem(self.second + d, 4)
        peer = {"dp": self.dp, "ctx": self.ctx + (b - self.second) * self.sb}
        return remote(self.h2.at[b], self.r2.at[d - 1], self.s2.at[d - 1], self.v2.at[d - 1], peer)

    def third_copy(self, d):
        peer = {"dp": lax.rem(self.dp + 2 * d, 8), "ctx": self.ctx}
        return remote(self.x4.at[self.x], self.x4.at[self.x], self.s3.at[d - 1], self.v3.at[d - 1], peer)

    def last_copy(self):
        return remote(self.fin.at[self.core], self.fin.at[self.core], self.s4.at[0], self.v4.at[0], self.sibling)

    def start(self):
        sa, sb = pick(1 - self.core, 1, 4), pick(1 - self.core, 4, 1)
        first = pick(1 - self.core, lax.rem(self.ctx, 4), lax.div(self.ctx, 4))

        def step(i, carry):
            a = lax.rem(first + self.order(lax.div(i, 4)), 4)
            self.pair_copy(a * sa + lax.rem(i, 4) * sb).start()
            return carry

        lax.fori_loop(0, 16, step, 0)

    def pair_sum(self):
        def step(i, carry):
            d = self.order(i)
            a = lax.rem(self.first + d, 4)

            def inner(b, carry):
                s = a * self.sa + b * self.sb
                self.pair_copy(s).wait_recv()
                self.h[a, b] = (self.g[self.core, s].astype(f32) + self.rx[s].astype(f32)).astype(bf16)
                return carry

            lax.fori_loop(0, 4, inner, 0)

            @pl.when(d != 0)
            def _():
                self.first_copy(d).start()

            return carry

        lax.fori_loop(0, 4, step, 0)

    def first_sum(self):
        for d in range(1, 4):
            self.first_copy(d).wait_recv()

        def step(i, carry):
            d = self.order(i)
            b = lax.rem(self.second + d, 4)
            total = self.h[self.first, b].astype(f32)
            for k in range(3):
                total = total + self.r1[k, b].astype(f32)
            self.h2[b] = total.astype(bf16)

            @pl.when(d != 0)
            def _():
                self.second_copy(d).start()

            return carry

        lax.fori_loop(0, 4, step, 0)

    def second_sum(self):
        for d in range(1, 4):
            self.second_copy(d).wait_recv()
        total = self.h2[self.second].astype(f32)
        for k in range(3):
            total = total + self.r2[k].astype(f32)
        self.x4[self.x] = total.astype(bf16)
        for d in range(1, 4):
            self.third_copy(d).start()

    def third_sum(self):
        for d in range(1, 4):
            src = lax.rem(self.x + 4 - d, 4)
            remote(
                self.x4.at[src], self.x4.at[src], self.s3.at[d - 1], self.v3.at[d - 1], self.sibling
            ).wait_recv()
        total = self.x4[0].astype(f32)
        for k in range(1, 4):
            total = total + self.x4[k].astype(f32)
        self.fin[self.core] = total.astype(bf16)
        self.last_copy().start()

    def finish(self):
        other = 1 - self.core
        remote(
            self.fin.at[other], self.fin.at[other], self.s4.at[0], self.v4.at[0], self.sibling
        ).wait_recv()

    def drain(self):
        def step(s, carry):
            self.pair_copy(s).wait_send()
            return carry

        lax.fori_loop(0, 16, step, 0)
        for d in range(1, 4):
            self.first_copy(d).wait_send()
            self.second_copy(d).wait_send()
            self.third_copy(d).wait_send()
        self.last_copy().wait_send()


def newton_schulz(t_ref, x_ref):
    parts, rows, cols = t_ref.shape
    total = parts * rows
    t = t_ref[...].reshape(total, cols).astype(f32)
    scale = 1.0 / (jnp.sqrt(jnp.sum(t * t)) + 1e-07)
    x_ref[...] = (t * scale).astype(bf16).T

    def advance(_, carry):
        x = x_ref[...]
        gram = lax.dot_general(x, x, NT, preferred_element_type=f32)
        low = gram.astype(bf16)
        square = jnp.dot(low, low, preferred_element_type=f32)
        poly = (poly_second * gram + poly_third * square).astype(bf16)
        for at in range(0, total, 512):
            end = min(at + 512, total)
            part = x_ref[:, at:end]
            x_ref[:, at:end] = (
                poly_first * part.astype(f32) + jnp.dot(poly, part, preferred_element_type=f32)
            ).astype(bf16)
        return carry

    lax.fori_loop(0, NS_ITERS, advance, 0)
    t_ref[...] = x_ref[...].T.reshape(parts, rows, cols)


class Muon:
    @staticmethod
    def scratch(count, rows, cols):
        return [
            pltpu.VMEM((count, rows, cols), bf16),
            pltpu.VMEM((16, rows, cols), bf16),
            pltpu.VMEM((cols, 16 * rows), bf16),
            pltpu.SemaphoreType.DMA((count,)),
            pltpu.SemaphoreType.DMA((16,)),
            pltpu.SemaphoreType.DMA((16,)),
            pltpu.SemaphoreType.DMA((count,)),
        ]

    def __init__(self, owners, refs, out):
        self.u, self.t, self.x, self.us, self.uv, self.os, self.ov = refs
        self.out = out
        self.dp, self.ctx, _, self.core = place()
        self.owners = [pick(self.core, a, b) for a, b in zip(*owners)]
        self.mine = jnp.zeros((), jnp.bool_)
        self.which = 0
        for m, owner in enumerate(self.owners):
            self.mine = jnp.logical_or(self.mine, self.ctx == owner)
            self.which = self.which + jnp.where(self.ctx == owner, m, 0)

    def up(self, m):
        return remote(
            self.u.at[m], self.t.at[self.ctx], self.us.at[m], self.uv.at[self.ctx],
            {"dp": self.dp, "ctx": self.owners[m]},
        )

    def send(self, m):
        @pl.when(self.ctx != self.owners[m])
        def _():
            self.up(m).start()

        @pl.when(self.ctx == self.owners[m])
        def _():
            self.t[self.ctx] = self.u[m]

    def down(self, peer):
        return remote(
            self.t.at[peer], self.out.at[self.which], self.os.at[peer], self.ov.at[self.which],
            {"dp": self.dp, "ctx": peer},
        )

    def work(self):
        @pl.when(self.mine)
        def _():
            def arrive(d, carry):
                s = lax.rem(self.ctx + d, 16)
                remote(
                    self.t.at[s], self.t.at[s], self.us.at[0], self.uv.at[s], {"dp": self.dp, "ctx": s}
                ).wait_recv()
                return carry

            lax.fori_loop(1, 16, arrive, 0)
            newton_schulz(self.t, self.x)

            def leave(d, carry):
                self.down(lax.rem(self.ctx + d, 16)).start()
                return carry

            lax.fori_loop(1, 16, leave, 0)
            self.out[self.which] = self.t[self.ctx]

            def gone(d, carry):
                self.down(lax.rem(self.ctx + d, 16)).wait_send()
                return carry

            lax.fori_loop(1, 16, gone, 0)

    def collect(self):
        for m, owner in enumerate(self.owners):
            @pl.when(self.ctx != owner)
            def _():
                remote(
                    self.t.at[0], self.out.at[m], self.os.at[0], self.ov.at[m], {"dp": self.dp, "ctx": owner}
                ).wait_recv()
                self.up(m).wait_send()


def update_of(momentum, gradient):
    return gradient + momentum_decay * (momentum_decay * momentum + gradient)


def step_kernel(
    fg, ag, mom_square, mom_kv, mom_gate_up, mom_down, mom_gains,
    fin_f, fin_a, o_ff, o_sq, o_kv, gain_sums,
    pad_sq, pad_kv, gsend, gs, gv, *rest,
):
    ff = Reduce(fg, rest[:6] + (fin_f,) + rest[7:17])
    at = Reduce(ag, rest[17:23] + (fin_a,) + rest[24:34])
    m_ff = Muon(OWNERS_FF, rest[34:41], o_ff)
    m_sq = Muon(OWNERS_SQ, rest[41:48], o_sq)
    m_kv = Muon(OWNERS_KV, rest[48:55], o_kv)
    dp, ctx, x, core = place()
    greet_all(dp, ctx)
    at.start()
    ff.start()
    at.pair_sum()
    ff.pair_sum()
    at.first_sum()
    ff.first_sum()
    at.second_sum()
    ff.second_sum()
    at.third_sum()
    ff.third_sum()

    at.finish()
    pad_sq[...] = jnp.zeros_like(pad_sq)
    pad_kv[...] = jnp.zeros_like(pad_kv)
    pad_sq[:, 0:36, :] = mom_square[...]
    pad_kv[:, 0:36, :] = mom_kv[...]
    for m in range(2):
        m_sq.u[m] = update_of(pad_sq[m], fin_a[m, :, 0:576].astype(f32)).astype(bf16)
        m_sq.send(m)
    for m in range(2):
        m_kv.u[m] = update_of(pad_kv[m], fin_a[m, :, 576:768].astype(f32)).astype(bf16)
        m_kv.send(m)
    gain_grads = fin_a[0, :, 768:896].astype(f32).T[0:2, 0:36]
    gain_next = momentum_decay * mom_gains[...] + gain_grads
    sums = jnp.sum(gain_next * gain_next, axis=1, keepdims=True)
    gsend[0:2, :] = jnp.broadcast_to(sums, (2, 128))
    gsend[2:8, :] = jnp.zeros((6, 128), f32)

    def tell(d):
        return remote(
            gsend, gain_sums.at[ctx], gs.at[d - 1], gv.at[d - 1], {"dp": dp, "ctx": lax.rem(ctx + d, 16)}
        )

    for d in range(1, 16):
        tell(d).start()
    gain_sums[ctx] = gsend[...]

    ff.finish()
    m_ff.u[0] = update_of(mom_gate_up[0], fin_f[0, 0:96].astype(f32)).astype(bf16)
    m_ff.send(0)
    m_ff.u[1, 0:48] = update_of(mom_gate_up[1, 0:48], fin_f[0, 96:144].astype(f32)).astype(bf16)
    m_ff.u[1, 48:96] = update_of(mom_gate_up[1, 48:96], fin_f[1, 0:48].astype(f32)).astype(bf16)
    m_ff.send(1)
    m_ff.u[2] = update_of(mom_down[...], fin_f[1, 48:144].astype(f32)).astype(bf16)
    m_ff.send(2)

    m_ff.work()
    m_sq.work()
    m_kv.work()
    m_ff.collect()
    m_sq.collect()
    m_kv.collect()

    for d in range(1, 16):
        remote(
            gsend, gain_sums.at[lax.rem(ctx + 16 - d, 16)], gs.at[d - 1], gv.at[d - 1], {"dp": dp, "ctx": ctx}
        ).wait_recv()
        tell(d).wait_send()
    at.drain()
    ff.drain()


def whole(memory=pltpu.VMEM):
    return pl.BlockSpec(memory_space=memory)


def reduce_and_orthogonalize(fg, ag, mom_square, mom_kv, mom_gate_up, mom_down, mom_gains):
    scratch = [
        pltpu.VMEM((2, 48, 576), f32),
        pltpu.VMEM((2, 48, 192), f32),
        pltpu.VMEM((8, 128), f32),
        pltpu.SemaphoreType.DMA((15,)),
        pltpu.SemaphoreType.DMA((15,)),
        *Reduce.scratch(144, 576),
        *Reduce.scratch(48, 896),
        *Muon.scratch(3, 96, 576),
        *Muon.scratch(2, 48, 576),
        *Muon.scratch(2, 48, 192),
    ]
    return pl.pallas_call(
        step_kernel,
        out_shape=(
            jax.ShapeDtypeStruct((2, 144, 576), bf16),
            jax.ShapeDtypeStruct((2, 48, 896), bf16),
            jax.ShapeDtypeStruct((3, 96, 576), bf16),
            jax.ShapeDtypeStruct((2, 48, 576), bf16),
            jax.ShapeDtypeStruct((2, 48, 192), bf16),
            jax.ShapeDtypeStruct((16, 8, 128), f32),
        ),
        in_specs=[whole()] * 7,
        out_specs=[whole()] * 6,
        scratch_shapes=scratch,
        compiler_params=pltpu.CompilerParams(
            collective_id=3, has_side_effects=True, vmem_limit_bytes=58 * 2**20
        ),
    )(fg, ag, mom_square, mom_kv, mom_gate_up, mom_down, mom_gains)


def finish_kernel(
    fin_f, fin_a, o_ff, o_sq, o_kv, gain_sums, w_square, w_kv, w_gate_up, w_down, gains,
    mom_square, mom_kv, mom_gate_up, mom_down, mom_gains,
    grad_square, grad_kv, grad_gate_up, grad_down, grad_gains,
    next_square, next_kv, next_gate_up, next_down, next_gains,
    new_square, new_kv, new_gate_up, new_down, new_gains,
):
    shrink = 1.0 - learn_rate * weight_decay

    def one(at, grad, width, weight, momentum, ortho, grad_out, next_out, new_out):
        grad_out[at] = grad
        next_out[at] = momentum_decay * momentum[at] + grad
        new_out[at] = shrink * weight[at] - learn_rate * (0.2 * math.sqrt(width)) * ortho

    for m in range(2):
        one(m, fin_a[m, :, 0:576].astype(f32)[0:36], 576, w_square, mom_square,
            o_sq[m].astype(f32)[0:36], grad_square, next_square, new_square)
        one(m, fin_a[m, :, 576:768].astype(f32)[0:36], 576, w_kv, mom_kv,
            o_kv[m].astype(f32)[0:36], grad_kv, next_kv, new_kv)
    everything = slice(None)
    one((0, everything), fin_f[0, 0:96].astype(f32), 1536, w_gate_up, mom_gate_up,
        o_ff[0].astype(f32), grad_gate_up, next_gate_up, new_gate_up)
    one((1, slice(0, 48)), fin_f[0, 96:144].astype(f32), 1536, w_gate_up, mom_gate_up,
        o_ff[1, 0:48].astype(f32), grad_gate_up, next_gate_up, new_gate_up)
    one((1, slice(48, 96)), fin_f[1, 0:48].astype(f32), 1536, w_gate_up, mom_gate_up,
        o_ff[1, 48:96].astype(f32), grad_gate_up, next_gate_up, new_gate_up)
    one(everything, fin_f[1, 48:144].astype(f32), 1536, w_down, mom_down,
        o_ff[2].astype(f32), grad_down, next_down, new_down)
    gain_grads = fin_a[0, :, 768:896].astype(f32).T[0:2, 0:36]
    gain_next = momentum_decay * mom_gains[...] + gain_grads
    total = gain_sums[0]
    for k in range(1, 16):
        total = total + gain_sums[k]
    mean = total[0:2, 0:1] * (1.0 / 576)
    grad_gains[...] = gain_grads
    next_gains[...] = gain_next
    new_gains[...] = gains[...] - gain_rate * gain_next / jnp.sqrt(mean + 1e-06)


def finish(packed, weights, momenta):
    shapes = [jax.ShapeDtypeStruct(a.shape, f32) for a in weights]
    return pl.pallas_call(
        finish_kernel,
        out_shape=tuple(shapes * 3),
        in_specs=[whole()] * 16,
        out_specs=[whole()] * 15,
        compiler_params=pltpu.CompilerParams(vmem_limit_bytes=58 * 2**20),
    )(*packed, *weights, *momenta)


def shards(
    tokens,
    positions,
    cotangent,
    w_square,
    w_kv,
    w_gate_up,
    w_down,
    gains,
    mom_square,
    mom_kv,
    mom_gate_up,
    mom_down,
    mom_gains,
):
    ctx_count = lax.axis_size("ctx")
    ctx_here = lax.axis_index("ctx")
    rows_in = tokens[0].astype(broad_dtype)
    token_count, width = rows_in.shape
    length_all = token_count * ctx_count
    square_low, kv_low, gate_low, down_low, gain_low = (
        *side_by_side((w_square.astype(narrow_dtype), w_kv.astype(narrow_dtype)), "ctx", 1, 2),
        lax.all_gather(w_gate_up.astype(narrow_dtype), "ctx", axis=1, tiled=True),
        lax.all_gather(w_down.astype(narrow_dtype), "ctx", axis=0, tiled=True),
        lax.all_gather(gains.astype(narrow_dtype), "ctx", axis=1, tiled=True),
    )
    gain_rows = gain_low.astype(broad_dtype)
    kv_width = kv_low.shape[2]
    hidden_width = gate_low.shape[1]
    head_size = HEAD_WIDTH
    kv_heads = kv_width // head_size
    heads_all = width // head_size
    repeat = heads_all // kv_heads
    kv_joined = jnp.concatenate([kv_low[0], kv_low[1]], 1)
    cosine, sine = angles(positions[0], head_size)
    normed_one, unit_one, factor_one = norm_forward(rows_in, gain_rows[0])
    normed_low = normed_one.astype(narrow_dtype)
    query_pre = jnp.dot(normed_low, square_low[0], preferred_element_type=broad_dtype)
    kv_pre = jnp.dot(normed_low, kv_joined, preferred_element_type=broad_dtype)
    query_rows = rotate(query_pre.reshape(token_count, heads_all, head_size), cosine, sine).astype(
        narrow_dtype
    )
    key_rows = rotate(
        kv_pre[:, :kv_width].reshape(token_count, kv_heads, head_size), cosine, sine
    ).astype(narrow_dtype)
    local_kv = jnp.concatenate(
        [key_rows.reshape(token_count, kv_width), kv_pre[:, kv_width:].astype(narrow_dtype)], 1
    )
    all_kv = gathered_copies(local_kv, "ctx", 0)
    block_rows = math.gcd(512, length_all)
    first_row = ctx_here * token_count
    query_index = first_row + jnp.arange(token_count, dtype=jnp.int32)
    lowest_key = query_index - positions[0]
    grouped_heads = query_rows.reshape(token_count, kv_heads, repeat, head_size)
    block_count = (first_row + token_count + block_rows - 1) // block_rows
    heads_out, log_total = attend_forward(
        grouped_heads, all_kv, query_index, lowest_key, block_rows, block_count, head_size
    )
    mixed_low = heads_out.transpose(2, 0, 1, 3).reshape(token_count, width).astype(narrow_dtype)
    middle = rows_in + jnp.dot(mixed_low, square_low[1], preferred_element_type=broad_dtype)
    normed_two, unit_two, factor_two = norm_forward(middle, gain_rows[1])
    normed_two_low = normed_two.astype(narrow_dtype)
    gate_up = jnp.einsum(
        "td,kfd->ktf", normed_two_low, gate_low, preferred_element_type=broad_dtype
    )
    gate_rows = gate_up[0]
    up_rows = gate_up[1]
    sigmoid_rows = jax.nn.sigmoid(gate_rows)
    hidden = (gate_rows * sigmoid_rows * up_rows).astype(narrow_dtype)
    result = middle + jnp.dot(hidden, down_low, preferred_element_type=broad_dtype)
    grad_result_low = cotangent[0]
    grad_result = grad_result_low.astype(broad_dtype)
    grad_down_full = jnp.einsum(
        "tf,td->fd", hidden, grad_result_low, preferred_element_type=broad_dtype
    )
    grad_hidden = jnp.einsum(
        "td,fd->tf", grad_result_low, down_low, preferred_element_type=broad_dtype
    )
    grad_gate = (
        grad_hidden * up_rows * sigmoid_rows * (1.0 + gate_rows * (1.0 - sigmoid_rows))
    ).astype(narrow_dtype)
    grad_up = (grad_hidden * gate_rows * sigmoid_rows).astype(narrow_dtype)
    grad_pair = jnp.stack([grad_gate, grad_up])
    grad_gate_full = jnp.einsum(
        "td,ktf->kfd", normed_two_low, grad_pair, preferred_element_type=broad_dtype
    )
    grad_normed_two = jnp.einsum(
        "ktf,kfd->td", grad_pair, gate_low, preferred_element_type=broad_dtype
    )
    grad_middle_norm, grad_gain_two = norm_backward(
        grad_normed_two, unit_two, factor_two, gain_rows[1]
    )
    grad_middle = grad_result + grad_middle_norm
    grad_attn = grad_middle.astype(narrow_dtype)
    grad_out_proj = jnp.einsum(
        "tq,td->qd", mixed_low, grad_attn, preferred_element_type=broad_dtype
    )
    grad_mixed = jnp.einsum(
        "td,qd->tq", grad_attn, square_low[1], preferred_element_type=broad_dtype
    ).astype(narrow_dtype)
    head_gradient = grad_mixed.reshape(token_count, kv_heads, repeat, head_size).transpose(
        1, 2, 0, 3
    )
    delta_rows = jnp.sum(head_gradient.astype(broad_dtype) * heads_out, -1)
    grad_query, grad_keys = attend_backward(
        grouped_heads,
        all_kv,
        query_index,
        lowest_key,
        block_rows,
        block_count,
        head_size,
        log_total,
        delta_rows,
        head_gradient,
    )
    grad_kv_rows = summed_on_arrival(grad_keys.astype(jnp.bfloat16), "ctx", 0)
    grad_key_pre = rotate(
        grad_kv_rows[:, :kv_width].reshape(token_count, kv_heads, head_size), cosine, -sine
    ).reshape(token_count, kv_width)
    grad_kv_pre = jnp.concatenate([grad_key_pre, grad_kv_rows[:, kv_width:]], 1).astype(
        narrow_dtype
    )
    grad_query_pre = (
        rotate(grad_query.reshape(token_count, heads_all, head_size), cosine, -sine)
        .reshape(token_count, width)
        .astype(narrow_dtype)
    )
    grad_query_full = jnp.einsum(
        "td,tq->dq", normed_low, grad_query_pre, preferred_element_type=broad_dtype
    )
    grad_kv_full = jnp.einsum(
        "td,tk->dk", normed_low, grad_kv_pre, preferred_element_type=broad_dtype
    )
    grad_normed_one = jnp.einsum(
        "tq,dq->td", grad_query_pre, square_low[0], preferred_element_type=broad_dtype
    ) + jnp.einsum("tk,dk->td", grad_kv_pre, kv_joined, preferred_element_type=broad_dtype)
    grad_rows_norm, grad_gain_one = norm_backward(
        grad_normed_one, unit_one, factor_one, gain_rows[0]
    )
    grad_input = (grad_middle + grad_rows_norm).astype(narrow_dtype)
    def slices(full):
        parts = full.astype(bf16).reshape(ctx_count, full.shape[0] // ctx_count, full.shape[1])
        return jnp.pad(parts, ((0, 0), (0, 48 - parts.shape[1]), (0, 0)))

    gain_columns = jnp.pad(jnp.stack([grad_gain_one, grad_gain_two], 1), ((0, 0), (0, 126)))
    ag = jnp.stack(
        [
            jnp.concatenate(
                [slices(grad_query_full), slices(grad_kv_full[:, :kv_width]), slices(gain_columns)], 2
            ),
            jnp.concatenate(
                [
                    slices(grad_out_proj),
                    slices(grad_kv_full[:, kv_width:]),
                    jnp.zeros((ctx_count, 48, 128), bf16),
                ],
                2,
            ),
        ]
    )
    gate_parts = grad_gate_full.astype(bf16).reshape(2, ctx_count, 96, width)
    down_parts = grad_down_full.astype(bf16).reshape(ctx_count, 96, width)
    fg = jnp.stack(
        [
            jnp.concatenate([gate_parts[0], gate_parts[1, :, :48]], 1),
            jnp.concatenate([gate_parts[1, :, 48:], down_parts], 1),
        ]
    )
    packed = reduce_and_orthogonalize(fg, ag, mom_square, mom_kv, mom_gate_up, mom_down, mom_gains)
    updated = finish(
        packed,
        (w_square, w_kv, w_gate_up, w_down, gains),
        (mom_square, mom_kv, mom_gate_up, mom_down, mom_gains),
    )
    return (result.astype(narrow_dtype)[None], grad_input[None], *updated)


def solution(mesh):
    return jax.shard_map(
        shards,
        mesh=mesh,
        in_specs=(
            P("dp", "ctx", None),
            P("dp", "ctx"),
            P("dp", "ctx", None),
            P(None, "ctx", None),
            P(None, "ctx", None),
            P(None, "ctx", None),
            P("ctx", None),
            P(None, "ctx"),
            P(None, "ctx", None),
            P(None, "ctx", None),
            P(None, "ctx", None),
            P("ctx", None),
            P(None, "ctx"),
        ),
        out_specs=(
            P("dp", "ctx", None),
            P("dp", "ctx", None),
            P(None, "ctx", None),
            P(None, "ctx", None),
            P(None, "ctx", None),
            P("ctx", None),
            P(None, "ctx"),
            P(None, "ctx", None),
            P(None, "ctx", None),
            P(None, "ctx", None),
            P("ctx", None),
            P(None, "ctx"),
            P(None, "ctx", None),
            P(None, "ctx", None),
            P(None, "ctx", None),
            P("ctx", None),
            P(None, "ctx"),
        ),
        check_vma=False,
    )
```

```python
import math

import jax
import jax.numpy as jnp
import numpy as np
from jax import lax
from jax.experimental import pallas as pl
from jax.experimental.pallas import tpu as pltpu
from jax.sharding import PartitionSpec as P

HEAD_WIDTH = 64
NS_ITERS = 5

norm_eps = 1e-05
rope_base = 100000.0
momentum_decay = 0.95
learn_rate = 0.2
weight_decay = 0.1
gain_rate = 0.25
poly_first = 3.4445
poly_second = -4.775
poly_third = 2.0315

MESH = pl.DeviceIdType.MESH
bf16 = jnp.bfloat16
f32 = jnp.float32
NT = (((1,), (1,)), ((), ()))
HIDDEN = -1e30

OWNERS_FF = ((0, 5, 10), (15, 2, 8))
OWNERS_SQ = ((3, 12), (7, 13))
OWNERS_KV = ((6, 9), (4, 1))


def place():
    dp = lax.axis_index("dp")
    ctx = lax.axis_index("ctx")
    core = lax.rem(dp, 2)
    return dp, ctx, lax.div(dp, 2), core


def pick(core, first, second):
    return first + core * (second - first)


def remote(src, dst, send_sem, recv_sem, device):
    return pltpu.make_async_remote_copy(
        src_ref=src, dst_ref=dst, send_sem=send_sem, recv_sem=recv_sem, device_id=device, device_id_type=MESH
    )


def greet_all(dp, ctx):
    barrier = pltpu.get_barrier_semaphore()
    for d in range(1, 16):
        pl.semaphore_signal(
            barrier, inc=1, device_id={"dp": dp, "ctx": lax.rem(ctx + d, 16)}, device_id_type=MESH
        )
    for d in range(1, 4):
        pl.semaphore_signal(
            barrier, inc=1, device_id={"dp": lax.rem(dp + 2 * d, 8), "ctx": ctx}, device_id_type=MESH
        )
    pl.semaphore_signal(
        barrier, inc=1, device_id={"dp": dp + 1 - 2 * lax.rem(dp, 2), "ctx": ctx}, device_id_type=MESH
    )
    return barrier


class Axes:
    def __init__(self):
        self.dp, self.ctx, self.x, self.core = place()
        y, z = lax.div(self.ctx, 4), lax.rem(self.ctx, 4)
        self.first = pick(self.core, z, y)
        self.second = pick(self.core, y, z)
        self.sa = pick(self.core, 1, 4)
        self.sb = pick(self.core, 4, 1)
        self.sibling = {"dp": self.dp + 1 - 2 * self.core, "ctx": self.ctx}

    def near(self, d):
        a = lax.rem(self.first + d, 4)
        return {"dp": self.dp, "ctx": self.ctx + (a - self.first) * self.sa}

    def far(self, d):
        b = lax.rem(self.second + d, 4)
        return {"dp": self.dp, "ctx": self.ctx + (b - self.second) * self.sb}

    def slice_at(self, back_first, back_second):
        a = lax.rem(self.first + 4 - back_first, 4)
        b = lax.rem(self.second + 4 - back_second, 4)
        return a * self.sa + b * self.sb


class Gather:
    @staticmethod
    def scratch():
        return [
            pltpu.SemaphoreType.DMA((3,)),
            pltpu.SemaphoreType.DMA((3,)),
            pltpu.SemaphoreType.DMA((4, 3)),
            pltpu.SemaphoreType.DMA((4, 3)),
            pltpu.SemaphoreType.DMA((16,)),
            pltpu.SemaphoreType.DMA((16,)),
        ]

    def __init__(self, axes, region, refs):
        self.axes, self.region = axes, region
        self.s1, self.v1, self.s2, self.v2, self.sp, self.vp = refs

    def move(self, s, ssem, vsem, device, core=None):
        part = self.region(s, self.axes.core if core is None else core)
        return remote(part, part, ssem, vsem, device)

    def first_copy(self, d, s):
        return self.move(s, self.s1.at[d - 1], self.v1.at[d - 1], self.axes.near(d))

    def second_copy(self, e, d, s):
        return self.move(s, self.s2.at[e, d - 1], self.v2.at[e, d - 1], self.axes.far(d))

    def pair_copy(self, s, core=None):
        return self.move(s, self.sp.at[s], self.vp.at[s], self.axes.sibling, core)

    def start(self):
        for d in (2, 1, 3):
            self.first_copy(d, self.axes.ctx).start()

    def forward(self):
        for d in (2, 1, 3):
            self.second_copy(0, d, self.axes.ctx).start()
        for e in (1, 3, 2):
            s = self.axes.slice_at(e, 0)
            self.first_copy(e, s).wait_recv()
            for d in (2, 1, 3):
                self.second_copy(e, d, s).start()
            self.pair_copy(s).start()

    def swap(self):
        for e in (0, 1, 3, 2):
            for d in (1, 3, 2):
                s = self.axes.slice_at(e, d)
                self.second_copy(e, d, s).wait_recv()
                self.pair_copy(s).start()

    def finish(self):
        def step(i, carry):
            s = lax.rem(self.axes.ctx + i, 16)
            self.pair_copy(s, 1 - self.axes.core).wait_recv()
            return carry

        lax.fori_loop(1, 16, step, 0)

    def drain(self):
        for d in range(1, 4):
            self.first_copy(d, self.axes.ctx).wait_send()
            for e in range(4):
                self.second_copy(e, d, self.axes.ctx).wait_send()

        def step(i, carry):
            self.pair_copy(lax.rem(self.axes.ctx + i, 16)).wait_send()
            return carry

        lax.fori_loop(1, 16, step, 0)


class Reduce:
    @staticmethod
    def scratch(rows, cols):
        return [
            pltpu.VMEM((16, rows, cols), bf16),
            pltpu.VMEM((3, 4, rows, cols), bf16),
            pltpu.VMEM((3, rows, cols), bf16),
            pltpu.VMEM((4, rows, cols), bf16),
            pltpu.SemaphoreType.DMA((4,)),
            pltpu.SemaphoreType.DMA((4,)),
            pltpu.SemaphoreType.DMA((3,)),
            pltpu.SemaphoreType.DMA((3,)),
            pltpu.SemaphoreType.DMA((3,)),
            pltpu.SemaphoreType.DMA((3,)),
            pltpu.SemaphoreType.DMA((3,)),
            pltpu.SemaphoreType.DMA((3,)),
            pltpu.SemaphoreType.DMA((1,)),
            pltpu.SemaphoreType.DMA((1,)),
        ]

    def __init__(self, axes, g, fin, refs):
        self.axes, self.g, self.fin = axes, g, fin
        self.rx, self.r1, self.r2, self.x4 = refs[:4]
        self.s0, self.v0, self.s1, self.v1, self.s2, self.v2, self.s3, self.v3, self.s4, self.v4 = refs[4:]
        self.core, self.x = axes.core, axes.x

    def pair_copy(self, a):
        part = pl.ds(4 * a, 4)
        return remote(
            self.g.at[1 - self.core, part], self.rx.at[part], self.s0.at[a], self.v0.at[a], self.axes.sibling
        )

    def first_copy(self, d):
        a = lax.rem(self.axes.first + d, 4)
        return remote(
            self.g.at[self.core, pl.ds(4 * a, 4)], self.r1.at[d - 1], self.s1.at[d - 1], self.v1.at[d - 1],
            self.axes.near(d),
        )

    def second_copy(self, d):
        b = lax.rem(self.axes.second + d, 4)
        return remote(
            self.g.at[self.core, 4 * self.axes.first + b], self.r2.at[d - 1], self.s2.at[d - 1], self.v2.at[d - 1],
            self.axes.far(d),
        )

    def third_copy(self, d, slot):
        peer = {"dp": lax.rem(self.axes.dp + 2 * d, 8), "ctx": self.axes.ctx}
        return remote(self.x4.at[slot], self.x4.at[slot], self.s3.at[d - 1], self.v3.at[d - 1], peer)

    def last_copy(self, half):
        return remote(self.fin.at[half], self.fin.at[half], self.s4.at[0], self.v4.at[0], self.axes.sibling)

    def start(self):
        first = pick(self.core, self.axes.second, self.axes.second)
        for d in (2, 1, 3, 0):
            self.pair_copy(lax.rem(first + d, 4)).start()

    def pair_sum(self):
        for d in (2, 1, 3, 0):
            a = lax.rem(self.axes.first + d, 4)
            self.pair_copy(a).wait_recv()

            def inner(b, carry):
                i = 4 * a + b
                self.g[self.core, i] = (self.g[self.core, i].astype(f32) + self.rx[i].astype(f32)).astype(bf16)
                return carry

            lax.fori_loop(0, 4, inner, 0)
            if d:
                self.first_copy(d).start()

    def first_sum(self):
        for d in range(1, 4):
            self.first_copy(d).wait_recv()
        for d in (2, 1, 3, 0):
            b = lax.rem(self.axes.second + d, 4)
            i = 4 * self.axes.first + b
            total = self.g[self.core, i].astype(f32)
            for k in range(3):
                total = total + self.r1[k, b].astype(f32)
            self.g[self.core, i] = total.astype(bf16)
            if d:
                self.second_copy(d).start()

    def second_sum(self):
        for d in range(1, 4):
            self.second_copy(d).wait_recv()
        total = self.g[self.core, 4 * self.axes.first + self.axes.second].astype(f32)
        for k in range(3):
            total = total + self.r2[k].astype(f32)
        self.x4[self.x] = total.astype(bf16)
        for d in range(1, 4):
            self.third_copy(d, self.x).start()

    def third_sum(self):
        for d in range(1, 4):
            self.third_copy(d, lax.rem(self.x + 4 - d, 4)).wait_recv()
        total = self.x4[0].astype(f32)
        for k in range(1, 4):
            total = total + self.x4[k].astype(f32)
        self.fin[self.core] = total.astype(bf16)
        self.last_copy(self.core).start()

    def finish(self):
        self.last_copy(1 - self.core).wait_recv()

    def drain(self):
        for a in range(4):
            self.pair_copy(a).wait_send()
        for d in range(1, 4):
            self.first_copy(d).wait_send()
            self.second_copy(d).wait_send()
            self.third_copy(d, self.x).wait_send()
        self.last_copy(self.core).wait_send()


def newton_schulz(t_ref, x_ref):
    parts, rows, cols = t_ref.shape
    total = parts * rows
    t = t_ref[...].reshape(total, cols).astype(f32)
    scale = 1.0 / (jnp.sqrt(jnp.sum(t * t)) + 1e-07)
    x_ref[...] = (t * scale).astype(bf16).T

    def advance(_, carry):
        x = x_ref[...]
        gram = lax.dot_general(x, x, NT, preferred_element_type=f32)
        low = gram.astype(bf16)
        square = jnp.dot(low, low, preferred_element_type=f32)
        poly = (poly_second * gram + poly_third * square).astype(bf16)
        for at in range(0, total, 512):
            end = min(at + 512, total)
            part = x_ref[:, at:end]
            x_ref[:, at:end] = (
                poly_first * part.astype(f32) + jnp.dot(poly, part, preferred_element_type=f32)
            ).astype(bf16)
        return carry

    lax.fori_loop(0, NS_ITERS, advance, 0)
    t_ref[...] = x_ref[...].T.reshape(parts, rows, cols)


class Muon:
    @staticmethod
    def scratch(count, rows, cols):
        return [
            pltpu.VMEM((count, rows, cols), bf16),
            pltpu.VMEM((cols, 16 * rows), bf16),
            pltpu.SemaphoreType.DMA((count,)),
            pltpu.SemaphoreType.DMA((16,)),
            pltpu.SemaphoreType.DMA((16,)),
            pltpu.SemaphoreType.DMA((count,)),
        ]

    def __init__(self, owners, out, t, refs):
        self.t = t
        self.u, self.x, self.us, self.uv, self.os, self.ov = refs
        self.out = out
        self.dp, self.ctx, _, self.core = place()
        self.owners = [pick(self.core, a, b) for a, b in zip(*owners)]
        self.mine = self.ctx == self.owners[0]
        self.which = 0
        for m, owner in enumerate(self.owners[1:], 1):
            self.mine = jnp.logical_or(self.mine, self.ctx == owner)
            self.which = self.which + jnp.where(self.ctx == owner, m, 0)

    def up(self, m):
        return remote(
            self.u.at[m], self.t.at[self.ctx], self.us.at[m], self.uv.at[self.ctx],
            {"dp": self.dp, "ctx": self.owners[m]},
        )

    def send(self, m):
        @pl.when(self.ctx != self.owners[m])
        def _():
            self.up(m).start()

        @pl.when(self.ctx == self.owners[m])
        def _():
            self.t[self.ctx] = self.u[m]

    def down(self, peer):
        return remote(
            self.t.at[peer], self.out.at[self.which], self.os.at[peer], self.ov.at[self.which],
            {"dp": self.dp, "ctx": peer},
        )

    def work(self):
        @pl.when(self.mine)
        def _():
            def arrive(d, carry):
                s = lax.rem(self.ctx + d, 16)
                remote(
                    self.t.at[s], self.t.at[s], self.us.at[0], self.uv.at[s], {"dp": self.dp, "ctx": s}
                ).wait_recv()
                return carry

            lax.fori_loop(1, 16, arrive, 0)
            newton_schulz(self.t, self.x)

            def leave(d, carry):
                self.down(lax.rem(self.ctx + d, 16)).start()
                return carry

            lax.fori_loop(1, 16, leave, 0)
            self.out[self.which] = self.t[self.ctx]

            def gone(d, carry):
                self.down(lax.rem(self.ctx + d, 16)).wait_send()
                return carry

            lax.fori_loop(1, 16, gone, 0)

    def collect(self):
        for m, owner in enumerate(self.owners):
            @pl.when(self.ctx != owner)
            def _():
                remote(
                    self.t.at[0], self.out.at[m], self.os.at[0], self.ov.at[m], {"dp": self.dp, "ctx": owner}
                ).wait_recv()
                self.up(m).wait_send()


def update_of(momentum, gradient):
    return gradient + momentum_decay * (momentum_decay * momentum + gradient)


def dot(a, b):
    return jnp.dot(a, b, preferred_element_type=f32)


def rotated(u, cosine, sine):
    first, second = u[0:32], u[32:64]
    return first * cosine - second * sine, second * cosine + first * sine


def two_part(value):
    high = value.astype(bf16)
    return high, (value - high.astype(f32)).astype(bf16)


VALUE_AT = (128, 192, 64)


def layer_kernel(names, *refs):
    r = dict(zip(names, refs))
    dp, ctx, x, core = place()
    axes = Axes()
    barrier = greet_all(dp, ctx)
    A, W = r["A"], r["W"]
    gather_a = Gather(axes, lambda s, c: A.at[c, s], r["ga"])
    gather_w = Gather(axes, lambda s, c: W.at[:, s, pl.ds(pl.multiple_of(48 * c, 16), 48), :], r["gw"])
    ff = Reduce(axes, r["fg"], r["fin_f"], r["rf"])
    at = Reduce(axes, r["ag"], r["fin_a"], r["ra"])
    m_ff = Muon(OWNERS_FF, r["o_ff"], W.at[0], r["mf"])
    m_sq = Muon(OWNERS_SQ, r["o_sq"], W.at[1, :, 0:48], r["ms"])
    m_kv = Muon(OWNERS_KV, r["o_kv"], r["kv_whole"], r["mk"])

    pad, tile = r["pad"], r["tile"]
    pad[...] = jnp.zeros_like(pad)
    tile[...] = jnp.zeros_like(tile)
    tile[0:2, 0:36] = r["gains"][...]
    pad[0, 0:36, 768:896] = tile[...].T[0:36, :]
    for m in range(2):
        pad[m, 0:36, 0:576] = r["w_square"][:, m, :]
        pad[m, 0:36, 576:768] = r["w_kv"][:, m, :]
    for m in range(2):
        A[m, ctx] = pad[m].astype(bf16)
    pl.semaphore_wait(barrier, 19)
    gather_a.start()
    W[0, ctx] = r["w_gate_up"][0].astype(bf16)
    W[1, ctx] = r["w_gate_up"][1].astype(bf16)
    W[2, ctx] = r["w_down"][...].astype(bf16)
    gather_w.start()

    spread_in, spread_out = r["E"], r["ET"]
    row = lax.broadcasted_iota(jnp.int32, (576, 1), 0)
    step = jnp.zeros((576, 1), jnp.int32)
    for t in range(1, 16):
        step = step + (row >= 36 * t).astype(jnp.int32)
    col = lax.broadcasted_iota(jnp.int32, (576, 768), 1)
    spread_in[...] = (col == row + 12 * step).astype(f32).astype(bf16)
    row = lax.broadcasted_iota(jnp.int32, (768, 1), 0)
    step = jnp.zeros((768, 1), jnp.int32)
    for t in range(1, 16):
        step = step + (row >= 48 * t).astype(jnp.int32)
    home = jnp.where(row - 48 * step < 36, row - 12 * step, -1)
    col = lax.broadcasted_iota(jnp.int32, (768, 576), 1)
    spread_out[...] = (col == home).astype(f32).astype(bf16)

    xT = r["tokens"][...].astype(f32)
    r1 = lax.rsqrt(jnp.sum(xT * xT, axis=0, keepdims=True) * (1.0 / 576) + norm_eps)
    hat1 = xT * r1
    r["hat1"][...] = hat1
    high, low = two_part(hat1)
    hat1_wide = dot(spread_out[...], high) + dot(spread_out[...], low)
    pos = r["positions"][...]
    angle = r["freqs"][...] * pos.astype(f32)
    cosine, sine = jnp.cos(angle), jnp.sin(angle)
    r["cos"][...] = cosine
    r["sin"][...] = sine

    gather_a.forward()
    gather_a.swap()
    gather_a.finish()

    n1_wide = (hat1_wide * A[0, :, :, 768:769].reshape(768, 1).astype(f32)).astype(bf16)
    r["n1T"][...] = n1_wide
    n1 = n1_wide.T
    qkT = dot(n1, A[0, :, :, 0:768].reshape(768, 768)).T
    vT = dot(n1, A[1, :, :, 512:768].reshape(768, 256)).T
    kv, kvT, QT = r["kv"], r["kvT"], r["QT"]
    own = []
    for c in range(3):
        a, b = rotated(qkT[576 + 64 * c : 640 + 64 * c], cosine, sine)
        own += [a, b]
    own += [vT[192:256], vT[64:192]]
    kv[ctx] = jnp.concatenate(own, axis=0).T.astype(bf16)
    for i in range(1, 4):
        @pl.when(lax.rem(ctx, 4) + i < 4)
        def _():
            kv[ctx + i] = jnp.zeros((128, 384), bf16)

    def kv_copy(src, dst_rank, sem):
        return remote(kv.at[src], kv.at[src], r["ks"].at[sem], r["kr"].at[src], {"dp": dp, "ctx": dst_rank})

    def kv_send(d, carry):
        kv_copy(ctx, ctx + d, d).start()
        return carry

    lax.fori_loop(1, 16 - ctx, kv_send, 0)
    gather_w.forward()
    QT[...] = jnp.zeros_like(QT)
    for h in range(9):
        c = h // 3
        a, b = rotated(qkT[64 * h : 64 * h + 64], cosine, sine)
        lanes = slice(128 * h, 128 * h + 128)
        QT[64 * c : 64 * c + 32, lanes] = (a.astype(bf16).astype(f32) * 0.125).astype(bf16)
        QT[64 * c + 32 : 64 * c + 64, lanes] = (b.astype(bf16).astype(f32) * 0.125).astype(bf16)

    S, eb, tops, top, total, fade, oT = r["S"], r["eb"], r["tops"], r["top"], r["total"], r["fade"], r["oT"]
    top[...] = jnp.full_like(top, HIDDEN)
    total[...] = jnp.zeros_like(total)
    oT[...] = jnp.zeros_like(oT)
    groups = lax.div(ctx, 4) + 1

    def attend(g, carry):
        for i in range(4):
            j = 4 * g + i

            @pl.when(j < ctx)
            def _():
                kv_copy(j, ctx, 0).wait_recv()

        block = kv[pl.ds(4 * g, 4)].reshape(512, 384)
        kvT[g] = block.T
        S[...] = dot(block[:, 0:256], QT[...])
        key = 512 * g + lax.broadcasted_iota(jnp.int32, (512, 128), 0)
        query = 128 * ctx + lax.broadcasted_iota(jnp.int32, (512, 128), 1)
        allowed = (key <= query) & (key >= query - pos)
        for h in range(9):
            lanes = slice(128 * h, 128 * h + 128)
            s = jnp.where(allowed, S[:, lanes], HIDDEN)
            before = top[:, lanes]
            now = jnp.maximum(before, jnp.max(s, axis=0, keepdims=True))
            weights = jnp.exp(s - now)
            damping = jnp.exp(before - now)
            total[:, lanes] = total[:, lanes] * damping + jnp.sum(weights, axis=0, keepdims=True)
            fade[:, lanes] = damping
            top[:, lanes] = now
            tops[g, :, lanes] = now
            eb[g, :, lanes] = weights.astype(bf16)
        oT[...] = oT[...] * fade[...] + dot(kvT[g, 128:384, :], eb[g])
        return carry

    lax.fori_loop(0, groups, attend, 0)
    share = 1.0 / total[...]
    o = r["o"]
    for h in range(9):
        at_row = VALUE_AT[h // 3]
        lanes = slice(128 * h, 128 * h + 128)
        o[64 * h : 64 * h + 64, :] = oT[at_row : at_row + 64, lanes] * share[:, lanes]
    ob_wide = dot(spread_out[...], o[...].astype(bf16)).astype(bf16)
    r["obT"][...] = ob_wide
    hT = xT + dot(ob_wide.T, A[1, :, :, 0:576].reshape(768, 576)).T
    r2 = lax.rsqrt(jnp.sum(hT * hT, axis=0, keepdims=True) * (1.0 / 576) + norm_eps)
    hat2 = hT * r2
    gain_cols = dot(spread_in[...], A[0, :, :, 768:896].reshape(768, 128))
    n2T = (hat2 * gain_cols[:, 1:2]).astype(bf16)
    n2 = n2T.T

    gather_w.swap()
    gather_w.finish()
    dyT = r["cotangent"][...]
    hidT, dgT, duT = r["hidT"], r["dgT"], r["duT"]
    for y in range(4):
        rows = slice(384 * y, 384 * y + 384)
        parts = slice(4 * y, 4 * y + 4)
        gate = dot(W[0, parts].reshape(384, 576), n2T)
        up = dot(W[1, parts].reshape(384, 576), n2T)
        dhid = dot(W[2, parts].reshape(384, 576), dyT)
        sig = jax.nn.sigmoid(gate)
        silu = gate * sig
        hidT[rows, :] = (silu * up).astype(bf16)
        dgT[rows, :] = (dhid * up * sig * (1.0 + gate * (1.0 - sig))).astype(bf16)
        duT[rows, :] = (dhid * silu).astype(bf16)
    r["outT"][...] = (hT + dot(hidT[...].T, W[2].reshape(1536, 576)).T).astype(bf16)
    dy = dyT.T
    fg = r["fg"]
    for y in range(4):
        rows = slice(384 * y, 384 * y + 384)
        part = dot(dgT[rows, :], n2).astype(bf16)
        for z in range(4):
            fg[0, 4 * z + y, 0:96, :] = part[96 * z : 96 * z + 96]
        part = dot(duT[rows, :], n2).astype(bf16)
        for z in range(4):
            fg[0, 4 * z + y, 96:144, :] = part[96 * z : 96 * z + 48]
            fg[1, 4 * y + z, 0:48, :] = part[96 * z + 48 : 96 * z + 96]
        part = dot(hidT[rows, :], dy).astype(bf16)
        for z in range(4):
            fg[1, 4 * y + z, 48:144, :] = part[96 * z : 96 * z + 96]
    ff.start()
    gather_a.drain()
    gather_w.drain()

    dn2T = (dot(dgT[...].T, W[0].reshape(1536, 576)) + dot(duT[...].T, W[1].reshape(1536, 576))).T
    shaped = dn2T * gain_cols[:, 1:2]
    mean = jnp.sum(shaped * hat2, axis=0, keepdims=True) * (1.0 / 576)
    dhT = dyT.astype(f32) + r2 * (shaped - hat2 * mean)
    r["dhT"][...] = dhT
    gain_two = jnp.sum(dn2T * hat2, axis=1, keepdims=True)
    daT = dhT.astype(bf16)
    r["R"][0:128, 0:576] = daT.T
    dobT = dot(spread_in[...], dot(A[1, :, :, 0:576].reshape(768, 576), daT).astype(bf16))
    dO, dQ, delta = r["dO"], oT, r["delta"]
    dO[...] = jnp.zeros_like(dO)
    dQ[...] = jnp.zeros_like(dQ)
    for h in range(9):
        at_row = VALUE_AT[h // 3]
        lanes = slice(128 * h, 128 * h + 128)
        part = dobT[64 * h : 64 * h + 64]
        dO[at_row : at_row + 64, lanes] = part
        delta[:, lanes] = jnp.sum(part * o[64 * h : 64 * h + 64, :], axis=0, keepdims=True)
    ff.pair_sum()

    dkv_out, dkv_in, dOg = r["dkv_out"], r["dkv_in"], r["dOg"]

    def dkv_copy(j, source):
        return remote(
            dkv_out.at[j], dkv_in.at[source], r["ds_s"].at[j], r["ds_r"].at[source], {"dp": dp, "ctx": j}
        )

    def attend_back(g, carry):
        factor = jnp.exp(tops[g] - top[...]) / total[...]
        dOg[...] = (dO[...] * factor).astype(bf16)
        block = kv[pl.ds(4 * g, 4)].reshape(512, 384)
        S[...] = dot(block[:, 128:384], dOg[...])
        inner = delta[...] * factor
        dv = lax.dot_general(eb[g], dOg[...], NT, preferred_element_type=f32)
        for h in range(9):
            lanes = slice(128 * h, 128 * h + 128)
            eb[g, :, lanes] = (eb[g, :, lanes].astype(f32) * (S[:, lanes] - inner[:, lanes])).astype(bf16)
        dk = lax.dot_general(eb[g], QT[...], NT, preferred_element_type=f32)
        dQ[...] = dQ[...] + dot(kvT[g, 0:256, :], eb[g])
        out = jnp.concatenate([dk[:, 0:128], dk[:, 128:256] + dv[:, 0:128], dv[:, 128:256]], axis=1)
        dkv_out[pl.ds(4 * g, 4)] = out.astype(bf16).reshape(4, 128, 384)
        for i in range(4):
            j = 4 * g + i

            @pl.when(j < ctx)
            def _():
                dkv_copy(j, ctx).start()

        return carry

    lax.fori_loop(0, groups, attend_back, 0)
    ff.first_sum()

    cosine, sine = r["cos"][...], r["sin"][...]
    dqkT = r["dqkT"]
    for h in range(9):
        c = h // 3
        lanes = slice(128 * h, 128 * h + 128)
        a, b = rotated(dQ[64 * c : 64 * c + 64, lanes] * 0.125, cosine, -sine)
        dqkT[64 * h : 64 * h + 32, :] = a.astype(bf16)
        dqkT[64 * h + 32 : 64 * h + 64, :] = b.astype(bf16)

    own_sum = r["own_sum"]
    own_sum[...] = dkv_out[ctx].astype(f32)

    def arrive(d, carry):
        source = ctx + d
        dkv_copy(ctx, source).wait_recv()
        own_sum[...] += dkv_in[source].astype(f32)
        return carry

    lax.fori_loop(1, 16 - ctx, arrive, 0)
    dkvT = own_sum[...].T
    for c in range(3):
        a, b = rotated(dkvT[64 * c : 64 * c + 64], cosine, -sine)
        dqkT[576 + 64 * c : 608 + 64 * c, :] = a.astype(bf16)
        dqkT[608 + 64 * c : 640 + 64 * c, :] = b.astype(bf16)
    dvT = jnp.concatenate([jnp.zeros((64, 128), f32), dkvT[256:384], dkvT[192:256]], axis=0).astype(bf16)

    R, ag, n1T = r["R"], r["ag"], r["n1T"]
    R[0:128, 576:768] = jnp.zeros((128, 192), bf16)
    R[128:256, 0:512] = jnp.zeros((128, 512), bf16)
    R[128:256, 512:768] = dvT.T
    low_rows = (n1T[...], r["obT"][...])
    part = dot(jnp.concatenate([low_rows[1], low_rows[0]], axis=1), R[...]).astype(bf16)
    ag[1, :, :, 0:768] = part.reshape(16, 48, 768)
    ag[1, :, :, 768:896] = jnp.zeros((16, 48, 128), bf16)
    dn1_wide = dot(A[0, :, :, 0:768].reshape(768, 768), dqkT[...]) + dot(
        A[1, :, :, 512:768].reshape(768, 256), dvT
    )
    high, low = two_part(dn1_wide)
    dn1T = dot(spread_in[...], high) + dot(spread_in[...], low)
    hat1 = r["hat1"][...]
    gain_one = jnp.sum(dn1T * hat1, axis=1, keepdims=True)
    lane = lax.broadcasted_iota(jnp.int32, (576, 128), 1)
    columns = jnp.where(lane == 0, gain_one, jnp.where(lane == 1, gain_two, 0.0)).astype(bf16)
    gains_part = dot(spread_out[...], columns).astype(bf16)
    part = dot(n1T[...], dqkT[...].T).astype(bf16)
    for s in range(16):
        i = 4 * (s % 4) + s // 4
        ag[0, i, :, 0:768] = part[48 * s : 48 * s + 48]
        ag[0, i, :, 768:896] = gains_part[48 * s : 48 * s + 48]
    at.start()
    shaped = dn1T * gain_cols[:, 0:1]
    mean = jnp.sum(shaped * hat1, axis=0, keepdims=True) * (1.0 / 576)
    r["ginT"][...] = (r["dhT"][...] + r1 * (shaped - hat1 * mean)).astype(bf16)

    ff.second_sum()
    at.pair_sum()
    ff.third_sum()
    at.first_sum()
    ff.finish()
    fin_f, fin_a = r["fin_f"], r["fin_a"]
    gate_up = r["mom_gate_up"]
    m_ff.u[0] = update_of(gate_up[0], fin_f[0, 0:96].astype(f32)).astype(bf16)
    m_ff.send(0)
    m_ff.u[1, 0:48] = update_of(gate_up[1, 0:48], fin_f[0, 96:144].astype(f32)).astype(bf16)
    m_ff.u[1, 48:96] = update_of(gate_up[1, 48:96], fin_f[1, 0:48].astype(f32)).astype(bf16)
    m_ff.send(1)
    m_ff.u[2] = update_of(r["mom_down"][...], fin_f[1, 48:144].astype(f32)).astype(bf16)
    m_ff.send(2)
    at.second_sum()
    at.third_sum()

    pad[:, 0:36, 768:896] = jnp.zeros((2, 36, 128), f32)
    for m in range(2):
        pad[m, 0:36, 0:576] = r["mom_square"][:, m, :]
        pad[m, 0:36, 576:768] = r["mom_kv"][:, m, :]
    at.finish()
    for m in range(2):
        update = update_of(pad[m], fin_a[m].astype(f32)).astype(bf16)
        m_sq.u[m] = update[:, 0:576]
        m_sq.send(m)
        m_kv.u[m] = update[:, 576:768]
        m_kv.send(m)

    gsend, gain_sums = r["gsend"], r["gain_sums"]
    gain_grads = fin_a[0, :, 768:896].astype(f32).T[0:2, 0:36]
    gain_next = momentum_decay * r["mom_gains"][...] + gain_grads
    sums = jnp.sum(gain_next * gain_next, axis=1, keepdims=True)
    gsend[0:2, :] = jnp.broadcast_to(sums, (2, 128))
    gsend[2:8, :] = jnp.zeros((6, 128), f32)

    def tell(d, slot):
        return remote(
            gsend, gain_sums.at[slot], r["gs"].at[d - 1], r["gv"].at[d - 1],
            {"dp": dp, "ctx": lax.rem(ctx + d, 16)},
        )

    for d in range(1, 16):
        tell(d, ctx).start()
    gain_sums[ctx] = gsend[...]

    m_ff.work()
    m_sq.work()
    m_kv.work()
    m_ff.collect()
    m_sq.collect()
    m_kv.collect()

    for d in range(1, 16):
        tell(d, lax.rem(ctx + 16 - d, 16)).wait_recv()
        tell(d, ctx).wait_send()

    def kv_gone(d, carry):
        kv_copy(ctx, ctx + d, d).wait_send()
        return carry

    lax.fori_loop(1, 16 - ctx, kv_gone, 0)

    def dkv_gone(j, carry):
        dkv_copy(j, ctx).wait_send()
        return carry

    lax.fori_loop(0, ctx, dkv_gone, 0)
    at.drain()
    ff.drain()


def whole(memory=pltpu.VMEM):
    return pl.BlockSpec(memory_space=memory)


def run_layer(inputs):
    outs = {
        "outT": ((576, 128), bf16),
        "ginT": ((576, 128), bf16),
        "fin_f": ((2, 144, 576), bf16),
        "fin_a": ((2, 48, 896), bf16),
        "o_ff": ((3, 96, 576), bf16),
        "o_sq": ((2, 48, 576), bf16),
        "o_kv": ((2, 48, 192), bf16),
        "gain_sums": ((16, 8, 128), f32),
    }
    dma = pltpu.SemaphoreType.DMA
    scratch = {
        "A": pltpu.VMEM((2, 16, 48, 896), bf16),
        "W": pltpu.VMEM((3, 16, 96, 576), bf16),
        "pad": pltpu.VMEM((2, 48, 896), f32),
        "tile": pltpu.VMEM((128, 128), f32),
        "E": pltpu.VMEM((576, 768), bf16),
        "ET": pltpu.VMEM((768, 576), bf16),
        "hat1": pltpu.VMEM((576, 128), f32),
        "cos": pltpu.VMEM((32, 128), f32),
        "sin": pltpu.VMEM((32, 128), f32),
        "n1T": pltpu.VMEM((768, 128), bf16),
        "kv": pltpu.VMEM((16, 128, 384), bf16),
        "kvT": pltpu.VMEM((4, 384, 512), bf16),
        "QT": pltpu.VMEM((256, 1152), bf16),
        "S": pltpu.VMEM((512, 1152), f32),
        "eb": pltpu.VMEM((4, 512, 1152), bf16),
        "tops": pltpu.VMEM((4, 1, 1152), f32),
        "top": pltpu.VMEM((1, 1152), f32),
        "total": pltpu.VMEM((1, 1152), f32),
        "fade": pltpu.VMEM((1, 1152), f32),
        "delta": pltpu.VMEM((1, 1152), f32),
        "oT": pltpu.VMEM((256, 1152), f32),
        "o": pltpu.VMEM((576, 128), f32),
        "obT": pltpu.VMEM((768, 128), bf16),
        "hidT": pltpu.VMEM((1536, 128), bf16),
        "dgT": pltpu.VMEM((1536, 128), bf16),
        "duT": pltpu.VMEM((1536, 128), bf16),
        "fg": pltpu.VMEM((2, 16, 144, 576), bf16),
        "dhT": pltpu.VMEM((576, 128), f32),
        "R": pltpu.VMEM((256, 768), bf16),
        "dO": pltpu.VMEM((256, 1152), f32),
        "dOg": pltpu.VMEM((256, 1152), bf16),
        "dkv_out": pltpu.VMEM((16, 128, 384), bf16),
        "dkv_in": pltpu.VMEM((16, 128, 384), bf16),
        "own_sum": pltpu.VMEM((128, 384), f32),
        "dqkT": pltpu.VMEM((768, 128), bf16),
        "ag": pltpu.VMEM((2, 16, 48, 896), bf16),
        "gsend": pltpu.VMEM((8, 128), f32),
        "gs": dma((15,)),
        "gv": dma((15,)),
        "ks": dma((16,)),
        "kr": dma((16,)),
        "ds_s": dma((16,)),
        "ds_r": dma((16,)),
        "ga": Gather.scratch(),
        "gw": Gather.scratch(),
        "rf": Reduce.scratch(144, 576),
        "ra": Reduce.scratch(48, 896),
        "kv_whole": pltpu.VMEM((16, 48, 192), bf16),
        "mf": Muon.scratch(3, 96, 576),
        "ms": Muon.scratch(2, 48, 576),
        "mk": Muon.scratch(2, 48, 192),
    }
    names = [*inputs, *outs, *scratch]
    scratch_list = list(scratch.values())

    def kernel(*refs):
        layer_kernel(names, *refs)

    return pl.pallas_call(
        kernel,
        out_shape=tuple(jax.ShapeDtypeStruct(*o) for o in outs.values()),
        in_specs=[whole()] * len(inputs),
        out_specs=[whole()] * len(outs),
        scratch_shapes=scratch_list,
        compiler_params=pltpu.CompilerParams(
            collective_id=3, has_side_effects=True, vmem_limit_bytes=VMEM_LIMIT
        ),
    )(*inputs.values())


VMEM_LIMIT = 63 * 2**20


def finish_kernel(
    outT, ginT, fin_f, fin_a, o_ff, o_sq, o_kv, gain_sums, w_square, w_kv, w_gate_up, w_down, gains,
    mom_square, mom_kv, mom_gate_up, mom_down, mom_gains,
    out, gin, grad_square, grad_kv, grad_gate_up, grad_down, grad_gains,
    next_square, next_kv, next_gate_up, next_down, next_gains,
    new_square, new_kv, new_gate_up, new_down, new_gains,
):
    shrink = 1.0 - learn_rate * weight_decay
    out[...] = outT[...]
    gin[...] = ginT[...]

    def one(at, grad, width, weight, momentum, ortho, grad_out, next_out, new_out):
        grad_out[at] = grad
        next_out[at] = momentum_decay * momentum[at] + grad
        new_out[at] = shrink * weight[at] - learn_rate * (0.2 * math.sqrt(width)) * ortho

    everything = slice(None)
    for m in range(2):
        rows = (everything, m, everything)
        one(rows, fin_a[m, :, 0:576].astype(f32)[0:36], 576, w_square, mom_square,
            o_sq[m].astype(f32)[0:36], grad_square, next_square, new_square)
        one(rows, fin_a[m, :, 576:768].astype(f32)[0:36], 576, w_kv, mom_kv,
            o_kv[m].astype(f32)[0:36], grad_kv, next_kv, new_kv)
    one((0, everything), fin_f[0, 0:96].astype(f32), 1536, w_gate_up, mom_gate_up,
        o_ff[0].astype(f32), grad_gate_up, next_gate_up, new_gate_up)
    one((1, slice(0, 48)), fin_f[0, 96:144].astype(f32), 1536, w_gate_up, mom_gate_up,
        o_ff[1, 0:48].astype(f32), grad_gate_up, next_gate_up, new_gate_up)
    one((1, slice(48, 96)), fin_f[1, 0:48].astype(f32), 1536, w_gate_up, mom_gate_up,
        o_ff[1, 48:96].astype(f32), grad_gate_up, next_gate_up, new_gate_up)
    one(everything, fin_f[1, 48:144].astype(f32), 1536, w_down, mom_down,
        o_ff[2].astype(f32), grad_down, next_down, new_down)
    gain_grads = fin_a[0, :, 768:896].astype(f32).T[0:2, 0:36]
    gain_next = momentum_decay * mom_gains[...] + gain_grads
    total = gain_sums[0]
    for k in range(1, 16):
        total = total + gain_sums[k]
    mean = total[0:2, 0:1] * (1.0 / 576)
    grad_gains[...] = gain_grads
    next_gains[...] = gain_next
    new_gains[...] = gains[...] - gain_rate * gain_next / jnp.sqrt(mean + 1e-06)


def finish(packed, weights, momenta):
    shapes = [jax.ShapeDtypeStruct((576, 128), bf16)] * 2
    shapes += [jax.ShapeDtypeStruct(a.shape, f32) for a in weights] * 3
    return pl.pallas_call(
        finish_kernel,
        out_shape=tuple(shapes),
        in_specs=[whole()] * 18,
        out_specs=[whole()] * 17,
        compiler_params=pltpu.CompilerParams(vmem_limit_bytes=VMEM_LIMIT),
    )(*packed, *weights, *momenta)


def swapped(a):
    return jnp.transpose(a, (1, 0, 2))


def shards(
    tokens, positions, cotangent, w_square, w_kv, w_gate_up, w_down, gains,
    mom_square, mom_kv, mom_gate_up, mom_down, mom_gains,
):
    weights = (swapped(w_square), swapped(w_kv), w_gate_up, w_down, gains)
    momenta = (swapped(mom_square), swapped(mom_kv), mom_gate_up, mom_down, mom_gains)
    freqs = np.float32(rope_base) ** (-2.0 * np.arange(32, dtype=np.float32) / 64).astype(np.float32)
    inputs = {
        "tokens": tokens[0].T,
        "positions": positions,
        "cotangent": cotangent[0].T,
        "freqs": jnp.asarray(np.broadcast_to(freqs[:, None], (32, 128)), f32),
        **dict(zip(("w_square", "w_kv", "w_gate_up", "w_down", "gains"), weights)),
        **dict(zip(("mom_square", "mom_kv", "mom_gate_up", "mom_down", "mom_gains"), momenta)),
    }
    outs = list(finish(run_layer(inputs), weights, momenta))
    outs[0] = outs[0].T[None]
    outs[1] = outs[1].T[None]
    for i in (2, 3, 7, 8, 12, 13):
        outs[i] = swapped(outs[i])
    return tuple(outs)


def solution(mesh):
    return jax.shard_map(
        shards,
        mesh=mesh,
        in_specs=(
            P("dp", "ctx", None),
            P("dp", "ctx"),
            P("dp", "ctx", None),
            P(None, "ctx", None),
            P(None, "ctx", None),
            P(None, "ctx", None),
            P("ctx", None),
            P(None, "ctx"),
            P(None, "ctx", None),
            P(None, "ctx", None),
            P(None, "ctx", None),
            P("ctx", None),
            P(None, "ctx"),
        ),
        out_specs=(
            P("dp", "ctx", None),
            P("dp", "ctx", None),
            *(P(None, "ctx", None), P(None, "ctx", None), P(None, "ctx", None), P("ctx", None), P(None, "ctx")) * 3,
        ),
        check_vma=False,
    )
```

```python
import math
import types

import jax
import jax.numpy as jnp
from jax import lax
from jax.experimental import pallas as pl
from jax.experimental.pallas import tpu as pltpu
from jax.sharding import PartitionSpec as P

HEAD_WIDTH = 64
NS_ITERS = 5

norm_eps = 1e-05
rope_base = 100000.0
momentum_decay = 0.95
learn_rate = 0.2
weight_decay = 0.1
gain_rate = 0.25
poly_first = 3.4445
poly_second = -4.775
poly_third = 2.0315

MESH = pl.DeviceIdType.MESH
bf16 = jnp.bfloat16
f32 = jnp.float32
NT = (((1,), (1,)), ((), ()))
TN = (((0,), (0,)), ((), ()))
HIDDEN = -1e30

OWNERS_FF = ((0, 5, 10), (15, 2, 8))
OWNERS_SQ = ((3, 12), (7, 13))
OWNERS_KV = ((6, 9), (4, 1))


def place():
    dp = lax.axis_index("dp")
    ctx = lax.axis_index("ctx")
    core = lax.rem(dp, 2)
    return dp, ctx, lax.div(dp, 2), core


def pick(core, first, second):
    return first + core * (second - first)


def remote(src, dst, send_sem, recv_sem, device):
    return pltpu.make_async_remote_copy(
        src_ref=src, dst_ref=dst, send_sem=send_sem, recv_sem=recv_sem, device_id=device, device_id_type=MESH
    )


def greet_all(dp, ctx):
    barrier = pltpu.get_barrier_semaphore()
    for d in range(1, 16):
        pl.semaphore_signal(
            barrier, inc=1, device_id={"dp": dp, "ctx": lax.rem(ctx + d, 16)}, device_id_type=MESH
        )
    for d in range(1, 4):
        pl.semaphore_signal(
            barrier, inc=1, device_id={"dp": lax.rem(dp + 2 * d, 8), "ctx": ctx}, device_id_type=MESH
        )
    pl.semaphore_signal(
        barrier, inc=1, device_id={"dp": dp + 1 - 2 * lax.rem(dp, 2), "ctx": ctx}, device_id_type=MESH
    )
    return barrier


class Axes:
    def __init__(self):
        self.dp, self.ctx, self.x, self.core = place()
        y, z = lax.div(self.ctx, 4), lax.rem(self.ctx, 4)
        self.first = pick(self.core, z, y)
        self.second = pick(self.core, y, z)
        self.sa = pick(self.core, 1, 4)
        self.sb = pick(self.core, 4, 1)
        self.sibling = {"dp": self.dp + 1 - 2 * self.core, "ctx": self.ctx}

    def near(self, d):
        a = lax.rem(self.first + d, 4)
        return {"dp": self.dp, "ctx": self.ctx + (a - self.first) * self.sa}

    def far(self, d):
        b = lax.rem(self.second + d, 4)
        return {"dp": self.dp, "ctx": self.ctx + (b - self.second) * self.sb}

    def beside(self, before):
        return {"dp": lax.rem(self.dp + pick(before, 2, 6), 8), "ctx": self.ctx}

    def slice_at(self, back_first, back_second):
        a = lax.rem(self.first + 4 - back_first, 4)
        b = lax.rem(self.second + 4 - back_second, 4)
        return a * self.sa + b * self.sb


class Gather:
    @staticmethod
    def scratch():
        return [
            pltpu.SemaphoreType.DMA((3,)),
            pltpu.SemaphoreType.DMA((3,)),
            pltpu.SemaphoreType.DMA((4, 3)),
            pltpu.SemaphoreType.DMA((4, 3)),
            pltpu.SemaphoreType.DMA((16,)),
            pltpu.SemaphoreType.DMA((16,)),
        ]

    def __init__(self, axes, region, refs):
        self.axes, self.region = axes, region
        self.s1, self.v1, self.s2, self.v2, self.sp, self.vp = refs

    def move(self, s, ssem, vsem, device, core=None):
        part = self.region(s, self.axes.core if core is None else core)
        return remote(part, part, ssem, vsem, device)

    def first_copy(self, d, s):
        return self.move(s, self.s1.at[d - 1], self.v1.at[d - 1], self.axes.near(d))

    def second_copy(self, e, d, s):
        return self.move(s, self.s2.at[e, d - 1], self.v2.at[e, d - 1], self.axes.far(d))

    def pair_copy(self, s, core=None):
        return self.move(s, self.sp.at[s], self.vp.at[s], self.axes.sibling, core)

    def start(self):
        for d in (2, 1, 3):
            self.first_copy(d, self.axes.ctx).start()

    def forward(self):
        for d in (2, 1, 3):
            self.second_copy(0, d, self.axes.ctx).start()
        for e in (1, 3, 2):
            s = self.axes.slice_at(e, 0)
            self.first_copy(e, s).wait_recv()
            for d in (2, 1, 3):
                self.second_copy(e, d, s).start()
            self.pair_copy(s).start()

    def swap(self):
        for e in (0, 1, 3, 2):
            for d in (1, 3, 2):
                s = self.axes.slice_at(e, d)
                self.second_copy(e, d, s).wait_recv()
                self.pair_copy(s).start()

    def finish(self):
        def step(i, carry):
            s = lax.rem(self.axes.ctx + i, 16)
            self.pair_copy(s, 1 - self.axes.core).wait_recv()
            return carry

        lax.fori_loop(1, 16, step, 0)

    def drain(self):
        for d in range(1, 4):
            self.first_copy(d, self.axes.ctx).wait_send()
            for e in range(4):
                self.second_copy(e, d, self.axes.ctx).wait_send()

        def step(i, carry):
            self.pair_copy(lax.rem(self.axes.ctx + i, 16)).wait_send()
            return carry

        lax.fori_loop(1, 16, step, 0)


class SideGather:
    @staticmethod
    def scratch():
        dma = pltpu.SemaphoreType.DMA
        return [dma((3,)), dma((3,)), dma((4, 3)), dma((4, 3)), dma((16,)), dma((16,)), dma((2, 16)), dma((2, 16))]

    def __init__(self, axes, pack, refs):
        self.axes, self.pack = axes, pack
        self.s1, self.v1, self.s2, self.v2, self.sx, self.vx, self.sp, self.vp = refs
        self.fetched = lax.rem(axes.x, 2)
        self.missing = 1 - self.fetched

    def move(self, m, s, half, ssem, vsem, device):
        part = self.pack.at[m, half, s]
        return remote(part, part, ssem, vsem, device)

    def first_copy(self, d, s):
        return self.move(self.fetched, s, self.axes.core, self.s1.at[d - 1], self.v1.at[d - 1], self.axes.near(d))

    def second_copy(self, e, d, s):
        return self.move(
            self.fetched, s, self.axes.core, self.s2.at[e, d - 1], self.v2.at[e, d - 1], self.axes.far(d)
        )

    def side_copy(self, m, s):
        return self.move(m, s, self.axes.core, self.sx.at[s], self.vx.at[s], self.axes.beside(self.axes.core))

    def pair_copy(self, m, s, half):
        return self.move(m, s, half, self.sp.at[m, s], self.vp.at[m, s], self.axes.sibling)

    def start(self):
        for d in (2, 1, 3):
            self.first_copy(d, self.axes.ctx).start()

    def arrived(self, s):
        self.side_copy(self.fetched, s).start()
        self.pair_copy(self.fetched, s, self.axes.core).start()

    def forward(self):
        for d in (2, 1, 3):
            self.second_copy(0, d, self.axes.ctx).start()
        for e in (1, 3, 2):
            s = self.axes.slice_at(e, 0)
            self.first_copy(e, s).wait_recv()
            for d in (2, 1, 3):
                self.second_copy(e, d, s).start()
            self.arrived(s)

    def swap(self):
        for e in (0, 1, 3, 2):
            for d in (1, 3, 2):
                s = self.axes.slice_at(e, d)
                self.second_copy(e, d, s).wait_recv()
                self.arrived(s)

    def side(self):
        for d in (0, 1, 3, 2):
            for e in (1, 3, 2, 0):
                if d or e:
                    s = self.axes.slice_at(e, d)
                    self.side_copy(self.missing, s).wait_recv()
                    self.pair_copy(self.missing, s, self.axes.core).start()

    def finish(self):
        def step(i, carry):
            s = lax.rem(self.axes.ctx + i, 16)
            for m in range(2):
                self.pair_copy(m, s, 1 - self.axes.core).wait_recv()
            return carry

        lax.fori_loop(1, 16, step, 0)

    def drain(self):
        for d in range(1, 4):
            self.first_copy(d, self.axes.ctx).wait_send()
            for e in range(4):
                self.second_copy(e, d, self.axes.ctx).wait_send()

        def step(i, carry):
            s = lax.rem(self.axes.ctx + i, 16)
            self.side_copy(self.fetched, s).wait_send()
            for m in range(2):
                self.pair_copy(m, s, self.axes.core).wait_send()
            return carry

        lax.fori_loop(1, 16, step, 0)


class SplitGather:
    @staticmethod
    def scratch():
        dma = pltpu.SemaphoreType.DMA
        return [dma((2, 3)), dma((2, 3)), dma((2, 3)), dma((2, 3))]

    def __init__(self, axes, whole_ref, refs):
        self.axes, self.whole = axes, whole_ref
        self.s, self.v, self.sx, self.vx = refs
        self.odd = lax.rem(axes.x, 2)

    def region(self, k, odd, p):
        if k == 0:
            return self.whole.at[2 * odd, p]
        return self.whole.at[1, p, pl.ds(pl.multiple_of(48 * odd, 16), 48), :]

    def far_copy(self, k, d, p):
        part = self.region(k, self.odd, p)
        return remote(part, part, self.s.at[k, d - 1], self.v.at[k, d - 1], self.axes.far(d))

    def side_copy(self, k, d, p, odd):
        part = self.region(k, odd, p)
        side = self.axes.core if k == 0 else 1 - self.axes.core
        return remote(part, part, self.sx.at[k, d - 1], self.vx.at[k, d - 1], self.axes.beside(side))

    def place(self, d):
        return lax.rem(self.axes.second + 4 - d, 4)

    def start(self):
        for k in range(2):
            for d in (2, 1, 3):
                self.far_copy(k, d, self.axes.second).start()

    def forward(self):
        for k in range(2):
            for d in (1, 3, 2):
                p = self.place(d)
                self.far_copy(k, d, p).wait_recv()
                self.side_copy(k, d, p, self.odd).start()

    def wait(self):
        for k in range(2):
            for d in (1, 3, 2):
                self.side_copy(k, d, self.place(d), 1 - self.odd).wait_recv()

    def drain(self):
        for k in range(2):
            for d in range(1, 4):
                self.far_copy(k, d, self.axes.second).wait_send()
                self.side_copy(k, d, self.place(d), self.odd).wait_send()


class Along:
    @staticmethod
    def scratch():
        return [pltpu.SemaphoreType.DMA((3,)), pltpu.SemaphoreType.DMA((3,))]

    def __init__(self, axes, axis, src, dst, refs):
        self.src, self.dst = src, dst
        self.ssem, self.vsem = refs
        self.me = axes.second if axis else axes.first
        self.peer = axes.far if axis else axes.near

    def copy(self, d):
        return remote(
            self.src(lax.rem(self.me + d, 4)), self.dst(self.me), self.ssem.at[d - 1], self.vsem.at[d - 1],
            self.peer(d),
        )

    def start(self):
        for d in (2, 1, 3):
            self.copy(d).start()

    def wait(self):
        for d in range(1, 4):
            part = self.dst(lax.rem(self.me + 4 - d, 4))
            remote(part, part, self.ssem.at[d - 1], self.vsem.at[d - 1], self.peer(d)).wait_recv()

    def drain(self):
        for d in range(1, 4):
            self.copy(d).wait_send()


class Reduce:
    @staticmethod
    def scratch(rows, cols, halves):
        dma = pltpu.SemaphoreType.DMA
        part = (rows // 2, cols) if halves else (rows, cols)
        return [
            pltpu.VMEM((4, rows, cols), bf16),
            pltpu.VMEM((2, *part), bf16),
            pltpu.VMEM(part, bf16),
            pltpu.VMEM((4, *part), bf16),
            Along.scratch(),
            dma((1,)),
            dma((1,)),
            dma((3,)),
            dma((3,)),
            dma((1,)),
            dma((1,)),
        ]

    def __init__(self, axes, g, fin, halves, refs):
        self.axes, self.g, self.fin, self.halves = axes, g, fin, halves
        self.r2, self.h, self.hx, self.x4, along, self.s0, self.v0, self.s3, self.v3, self.s4, self.v4 = refs
        self.core, self.x = axes.core, axes.x
        self.second = Along(axes, 1, lambda p: g.at[p], lambda p: self.r2.at[p], along)

    def pair_copy(self):
        other = 1 - self.core if self.halves else 0
        return remote(self.h.at[other], self.hx, self.s0.at[0], self.v0.at[0], self.axes.sibling)

    def third_copy(self, d, slot):
        peer = {"dp": lax.rem(self.axes.dp + 2 * d, 8), "ctx": self.axes.ctx}
        return remote(self.x4.at[slot], self.x4.at[slot], self.s3.at[d - 1], self.v3.at[d - 1], peer)

    def last_copy(self, half):
        return remote(self.fin.at[half], self.fin.at[half], self.s4.at[0], self.v4.at[0], self.axes.sibling)

    def start(self):
        self.second.start()

    def second_sum(self):
        self.second.wait()
        me = self.axes.second
        total = self.g[me].astype(f32)
        for d in range(1, 4):
            total = total + self.r2[lax.rem(me + d, 4)].astype(f32)
        total = total.astype(bf16)
        rows = total.shape[0] // 2
        if self.halves:
            self.h[0] = total[0:rows]
            self.h[1] = total[rows:]
        else:
            self.h[0] = total
        self.pair_copy().start()

    def pair_sum(self):
        self.pair_copy().wait_recv()
        mine = self.h[self.core if self.halves else 0]
        self.x4[self.x] = (mine.astype(f32) + self.hx[...].astype(f32)).astype(bf16)
        for d in (2, 1, 3):
            self.third_copy(d, self.x).start()

    def third_sum(self):
        for d in range(1, 4):
            self.third_copy(d, lax.rem(self.x + 4 - d, 4)).wait_recv()
        total = self.x4[0].astype(f32)
        for k in range(1, 4):
            total = total + self.x4[k].astype(f32)
        if self.halves:
            self.fin[self.core] = total.astype(bf16)
            self.last_copy(self.core).start()
        else:
            self.fin[...] = total.astype(bf16)

    def finish(self):
        if self.halves:
            self.last_copy(1 - self.core).wait_recv()

    def drain(self):
        self.second.drain()
        self.pair_copy().wait_send()
        for d in range(1, 4):
            self.third_copy(d, self.x).wait_send()
        if self.halves:
            self.last_copy(self.core).wait_send()


def blocks(size):
    return [(b, min(b + 256, size)) for b in range(0, size, 256)]


def mirror(dst, lows):
    size = dst.shape[0]
    for low, (b, e) in zip(lows, blocks(size)):
        dst[b:size, b:e] = low
        if e < size:
            dst[b:e, e:size] = low[e - b :].T


def diagonal(rows, cols):
    shape = (rows, cols)
    return lax.broadcasted_iota(jnp.int32, shape, 0) == lax.broadcasted_iota(jnp.int32, shape, 1)


def newton_schulz_step(x_ref, a_ref, p_ref, first):
    size, total = x_ref.shape
    parts = blocks(size)
    gram = [
        lax.dot_general(x_ref[b:size, :], x_ref[b:e, :], NT, preferred_element_type=f32) for b, e in parts
    ]
    if first:
        squares = 0.0
        for g, (b, e) in zip(gram, parts):
            squares = squares + jnp.sum(jnp.where(diagonal(e - b, e - b), g[0 : e - b], 0.0))
        scale = 1.0 / (jnp.sqrt(squares) + 1e-07)
        gram = [g * (scale * scale) for g in gram]
    mirror(a_ref, [g.astype(bf16) for g in gram])
    poly = []
    for g, (b, e) in zip(gram, parts):
        value = poly_second * g + poly_third * dot(a_ref[b:size, :], a_ref[:, b:e])
        value = value + jnp.where(diagonal(size - b, e - b), poly_first, 0.0)
        poly.append((value * scale if first else value).astype(bf16))
    mirror(p_ref, poly)
    for at in range(0, total, 512):
        end = min(at + 512, total)
        x_ref[:, at:end] = dot(p_ref[...], x_ref[:, at:end]).astype(bf16)


class Muon:
    @staticmethod
    def scratch(count, rows, cols):
        return [
            pltpu.VMEM((count, rows, cols), bf16),
            pltpu.SemaphoreType.DMA((count,)),
            pltpu.SemaphoreType.DMA((16,)),
            pltpu.SemaphoreType.DMA((16,)),
            pltpu.SemaphoreType.DMA((count,)),
            pltpu.SemaphoreType.DMA((count,)),
            pltpu.SemaphoreType.DMA((count,)),
        ]

    def __init__(self, owners, out, t, work, halves, refs):
        self.t, self.halves = t, halves
        self.u, self.us, self.uv, self.os, self.ov, self.ps, self.pv = refs
        _, self.rows, self.cols = self.u.shape
        x, a, p = work
        self.x = x.at[0 : self.cols, 0 : 16 * self.rows]
        self.a, self.p = a, p
        self.out = out
        self.dp, self.ctx, _, self.core = place()
        self.owners = [pick(self.core, a, b) for a, b in zip(*owners)]
        self.mine = self.ctx == self.owners[0]
        self.which = 0
        for m, owner in enumerate(self.owners[1:], 1):
            self.mine = jnp.logical_or(self.mine, self.ctx == owner)
            self.which = self.which + jnp.where(self.ctx == owner, m, 0)

    def up(self, m):
        return remote(
            self.u.at[m], self.t.at[self.ctx], self.us.at[m], self.uv.at[self.ctx],
            {"dp": self.dp, "ctx": self.owners[m]},
        )

    def send(self, m):
        @pl.when(self.ctx != self.owners[m])
        def _():
            self.up(m).start()

        @pl.when(self.ctx == self.owners[m])
        def _():
            self.t[self.ctx] = self.u[m]

    def part(self, ref, i, core):
        if self.halves:
            half = self.rows // 2
            return ref.at[i, pl.ds(pl.multiple_of(half * core, 16), half), :]
        return ref.at[i]

    def down(self, peer):
        return remote(
            self.part(self.t, peer, self.core), self.part(self.out, self.which, self.core),
            self.os.at[peer], self.ov.at[self.which], {"dp": self.dp, "ctx": peer},
        )

    def pair_copy(self, m, core):
        part = self.part(self.out, m, core)
        sibling = {"dp": self.dp + 1 - 2 * self.core, "ctx": self.ctx}
        return remote(part, part, self.ps.at[m], self.pv.at[m], sibling)

    def begin(self):
        @pl.when(self.mine)
        def _():
            def arrive(d, carry):
                s = lax.rem(self.ctx + d, 16)
                remote(
                    self.t.at[s], self.t.at[s], self.us.at[0], self.uv.at[s], {"dp": self.dp, "ctx": s}
                ).wait_recv()
                return carry

            lax.fori_loop(1, 16, arrive, 0)
            self.x[...] = self.t[...].reshape(16 * self.rows, self.cols).T
            newton_schulz_step(self.x, self.a, self.p, True)

    def go_on(self, steps):
        @pl.when(self.mine)
        def _():
            def step(_, carry):
                newton_schulz_step(self.x, self.a, self.p, False)
                return carry

            lax.fori_loop(0, steps, step, 0)

    def end(self):
        @pl.when(self.mine)
        def _():
            self.t[...] = self.x[...].T.reshape(16, self.rows, self.cols)

            def leave(d, carry):
                self.down(lax.rem(self.ctx + d, 16)).start()
                return carry

            lax.fori_loop(1, 16, leave, 0)
            self.part(self.out, self.which, self.core)[...] = self.part(self.t, self.ctx, self.core)[...]

            def gone(d, carry):
                self.down(lax.rem(self.ctx + d, 16)).wait_send()
                return carry

            lax.fori_loop(1, 16, gone, 0)

    def collect(self):
        for m, owner in enumerate(self.owners):
            @pl.when(self.ctx != owner)
            def _():
                part = self.part(self.out, m, self.core)
                remote(part, part, self.os.at[0], self.ov.at[m], {"dp": self.dp, "ctx": owner}).wait_recv()
                self.up(m).wait_send()

            if self.halves:
                self.pair_copy(m, self.core).start()
        if self.halves:
            for m in range(len(self.owners)):
                self.pair_copy(m, 1 - self.core).wait_recv()
                self.pair_copy(m, self.core).wait_send()


def update_of(momentum, gradient):
    return gradient + momentum_decay * (momentum_decay * momentum + gradient)


def dot(a, b):
    return jnp.dot(a, b, preferred_element_type=f32)


def rotated(u, cosine, sine):
    first, second = u[0:32], u[32:64]
    return first * cosine - second * sine, second * cosine + first * sine


def two_part(value):
    high = value.astype(bf16)
    return high, (value - high.astype(f32)).astype(bf16)


VALUE_AT = (128, 192, 64)


def layer_kernel(names, *refs):
    r = types.SimpleNamespace(**dict(zip(names, refs)))
    dp, ctx, x, core = place()
    axes = Axes()
    first, second, sa, sb = axes.first, axes.second, axes.sa, axes.sb
    barrier = greet_all(dp, ctx)
    K, QO, W = r.K, r.QO, r.W
    Q, O = QO.at[0], QO.at[1]
    gather_k = Gather(axes, lambda s, c: K.at[c, s], r.gk)
    gather_qo = SideGather(axes, QO, r.gqo)
    gather_w = SplitGather(axes, W, r.gw)

    def lanes_at(p):
        return pl.ds(pl.multiple_of(128 * p, 128), 128)

    def spread(buffer, refs):
        return Along(axes, 0, lambda p: buffer.at[:, lanes_at(first)], lambda p: buffer.at[:, lanes_at(p)], refs)

    def deliver(source, target, refs):
        return Along(axes, 0, lambda p: source.at[p], lambda p: target.at[p], refs)

    N2, DY, DA, DQ, DKV = r.N2, r.DY, r.DA, r.DQ, r.DKV
    share_n2, share_dy = spread(N2, r.c_n2), spread(DY, r.c_dy)
    share_da, share_dq, share_dkv = spread(DA, r.c_da), spread(DQ, r.c_dq), spread(DKV, r.c_dkv)
    send_n1 = deliver(r.n1s, r.N1, r.c_n1)
    send_ob = deliver(r.obs, r.OB, r.c_ob)
    send_out = deliver(r.outs, r.outr, r.c_out)
    send_dn = deliver(r.dns, r.dnr, r.c_dn)
    send_gain = deliver(r.gps, r.gpr, r.c_gain)

    fin_f = r.fin_f
    ff = [Reduce(axes, r.fg.at[m], fin_f.at[m], True, r.rf[m]) for m in range(3)]
    sum_q = Reduce(axes, r.qg, r.fin_q, False, r.rq)
    sum_o = Reduce(axes, r.og, r.fin_o, False, r.ro)
    sum_k = Reduce(axes, r.kg, r.fin_k, False, r.rk)
    work = (r.nx, r.na, r.np)
    m_ff = Muon(OWNERS_FF, r.o_ff, r.whole, work, True, r.mf)
    m_sq = Muon(OWNERS_SQ, r.o_sq, r.whole.at[:, 0:48], work, False, r.ms)
    m_kv = Muon(OWNERS_KV, r.o_kv, r.kv_whole, (r.nx, r.ka, r.kp), False, r.mk)

    def grouped(buffer, value):
        for s in range(16):
            a, b = pick(core, s % 4, s // 4), pick(core, s // 4, s % 4)
            buffer[a, pl.ds(pl.multiple_of(48 * b, 16), 48), :] = value[48 * s : 48 * s + 48]

    pad_sq, pad_kv, tile = r.pad_sq, r.pad_kv, r.tile
    pad_sq[...] = jnp.zeros_like(pad_sq)
    pad_kv[...] = jnp.zeros_like(pad_kv)
    tile[...] = jnp.zeros_like(tile)
    tile[64:66, 0:36] = r.gains[...]
    pad_kv[0, 0:36, 128:256] = tile[...].T[0:36, :]
    for m in range(2):
        pad_sq[m, 0:36, 0:576] = r.w_square[:, m, :]
        pad_kv[m, 0:36, 0:192] = r.w_kv[:, m, :]
        K[m, ctx] = pad_kv[m].astype(bf16)
    for half in range(2):
        for m in range(2):
            QO[m, half, ctx] = pad_sq[m, :, 384 * half : 384 * half + 384].astype(bf16)
    W[0, second] = r.w_gate_up[0].astype(bf16)
    W[1, second] = r.w_gate_up[1].astype(bf16)
    W[2, second] = r.w_down[...].astype(bf16)
    pl.semaphore_wait(barrier, 19)
    gather_k.start()
    gather_qo.start()
    gather_w.start()
    DY[:, lanes_at(first)] = r.cotangent[...]

    spread_in, spread_out = r.E, r.ET
    row = lax.broadcasted_iota(jnp.int32, (768, 1), 0)
    step = jnp.zeros((768, 1), jnp.int32)
    for t in range(1, 16):
        step = step + (row >= 48 * t).astype(jnp.int32)
    home = jnp.where(row - 48 * step < 36, row - 12 * step, -1)
    col = lax.broadcasted_iota(jnp.int32, (768, 576), 1)
    spread_out[...] = (col == home).astype(f32).astype(bf16)

    xT = r.tokens[...].astype(f32)
    r1 = lax.rsqrt(jnp.sum(xT * xT, axis=0, keepdims=True) * (1.0 / 576) + norm_eps)
    hat1 = xT * r1
    r.hat1[...] = hat1
    high, low = two_part(hat1)
    hat1_wide = dot(spread_out[...], high) + dot(spread_out[...], low)
    gather_k.forward()
    gather_qo.forward()
    row = lax.broadcasted_iota(jnp.int32, (576, 1), 0)
    step = jnp.zeros((576, 1), jnp.int32)
    for t in range(1, 16):
        step = step + (row >= 36 * t).astype(jnp.int32)
    col = lax.broadcasted_iota(jnp.int32, (576, 768), 1)
    spread_in[...] = (col == row + 12 * step).astype(f32).astype(bf16)
    pos = r.positions[...]
    row = lax.broadcasted_iota(jnp.int32, (32, 128), 0)
    freqs = jnp.zeros((32, 128), f32)
    for i in range(32):
        freqs = jnp.where(row == i, rope_base ** (-2.0 * i / HEAD_WIDTH), freqs)
    angle = freqs * pos.astype(f32)
    cosine, sine = jnp.cos(angle), jnp.sin(angle)
    r.cos[...] = cosine
    r.sin[...] = sine
    gather_w.forward()
    gather_k.swap()
    gather_k.finish()

    n1_wide = (hat1_wide * K[0, :, :, 192:193].reshape(768, 1).astype(f32)).astype(bf16)
    n1 = n1_wide.T
    kT = dot(n1, K[0].reshape(768, 256)).T
    vT = dot(n1, K[1].reshape(768, 256)).T
    kv, kvT, QT = r.kv, r.kvT, r.QT
    own = []
    for c in range(3):
        own += rotated(kT[64 * c : 64 * c + 64], cosine, sine)
    own += [vT[128:192], vT[0:128]]
    kv[ctx] = jnp.concatenate(own, axis=0).T.astype(bf16)

    def slice_of(a, b):
        return a * sa + b * sb

    def reach(a):
        return a * sa + 3 * sb

    def kv_near(d):
        return remote(kv.at[ctx], kv.at[ctx], r.ks1.at[d - 1], r.kr.at[ctx], axes.near(d))

    def kv_far(src, e, d):
        return remote(kv.at[src], kv.at[src], r.ks2.at[e, d - 1], r.kr.at[src], axes.far(d))

    def kv_arrive(src):
        remote(kv.at[src], kv.at[src], r.ks1.at[0], r.kr.at[src], axes.sibling).wait_recv()

    def near_wanted(d):
        return reach(lax.rem(first + d, 4)) > ctx

    def far_wanted(src, d):
        return slice_of(first, lax.rem(second + d, 4)) > src

    for d in (2, 1, 3):
        @pl.when(near_wanted(d))
        def _():
            kv_near(d).start()

    for d in (2, 1, 3):
        @pl.when(far_wanted(ctx, d))
        def _():
            kv_far(ctx, 0, d).start()

    for i in range(1, 4):
        @pl.when((lax.rem(ctx, 4) + i < 4) & ((core == 1) | (ctx >= 12)))
        def _():
            kv[ctx + i] = jnp.zeros((128, 384), bf16)

    gather_qo.swap()
    for e in (1, 3, 2):
        src = axes.slice_at(e, 0)

        @pl.when(reach(first) > src)
        def _():
            kv_arrive(src)
            for d in (2, 1, 3):
                @pl.when(far_wanted(src, d))
                def _():
                    kv_far(src, e, d).start()

    gather_qo.side()
    gather_qo.finish()
    QT[...] = jnp.zeros_like(QT)
    qT = [dot(n1, Q[half].reshape(768, 384)).T for half in range(2)]
    for h in range(9):
        c = h // 3
        part = qT[h // 6][64 * (h % 6) : 64 * (h % 6) + 64]
        a, b = rotated(part, cosine, sine)
        lanes = slice(128 * h, 128 * h + 128)
        QT[64 * c : 64 * c + 32, lanes] = (a.astype(bf16).astype(f32) * 0.125).astype(bf16)
        QT[64 * c + 32 : 64 * c + 64, lanes] = (b.astype(bf16).astype(f32) * 0.125).astype(bf16)

    @pl.when(core == 0)
    def _():
        share_dy.start()

    S, eb, tops, top, total, fade, oT = r.S, r.eb, r.tops, r.top, r.total, r.fade, r.oT
    top[...] = jnp.full_like(top, HIDDEN)
    total[...] = jnp.zeros_like(total)
    oT[...] = jnp.zeros_like(oT)
    groups = lax.div(ctx, 4) + 1

    def attend(g, carry):
        for i in range(4):
            j = 4 * g + i

            @pl.when((j < ctx) & (pick(core, g, i) != second))
            def _():
                kv_arrive(j)

        block = kv[pl.ds(4 * g, 4)].reshape(512, 384)
        kvT[g] = block.T
        S[...] = dot(block[:, 0:256], QT[...])
        key = 512 * g + lax.broadcasted_iota(jnp.int32, (512, 128), 0)
        query = 128 * ctx + lax.broadcasted_iota(jnp.int32, (512, 128), 1)
        allowed = (key <= query) & (key >= query - pos)
        for h in range(9):
            lanes = slice(128 * h, 128 * h + 128)
            s = jnp.where(allowed, S[:, lanes], HIDDEN)
            before = top[:, lanes]
            now = jnp.maximum(before, jnp.max(s, axis=0, keepdims=True))
            weights = jnp.exp(s - now)
            damping = jnp.exp(before - now)
            total[:, lanes] = total[:, lanes] * damping + jnp.sum(weights, axis=0, keepdims=True)
            fade[:, lanes] = damping
            top[:, lanes] = now
            tops[g, :, lanes] = now
            eb[g, :, lanes] = weights.astype(bf16)
        oT[...] = oT[...] * fade[...] + dot(kvT[g, 128:384, :], eb[g])
        return carry

    lax.fori_loop(0, groups, attend, 0)
    @pl.when(core == 1)
    def _():
        share_dy.start()

    share = 1.0 / total[...]
    o = r.o
    for h in range(9):
        at_row = VALUE_AT[h // 3]
        lanes = slice(128 * h, 128 * h + 128)
        o[64 * h : 64 * h + 64, :] = oT[at_row : at_row + 64, lanes] * share[:, lanes]
    ob_wide = dot(spread_out[...], o[...].astype(bf16)).astype(bf16)
    ob = ob_wide.T
    mixed = [dot(ob, O[half].reshape(768, 384)).T for half in range(2)]
    hT = r.tokens[...].astype(f32) + jnp.concatenate([mixed[0], mixed[1][0:192]], axis=0)
    r2 = lax.rsqrt(jnp.sum(hT * hT, axis=0, keepdims=True) * (1.0 / 576) + norm_eps)
    hat2 = hT * r2
    gain_cols = dot(spread_in[...], K[0, :, :, 128:256].reshape(768, 128))
    N2[:, lanes_at(first)] = (hat2 * gain_cols[:, 65:66]).astype(bf16)
    share_n2.start()
    r.h[...] = hT
    r.hat2[...] = hat2
    grouped(r.obs, ob_wide)
    r.OB[first] = r.obs[first]
    grouped(r.n1s, n1_wide)
    r.N1[first] = r.n1s[first]
    gather_w.wait()
    share_dy.wait()
    dhid = dot(W[2].reshape(384, 576), DY[...])
    share_n2.wait()

    gate = dot(W[0].reshape(384, 576), N2[...])
    up = dot(W[1].reshape(384, 576), N2[...])
    sig = jax.nn.sigmoid(gate)
    silu = gate * sig
    hid, dgate, dup = r.hid, r.dgate, r.dup
    dgate[...] = (dhid * up * sig * (1.0 + gate * (1.0 - sig))).astype(bf16)
    dup[...] = (dhid * silu).astype(bf16)
    hid[...] = (silu * up).astype(bf16)
    part = lax.dot_general(W[0].reshape(384, 576), dgate[...], TN, preferred_element_type=f32)
    part = part + lax.dot_general(W[1].reshape(384, 576), dup[...], TN, preferred_element_type=f32)
    for p in range(4):
        r.dns[p] = part[:, 128 * p : 128 * p + 128].astype(bf16)
    send_dn.start()
    for m, left, right in ((2, hid, DY), (0, dgate, N2), (1, dup, N2)):
        part = lax.dot_general(left[...], right[...], NT, preferred_element_type=f32).astype(bf16)
        for p in range(4):
            r.fg[m, p] = part[96 * p : 96 * p + 96]
        ff[m].start()
    part = lax.dot_general(W[2].reshape(384, 576), hid[...], TN, preferred_element_type=f32)
    for p in range(4):
        r.outs[p] = part[:, 128 * p : 128 * p + 128].astype(bf16)

    send_dn.wait()
    dn2T = r.dns[first].astype(f32)
    for d in range(1, 4):
        dn2T = dn2T + r.dnr[lax.rem(first + d, 4)].astype(f32)
    hat2 = r.hat2[...]
    shaped = dn2T * gain_cols[:, 65:66]
    mean = jnp.sum(shaped * hat2, axis=0, keepdims=True) * (1.0 / 576)
    dhT = r.cotangent[...].astype(f32) + r2 * (shaped - hat2 * mean)
    r.dhT[...] = dhT
    gain_two = jnp.sum(dn2T * hat2, axis=1, keepdims=True)
    daT = dhT.astype(bf16)
    DA[:, lanes_at(first)] = daT
    dob_wide = dot(O[0].reshape(768, 384), daT[0:384]) + dot(O[1, :, :, 0:192].reshape(768, 192), daT[384:576])
    dobT = dot(spread_in[...], dob_wide.astype(bf16))
    dO, dQ, delta = r.dO, oT, r.delta
    dO[...] = jnp.zeros_like(dO)
    dQ[...] = jnp.zeros_like(dQ)
    for h in range(9):
        at_row = VALUE_AT[h // 3]
        lanes = slice(128 * h, 128 * h + 128)
        part = dobT[64 * h : 64 * h + 64]
        dO[at_row : at_row + 64, lanes] = part.astype(bf16)
        delta[:, lanes] = jnp.sum(part * o[64 * h : 64 * h + 64, :], axis=0, keepdims=True)

    dkv_out, dkv_in, dOg = r.dkv_out, r.dkv_in, r.dOg

    def dkv_far(j, a, b):
        device = {"dp": dp, "ctx": ctx + (b - second) * sb}
        return remote(dkv_out.at[j], dkv_in.at[second, a], r.ds1.at[j], r.dr1.at[second, a], device)

    def attend_back(g, carry):
        factor = jnp.exp(tops[g] - top[...]) / total[...]
        dOg[...] = (dO[...].astype(f32) * factor).astype(bf16)
        block = kv[pl.ds(4 * g, 4)].reshape(512, 384)
        S[...] = dot(block[:, 128:384], dOg[...])
        inner = delta[...] * factor
        dv = lax.dot_general(eb[g], dOg[...], NT, preferred_element_type=f32)
        for h in range(9):
            lanes = slice(128 * h, 128 * h + 128)
            eb[g, :, lanes] = (eb[g, :, lanes].astype(f32) * (S[:, lanes] - inner[:, lanes])).astype(bf16)
        dk = lax.dot_general(eb[g], QT[...], NT, preferred_element_type=f32)
        dQ[...] = dQ[...] + dot(kvT[g, 0:256, :], eb[g])
        out = jnp.concatenate([dk[:, 0:128], dk[:, 128:256] + dv[:, 0:128], dv[:, 128:256]], axis=1)
        dkv_out[pl.ds(4 * g, 4)] = out.astype(bf16).reshape(4, 128, 384)
        for i in range(4):
            j = 4 * g + i
            a, b = pick(core, i, g), pick(core, g, i)

            @pl.when((j < ctx) & (b != second))
            def _():
                dkv_far(j, a, b).start()

        return carry

    lax.fori_loop(0, groups, attend_back, 0)
    cosine, sine = r.cos[...], r.sin[...]
    dqT = r.dqT
    for h in range(9):
        c = h // 3
        lanes = slice(128 * h, 128 * h + 128)
        a, b = rotated(dQ[64 * c : 64 * c + 64, lanes] * 0.125, cosine, -sine)
        dqT[64 * h : 64 * h + 32, :] = a.astype(bf16)
        dqT[64 * h + 32 : 64 * h + 64, :] = b.astype(bf16)
    DQ[:, lanes_at(first)] = dqT[...]
    send_ob.start()
    share_da.start()
    send_n1.start()
    share_dq.start()
    dn1_wide = dot(Q[0].reshape(768, 384), dqT[0:384]) + dot(Q[1, :, :, 0:192].reshape(768, 192), dqT[384:576])
    def gathered_rows(buffer):
        return jnp.concatenate([buffer[p] for p in range(4)], axis=1)

    def gradient(rows, columns):
        return lax.dot_general(rows, columns, NT, preferred_element_type=f32)

    ff[2].second_sum()
    ff[0].second_sum()
    ff[2].pair_sum()
    ff[1].second_sum()
    ff[0].pair_sum()
    ff[1].pair_sum()

    send_ob.wait()
    share_da.wait()
    part = gradient(gathered_rows(r.OB), DA[...]).astype(bf16)
    for p in range(4):
        r.og[p] = part[48 * p : 48 * p + 48]
    sum_o.start()
    send_n1.wait()
    share_dq.wait()
    n1_rows = gathered_rows(r.N1)
    part = gradient(n1_rows, DQ[...]).astype(bf16)
    for p in range(4):
        r.qg[p] = part[48 * p : 48 * p + 48]
    sum_q.start()
    mid, mid_in, own_sum = r.mid, r.mid_in, r.own_sum

    def dkv_near(d):
        return remote(mid.at[d - 1], mid_in.at[d - 1], r.ds2.at[d - 1], r.dr2.at[d - 1], axes.near(d))

    for e in (2, 1, 3, 0):
        a = lax.rem(first + e, 4)
        target = slice_of(a, second)
        own_sum[...] = jnp.zeros_like(own_sum)

        @pl.when(target <= ctx)
        def _():
            own_sum[...] = dkv_out[target].astype(f32)

        for k in range(1, 4):
            b = lax.rem(second + k, 4)

            @pl.when(target < slice_of(first, b))
            def _():
                remote(
                    dkv_in.at[b, a], dkv_in.at[b, a], r.ds1.at[0], r.dr1.at[b, a], axes.sibling
                ).wait_recv()
                own_sum[...] += dkv_in[b, a].astype(f32)

        if e:
            @pl.when(reach(first) > target)
            def _():
                mid[e - 1] = own_sum[...].astype(bf16)
                dkv_near(e).start()

    sum_o.second_sum()
    sum_o.pair_sum()
    sum_q.second_sum()
    for m in (2, 0, 1):
        ff[m].third_sum()
    def send_ff(m, momentum):
        ff[m].finish()
        for half in range(2):
            rows = slice(48 * half, 48 * half + 48)
            m_ff.u[m, rows] = update_of(momentum[rows, :], fin_f[m, half].astype(f32)).astype(bf16)
        m_ff.send(m)

    send_ff(2, r.mom_down)
    send_ff(0, r.mom_gate_up.at[0])
    send_ff(1, r.mom_gate_up.at[1])
    for d in range(1, 4):
        @pl.when(reach(lax.rem(first + 4 - d, 4)) > ctx)
        def _():
            dkv_near(d).wait_recv()
            own_sum[...] += mid_in[d - 1].astype(f32)

    dkvT = own_sum[...].T
    dk = []
    for c in range(3):
        dk += rotated(dkvT[64 * c : 64 * c + 64], cosine, -sine)
    dkT = jnp.concatenate(dk, axis=0).astype(bf16)
    dvT = jnp.concatenate([dkvT[256:384], dkvT[192:256]], axis=0).astype(bf16)
    DKV[0:192, lanes_at(first)] = dkT
    DKV[192:384, lanes_at(first)] = dvT
    share_dkv.start()
    dn1_wide = dn1_wide + dot(K[0, :, :, 0:192].reshape(768, 192), dkT) + dot(
        K[1, :, :, 0:192].reshape(768, 192), dvT
    )
    high, low = two_part(dn1_wide)
    dn1T = dot(spread_in[...], high) + dot(spread_in[...], low)
    hat1 = r.hat1[...]
    gain_one = jnp.sum(dn1T * hat1, axis=1, keepdims=True)
    lane = lax.broadcasted_iota(jnp.int32, (576, 128), 1)
    columns = jnp.where(lane == 64, gain_one, jnp.where(lane == 65, gain_two, 0.0)).astype(bf16)
    grouped(r.gps, dot(spread_out[...], columns).astype(bf16))
    send_gain.start()
    shaped = dn1T * gain_cols[:, 64:65]
    mean = jnp.sum(shaped * hat1, axis=0, keepdims=True) * (1.0 / 576)
    r.ginT[...] = (r.dhT[...] + r1 * (shaped - hat1 * mean)).astype(bf16)

    sum_q.pair_sum()
    pad_kv[0, 0:36, 192:256] = jnp.zeros((36, 64), f32)
    for m in range(2):
        pad_sq[m, 0:36, 0:576] = r.mom_square[:, m, :]
        pad_kv[m, 0:36, 0:192] = r.mom_kv[:, m, :]

    share_dkv.wait()
    part_k = gradient(n1_rows, DKV[0:192, :])
    part_v = gradient(n1_rows, DKV[192:384, :]).astype(bf16)
    send_gain.wait()
    gains_sum = r.gps[first].astype(f32)
    for d in range(1, 4):
        gains_sum = gains_sum + r.gpr[lax.rem(first + d, 4)].astype(f32)
    edge = (jnp.concatenate([part_k[:, 128:192], jnp.zeros((192, 64), f32)], axis=1) + gains_sum).astype(bf16)
    part_k = part_k.astype(bf16)
    kg = r.kg
    for p in range(4):
        rows = slice(48 * p, 48 * p + 48)
        kg[p, :, 0:128] = part_k[rows, 0:128]
        kg[p, :, 128:256] = edge[rows]
        kg[p, :, 256:448] = part_v[rows]
        kg[p, :, 448:512] = jnp.zeros((48, 64), bf16)
    sum_k.start()

    def send_sq(m, reduced):
        reduced.third_sum()
        m_sq.u[m] = update_of(pad_sq[m, :, 0:576], reduced.fin[...].astype(f32)).astype(bf16)
        m_sq.send(m)

    send_sq(1, sum_o)
    send_sq(0, sum_q)
    m_ff.begin()
    sum_k.second_sum()
    sum_k.pair_sum()
    m_ff.go_on(2)
    m_sq.begin()
    sum_k.third_sum()
    fin_k = r.fin_k
    for m in range(2):
        part = fin_k[:, 256 * m : 256 * m + 192].astype(f32)
        m_kv.u[m] = update_of(pad_kv[m, :, 0:192], part).astype(bf16)
        m_kv.send(m)

    send_out.start()
    gsend, gain_sums = r.gsend, r.gain_sums
    gain_grads = fin_k[:, 128:256].astype(f32).T[64:66, 0:36]
    gain_next = momentum_decay * r.mom_gains[...] + gain_grads
    sums = jnp.sum(gain_next * gain_next, axis=1, keepdims=True)
    gsend[0:2, :] = jnp.broadcast_to(sums, (2, 128))
    gsend[2:8, :] = jnp.zeros((6, 128), f32)

    def tell(d, slot):
        return remote(
            gsend, gain_sums.at[slot], r.gs.at[d - 1], r.gv.at[d - 1],
            {"dp": dp, "ctx": lax.rem(ctx + d, 16)},
        )

    for d in range(1, 16):
        tell(d, ctx).start()
    gain_sums[ctx] = gsend[...]

    m_ff.go_on(NS_ITERS - 3)
    m_ff.end()
    m_kv.begin()
    m_kv.go_on(NS_ITERS - 1)
    m_kv.end()
    m_sq.go_on(NS_ITERS - 1)
    m_sq.end()
    send_out.wait()
    total_out = r.h[...] + r.outs[first].astype(f32)
    for d in range(1, 4):
        total_out = total_out + r.outr[lax.rem(first + d, 4)].astype(f32)
    r.outT[...] = total_out.astype(bf16)
    m_kv.collect()
    m_sq.collect()
    m_ff.collect()

    for d in range(1, 16):
        tell(d, lax.rem(ctx + 16 - d, 16)).wait_recv()
        tell(d, ctx).wait_send()
    for d in range(1, 4):
        @pl.when(near_wanted(d))
        def _():
            kv_near(d).wait_send()

        @pl.when(reach(first) > slice_of(lax.rem(first + d, 4), second))
        def _():
            dkv_near(d).wait_send()

        for e in range(4):
            src = axes.slice_at(e, 0)
            came = True if e == 0 else reach(first) > src

            @pl.when(far_wanted(src, d) & came)
            def _():
                kv_far(src, e, d).wait_send()

    def dkv_gone(j, carry):
        y, z = lax.div(j, 4), lax.rem(j, 4)
        a, b = pick(core, z, y), pick(core, y, z)

        @pl.when(b != second)
        def _():
            dkv_far(j, a, b).wait_send()

        return carry

    lax.fori_loop(0, ctx, dkv_gone, 0)
    for each in (
        *ff, sum_o, sum_q, sum_k, gather_k, gather_qo, gather_w, share_n2, share_dy, share_da, share_dq,
        share_dkv, send_n1, send_ob, send_out, send_dn, send_gain,
    ):
        each.drain()


def whole(memory=pltpu.VMEM):
    return pl.BlockSpec(memory_space=memory)


def run_layer(inputs):
    outs = dict(
        outT=((576, 128), bf16),
        ginT=((576, 128), bf16),
        fin_f=((3, 2, 48, 576), bf16),
        fin_q=((48, 576), bf16),
        fin_o=((48, 576), bf16),
        fin_k=((48, 512), bf16),
        o_ff=((3, 96, 576), bf16),
        o_sq=((2, 48, 576), bf16),
        o_kv=((2, 48, 192), bf16),
        gain_sums=((16, 8, 128), f32),
    )
    dma = pltpu.SemaphoreType.DMA
    scratch = dict(
        K=pltpu.VMEM((2, 16, 48, 256), bf16),
        QO=pltpu.VMEM((2, 2, 16, 48, 384), bf16),
        W=pltpu.VMEM((3, 4, 96, 576), bf16),
        pad_sq=pltpu.VMEM((2, 48, 768), f32),
        pad_kv=pltpu.VMEM((2, 48, 256), f32),
        tile=pltpu.VMEM((128, 128), f32),
        E=pltpu.VMEM((576, 768), bf16),
        ET=pltpu.VMEM((768, 576), bf16),
        cos=pltpu.VMEM((32, 128), f32),
        sin=pltpu.VMEM((32, 128), f32),
        kv=pltpu.VMEM((16, 128, 384), bf16),
        kvT=pltpu.VMEM((4, 384, 512), bf16),
        QT=pltpu.VMEM((256, 1152), bf16),
        S=pltpu.VMEM((512, 1152), f32),
        eb=pltpu.VMEM((4, 512, 1152), bf16),
        tops=pltpu.VMEM((4, 1, 1152), f32),
        oT=pltpu.VMEM((256, 1152), f32),
        dO=pltpu.VMEM((256, 1152), bf16),
        dOg=pltpu.VMEM((256, 1152), bf16),
        dkv_out=pltpu.VMEM((16, 128, 384), bf16),
        dkv_in=pltpu.VMEM((4, 4, 128, 384), bf16),
        mid=pltpu.VMEM((3, 128, 384), bf16),
        mid_in=pltpu.VMEM((3, 128, 384), bf16),
        own_sum=pltpu.VMEM((128, 384), f32),
        dqT=pltpu.VMEM((576, 128), bf16),
        DKV=pltpu.VMEM((384, 512), bf16),
        fg=pltpu.VMEM((3, 4, 96, 576), bf16),
        qg=pltpu.VMEM((4, 48, 576), bf16),
        og=pltpu.VMEM((4, 48, 576), bf16),
        kg=pltpu.VMEM((4, 48, 512), bf16),
        gsend=pltpu.VMEM((8, 128), f32),
        nx=pltpu.VMEM((576, 1536), bf16),
        na=pltpu.VMEM((576, 576), bf16),
        np=pltpu.VMEM((576, 576), bf16),
        ka=pltpu.VMEM((192, 192), bf16),
        kp=pltpu.VMEM((192, 192), bf16),
        whole=pltpu.VMEM((16, 96, 576), bf16),
        kv_whole=pltpu.VMEM((16, 48, 192), bf16),
        gs=dma((15,)),
        gv=dma((15,)),
        ks1=dma((3,)),
        ks2=dma((4, 3)),
        kr=dma((16,)),
        ds1=dma((16,)),
        dr1=dma((4, 4)),
        ds2=dma((3,)),
        dr2=dma((3,)),
        gk=Gather.scratch(),
        gqo=SideGather.scratch(),
        gw=SplitGather.scratch(),
        rf=[Reduce.scratch(96, 576, True) for _ in range(3)],
        rq=Reduce.scratch(48, 576, False),
        ro=Reduce.scratch(48, 576, False),
        rk=Reduce.scratch(48, 512, False),
        mf=Muon.scratch(3, 96, 576),
        ms=Muon.scratch(2, 48, 576),
        mk=Muon.scratch(2, 48, 192),
        top=pltpu.VMEM((1, 1152), f32),
        total=pltpu.VMEM((1, 1152), f32),
        fade=pltpu.VMEM((1, 1152), f32),
        delta=pltpu.VMEM((1, 1152), f32),
        hat1=pltpu.VMEM((576, 128), f32),
        hat2=pltpu.VMEM((576, 128), f32),
        h=pltpu.VMEM((576, 128), f32),
        o=pltpu.VMEM((576, 128), f32),
        dhT=pltpu.VMEM((576, 128), f32),
        N2=pltpu.VMEM((576, 512), bf16),
        DY=pltpu.VMEM((576, 512), bf16),
        DA=pltpu.VMEM((576, 512), bf16),
        DQ=pltpu.VMEM((576, 512), bf16),
        hid=pltpu.VMEM((384, 512), bf16),
        dgate=pltpu.VMEM((384, 512), bf16),
        dup=pltpu.VMEM((384, 512), bf16),
        outs=pltpu.VMEM((4, 576, 128), bf16),
        outr=pltpu.VMEM((4, 576, 128), bf16),
        dns=pltpu.VMEM((4, 576, 128), bf16),
        dnr=pltpu.VMEM((4, 576, 128), bf16),
        n1s=pltpu.VMEM((4, 192, 128), bf16),
        N1=pltpu.VMEM((4, 192, 128), bf16),
        obs=pltpu.VMEM((4, 192, 128), bf16),
        OB=pltpu.VMEM((4, 192, 128), bf16),
        gps=pltpu.VMEM((4, 192, 128), bf16),
        gpr=pltpu.VMEM((4, 192, 128), bf16),
        c_n2=Along.scratch(),
        c_dy=Along.scratch(),
        c_da=Along.scratch(),
        c_dq=Along.scratch(),
        c_dkv=Along.scratch(),
        c_n1=Along.scratch(),
        c_ob=Along.scratch(),
        c_out=Along.scratch(),
        c_dn=Along.scratch(),
        c_gain=Along.scratch(),
    )
    names = [*inputs, *outs, *scratch]
    scratch_list = list(scratch.values())

    def kernel(*refs):
        layer_kernel(names, *refs)

    return pl.pallas_call(
        kernel,
        out_shape=tuple(jax.ShapeDtypeStruct(*o) for o in outs.values()),
        in_specs=[whole()] * len(inputs),
        out_specs=[whole()] * len(outs),
        scratch_shapes=scratch_list,
        compiler_params=pltpu.CompilerParams(
            collective_id=3, has_side_effects=True, vmem_limit_bytes=VMEM_LIMIT
        ),
    )(*inputs.values())


VMEM_LIMIT = 63 * 2**20


def finish_kernel(
    outT, ginT, fin_f, fin_q, fin_o, fin_k, o_ff, o_sq, o_kv, gain_sums, w_square, w_kv, w_gate_up, w_down, gains,
    mom_square, mom_kv, mom_gate_up, mom_down, mom_gains,
    out, gin, grad_square, grad_kv, grad_gate_up, grad_down, grad_gains,
    next_square, next_kv, next_gate_up, next_down, next_gains,
    new_square, new_kv, new_gate_up, new_down, new_gains,
):
    shrink = 1.0 - learn_rate * weight_decay
    out[...] = outT[...]
    gin[...] = ginT[...]

    def one(at, grad, width, weight, momentum, ortho, grad_out, next_out, new_out):
        grad_out[at] = grad
        next_out[at] = momentum_decay * momentum[at] + grad
        new_out[at] = shrink * weight[at] - learn_rate * (0.2 * math.sqrt(width)) * ortho

    everything = slice(None)
    for m, fin in enumerate((fin_q, fin_o)):
        one((everything, m, everything), fin[...].astype(f32)[0:36], 576, w_square, mom_square,
            o_sq[m].astype(f32)[0:36], grad_square, next_square, new_square)
    for m in range(2):
        one((everything, m, everything), fin_k[:, 256 * m : 256 * m + 192].astype(f32)[0:36], 576, w_kv, mom_kv,
            o_kv[m].astype(f32)[0:36], grad_kv, next_kv, new_kv)
    for half in range(2):
        rows = slice(48 * half, 48 * half + 48)
        for m in range(2):
            one((m, rows), fin_f[m, half].astype(f32), 1536, w_gate_up, mom_gate_up,
                o_ff[m, rows].astype(f32), grad_gate_up, next_gate_up, new_gate_up)
        one(rows, fin_f[2, half].astype(f32), 1536, w_down, mom_down,
            o_ff[2, rows].astype(f32), grad_down, next_down, new_down)
    gain_grads = fin_k[:, 128:256].astype(f32).T[64:66, 0:36]
    gain_next = momentum_decay * mom_gains[...] + gain_grads
    total = gain_sums[0]
    for k in range(1, 16):
        total = total + gain_sums[k]
    mean = total[0:2, 0:1] * (1.0 / 576)
    grad_gains[...] = gain_grads
    next_gains[...] = gain_next
    new_gains[...] = gains[...] - gain_rate * gain_next / jnp.sqrt(mean + 1e-06)


def finish(packed, weights, momenta):
    shapes = [jax.ShapeDtypeStruct((576, 128), bf16)] * 2
    shapes += [jax.ShapeDtypeStruct(a.shape, f32) for a in weights] * 3
    return pl.pallas_call(
        finish_kernel,
        out_shape=tuple(shapes),
        in_specs=[whole()] * 20,
        out_specs=[whole()] * 17,
        compiler_params=pltpu.CompilerParams(vmem_limit_bytes=VMEM_LIMIT),
    )(*packed, *weights, *momenta)


def swapped(a):
    return jnp.transpose(a, (1, 0, 2))


def shards(
    tokens, positions, cotangent, w_square, w_kv, w_gate_up, w_down, gains,
    mom_square, mom_kv, mom_gate_up, mom_down, mom_gains,
):
    weights = (swapped(w_square), swapped(w_kv), w_gate_up, w_down, gains)
    momenta = (swapped(mom_square), swapped(mom_kv), mom_gate_up, mom_down, mom_gains)
    inputs = dict(
        tokens=tokens[0].T,
        positions=positions,
        cotangent=cotangent[0].T,
        w_square=weights[0],
        w_kv=weights[1],
        w_gate_up=weights[2],
        w_down=weights[3],
        gains=weights[4],
        mom_square=momenta[0],
        mom_kv=momenta[1],
        mom_gate_up=momenta[2],
        mom_down=momenta[3],
        mom_gains=momenta[4],
    )
    outs = list(finish(run_layer(inputs), weights, momenta))
    outs[0] = outs[0].T[None]
    outs[1] = outs[1].T[None]
    for i in (2, 3, 7, 8, 12, 13):
        outs[i] = swapped(outs[i])
    return tuple(outs)


def solution(mesh):
    return jax.shard_map(
        shards,
        mesh=mesh,
        in_specs=(
            P("dp", "ctx", None),
            P("dp", "ctx"),
            P("dp", "ctx", None),
            P(None, "ctx", None),
            P(None, "ctx", None),
            P(None, "ctx", None),
            P("ctx", None),
            P(None, "ctx"),
            P(None, "ctx", None),
            P(None, "ctx", None),
            P(None, "ctx", None),
            P("ctx", None),
            P(None, "ctx"),
        ),
        out_specs=(
            P("dp", "ctx", None),
            P("dp", "ctx", None),
            *(P(None, "ctx", None), P(None, "ctx", None), P(None, "ctx", None), P("ctx", None), P(None, "ctx")) * 3,
        ),
        check_vma=False,
    )
```

```python
import math
import types

import jax
import jax.numpy as jnp
from jax import lax
from jax.experimental import pallas as pl
from jax.experimental.pallas import tpu as pltpu
from jax.sharding import PartitionSpec as P

HEAD_WIDTH = 64
NS_ITERS = 5

norm_eps = 1e-05
rope_base = 100000.0
momentum_decay = 0.95
learn_rate = 0.2
weight_decay = 0.1
gain_rate = 0.25
poly_first = 3.4445
poly_second = -4.775
poly_third = 2.0315

MESH = pl.DeviceIdType.MESH
bf16 = jnp.bfloat16
f32 = jnp.float32
NT = (((1,), (1,)), ((), ()))
TN = (((0,), (0,)), ((), ()))
HIDDEN = -1e30

OWNERS_FF = ((0, 5, 10), (15, 2, 8))
OWNERS_SQ = ((3, 12), (7, 13))
OWNERS_KV = ((6, 9), (4, 1))
PLANES_FF = (1, 2, 0)
PLANES_SQ = (3, 3)
PLANES_KV = (3, 3)


def place():
    dp = lax.axis_index("dp")
    ctx = lax.axis_index("ctx")
    core = lax.rem(dp, 2)
    return dp, ctx, lax.div(dp, 2), core


def pick(core, first, second):
    return first + core * (second - first)


def remote(src, dst, send_sem, recv_sem, device):
    return pltpu.make_async_remote_copy(
        src_ref=src, dst_ref=dst, send_sem=send_sem, recv_sem=recv_sem, device_id=device, device_id_type=MESH
    )


def greet_all(dp, ctx):
    barrier = pltpu.get_barrier_semaphore()
    for d in range(1, 16):
        pl.semaphore_signal(
            barrier, inc=1, device_id={"dp": dp, "ctx": lax.rem(ctx + d, 16)}, device_id_type=MESH
        )
    for d in range(1, 4):
        pl.semaphore_signal(
            barrier, inc=1, device_id={"dp": lax.rem(dp + 2 * d, 8), "ctx": ctx}, device_id_type=MESH
        )
    pl.semaphore_signal(
        barrier, inc=1, device_id={"dp": dp + 1 - 2 * lax.rem(dp, 2), "ctx": ctx}, device_id_type=MESH
    )
    return barrier


def sent(bytes_like, sem, device):
    remote(bytes_like, bytes_like, sem, sem, device).wait_send()


def came(bytes_like, sem, device):
    remote(bytes_like, bytes_like, sem, sem, device).wait_recv()


class Axes:
    def __init__(self):
        self.dp, self.ctx, self.x, self.core = place()
        y, z = lax.div(self.ctx, 4), lax.rem(self.ctx, 4)
        self.first = pick(self.core, z, y)
        self.second = pick(self.core, y, z)
        self.sa = pick(self.core, 1, 4)
        self.sb = pick(self.core, 4, 1)
        self.sibling = {"dp": self.dp + 1 - 2 * self.core, "ctx": self.ctx}

    def near(self, d):
        a = lax.rem(self.first + d, 4)
        return {"dp": self.dp, "ctx": self.ctx + (a - self.first) * self.sa}

    def far(self, d):
        b = lax.rem(self.second + d, 4)
        return {"dp": self.dp, "ctx": self.ctx + (b - self.second) * self.sb}

    def beside(self, before):
        return {"dp": lax.rem(self.dp + pick(before, 2, 6), 8), "ctx": self.ctx}

    def slice_at(self, back_first, back_second):
        a = lax.rem(self.first + 4 - back_first, 4)
        b = lax.rem(self.second + 4 - back_second, 4)
        return a * self.sa + b * self.sb


class Gather:
    @staticmethod
    def scratch():
        dma = pltpu.SemaphoreType.DMA
        return [dma((2,)), dma((3,)), dma((4, 3)), dma((1,))]

    def __init__(self, axes, pack, refs):
        self.axes, self.pack = axes, pack
        self.s, self.v1, self.v2, self.vp = refs

    def move(self, s, ssem, vsem, device):
        part = self.pack.at[self.axes.core, s]
        return remote(part, part, self.s.at[ssem], vsem, device)

    def first_copy(self, d, s):
        return self.move(s, 0, self.v1.at[d - 1], self.axes.near(d))

    def second_copy(self, e, d, s):
        return self.move(s, 0, self.v2.at[e, d - 1], self.axes.far(d))

    def pair_copy(self, s):
        return self.move(s, 1, self.vp.at[0], self.axes.sibling)

    def start(self):
        for d in (2, 1, 3):
            self.first_copy(d, self.axes.ctx).start()

    def forward(self):
        for d in (2, 1, 3):
            self.second_copy(0, d, self.axes.ctx).start()
        for e in (1, 3, 2):
            s = self.axes.slice_at(e, 0)
            self.first_copy(e, s).wait_recv()
            for d in (2, 1, 3):
                self.second_copy(e, d, s).start()
            self.pair_copy(s).start()

    def swap(self):
        for e in (0, 1, 3, 2):
            for d in (1, 3, 2):
                s = self.axes.slice_at(e, d)
                self.second_copy(e, d, s).wait_recv()
                self.pair_copy(s).start()

    def finish(self):
        came(self.pack.at[0, 0:15], self.vp.at[0], self.axes.sibling)

    def drain(self):
        for i in range(2):
            sent(self.pack.at[0, 0:15], self.s.at[i], self.axes.sibling)


class SideGather:
    @staticmethod
    def scratch():
        dma = pltpu.SemaphoreType.DMA
        return [dma((4,)), dma((3,)), dma((4, 3)), dma((4,)), dma((2,))]

    def __init__(self, axes, pack, refs):
        self.axes, self.pack = axes, pack
        self.s, self.v1, self.v2, self.vx, self.vp = refs
        self.fetched = lax.rem(axes.x, 2)
        self.missing = 1 - self.fetched

    def move(self, m, s, ssem, vsem, device):
        part = self.pack.at[m, self.axes.core, s]
        return remote(part, part, self.s.at[ssem], vsem, device)

    def first_copy(self, d, s):
        return self.move(self.fetched, s, 0, self.v1.at[d - 1], self.axes.near(d))

    def second_copy(self, e, d, s):
        return self.move(self.fetched, s, 0, self.v2.at[e, d - 1], self.axes.far(d))

    def side_copy(self, s, d):
        return self.move(self.fetched, s, 1, self.vx.at[d], self.axes.beside(self.axes.core))

    def pair_copy(self, m, s):
        return self.move(m, s, 2 + m, self.vp.at[m], self.axes.sibling)

    def start(self):
        for d in (2, 1, 3):
            self.first_copy(d, self.axes.ctx).start()

    def arrived(self, s, d):
        self.side_copy(s, d).start()
        self.pair_copy(self.fetched, s).start()

    def forward(self):
        for d in (2, 1, 3):
            self.second_copy(0, d, self.axes.ctx).start()
        for e in (1, 3, 2):
            s = self.axes.slice_at(e, 0)
            self.first_copy(e, s).wait_recv()
            for d in (2, 1, 3):
                self.second_copy(e, d, s).start()
            self.arrived(s, 0)

    def swap(self):
        for e in (0, 1, 3, 2):
            for d in (1, 3, 2):
                s = self.axes.slice_at(e, d)
                self.second_copy(e, d, s).wait_recv()
                self.arrived(s, d)

    def side(self):
        for d in (0, 1, 3, 2):
            came(self.pack.at[0, 0, 0 : 4 if d else 3], self.vx.at[d], self.axes.sibling)
            for e in (1, 3, 2, 0):
                if d or e:
                    self.pair_copy(self.missing, self.axes.slice_at(e, d)).start()

    def finish(self):
        for m in range(2):
            came(self.pack.at[0, 0, 0:15], self.vp.at[m], self.axes.sibling)

    def drain(self):
        for i in range(4):
            sent(self.pack.at[0, 0, 0:15], self.s.at[i], self.axes.sibling)


class SplitGather:
    @staticmethod
    def scratch():
        dma = pltpu.SemaphoreType.DMA
        return [dma((2,)), dma((2, 3)), dma((2,)), dma((2,))]

    def __init__(self, axes, whole_ref, refs):
        self.axes, self.whole = axes, whole_ref
        self.s, self.v, self.sx, self.vx = refs
        self.odd = lax.rem(axes.x, 2)

    def region(self, k, odd, p):
        if k == 0:
            return self.whole.at[2 * odd, p]
        return self.whole.at[1, p, pl.ds(pl.multiple_of(48 * odd, 16), 48), :]

    def far_copy(self, k, d, p):
        part = self.region(k, self.odd, p)
        return remote(part, part, self.s.at[k], self.v.at[k, d - 1], self.axes.far(d))

    def side_copy(self, k, d, p, odd):
        part = self.region(k, odd, p)
        side = self.axes.core if k == 0 else 1 - self.axes.core
        return remote(part, part, self.sx.at[k], self.vx.at[k], self.axes.beside(side))

    def place(self, d):
        return lax.rem(self.axes.second + 4 - d, 4)

    def start(self, k):
        for d in (2, 1, 3):
            self.far_copy(k, d, self.axes.second).start()

    def forward(self):
        for k in (1, 0):
            for d in (1, 3, 2):
                p = self.place(d)
                self.far_copy(k, d, p).wait_recv()
                self.side_copy(k, d, p, self.odd).start()

    def three(self, k):
        return self.whole.at[0, 0:3] if k == 0 else self.whole.at[1, 0:3, 0:48]

    def wait(self):
        for k in range(2):
            came(self.three(k), self.vx.at[k], self.axes.sibling)

    def drain(self):
        for k in range(2):
            sent(self.three(k), self.s.at[k], self.axes.sibling)
            sent(self.three(k), self.sx.at[k], self.axes.sibling)


class Along:
    @staticmethod
    def scratch():
        return [pltpu.SemaphoreType.DMA((1,)), pltpu.SemaphoreType.DMA((1,))]

    def __init__(self, axes, axis, src, dst, three, refs):
        self.axes, self.src, self.dst, self.three = axes, src, dst, three
        self.ssem, self.vsem = refs
        self.me = axes.second if axis else axes.first
        self.peer = axes.far if axis else axes.near

    def start(self):
        for d in (2, 1, 3):
            remote(
                self.src(lax.rem(self.me + d, 4)), self.dst(self.me), self.ssem.at[0], self.vsem.at[0], self.peer(d)
            ).start()

    def wait(self):
        came(self.three, self.vsem.at[0], self.axes.sibling)

    def drain(self):
        sent(self.three, self.ssem.at[0], self.axes.sibling)


class Reduce:
    @staticmethod
    def scratch(rows, cols, halves):
        dma = pltpu.SemaphoreType.DMA
        part = (rows // 2, cols) if halves else (rows, cols)
        return [
            pltpu.VMEM((4, rows, cols), bf16),
            pltpu.VMEM((2, *part), bf16),
            pltpu.VMEM(part, bf16),
            pltpu.VMEM((4, *part), bf16),
            Along.scratch(),
            dma((4,)),
            dma((4,)),
        ]

    def __init__(self, axes, g, fin, halves, plane, refs):
        self.axes, self.g, self.fin, self.halves = axes, g, fin, halves
        self.plane, self.here = plane, axes.x == plane
        self.r2, self.h, self.hx, self.x4, along, self.s, self.v = refs
        self.core, self.x = axes.core, axes.x
        self.second = Along(axes, 1, lambda p: g.at[p], lambda p: self.r2.at[p], self.r2.at[0:3], along)

    def pair_copy(self):
        other = 1 - self.core if self.halves else 0
        return remote(self.h.at[other], self.hx, self.s.at[0], self.v.at[0], self.axes.sibling)

    def third_copy(self):
        slot = self.x4.at[self.x]
        device = {"dp": 2 * self.plane + self.core, "ctx": self.axes.ctx}
        return remote(slot, slot, self.s.at[1], self.v.at[1], device)

    def tell_copy(self, d):
        part = self.fin.at[self.core] if self.halves else self.fin
        peer = {"dp": lax.rem(self.axes.dp + 2 * d, 8), "ctx": self.axes.ctx}
        return remote(part, part, self.s.at[3], self.v.at[3], peer)

    def last_copy(self, half):
        return remote(self.fin.at[half], self.fin.at[half], self.s.at[2], self.v.at[2], self.axes.sibling)

    def start(self):
        self.second.start()

    def second_sum(self):
        self.second.wait()
        me = self.axes.second
        total = self.g[me].astype(f32)
        for d in range(1, 4):
            total = total + self.r2[lax.rem(me + d, 4)].astype(f32)
        total = total.astype(bf16)
        rows = total.shape[0] // 2
        if self.halves:
            self.h[0] = total[0:rows]
            self.h[1] = total[rows:]
        else:
            self.h[0] = total
        self.pair_copy().start()

    def pair_sum(self):
        self.pair_copy().wait_recv()
        mine = self.h[self.core if self.halves else 0]
        self.x4[self.x] = (mine.astype(f32) + self.hx[...].astype(f32)).astype(bf16)

        @pl.when(jnp.logical_not(self.here))
        def _():
            self.third_copy().start()

    def third_sum(self):
        came(self.x4.at[0:3], self.v.at[1], self.axes.sibling)
        total = self.x4[0].astype(f32)
        for k in range(1, 4):
            total = total + self.x4[k].astype(f32)
        if self.halves:
            self.fin[self.core] = total.astype(bf16)
            self.last_copy(self.core).start()
        else:
            self.fin[...] = total.astype(bf16)
        for d in (2, 1, 3):
            self.tell_copy(d).start()

    def finish(self):
        if self.halves:
            self.last_copy(1 - self.core).wait_recv()

    def collect(self):
        @pl.when(jnp.logical_not(self.here))
        def _():
            self.tell_copy(1).wait_recv()
            if self.halves:
                self.last_copy(self.core).start()

    def drain(self):
        self.second.drain()
        self.pair_copy().wait_send()

        @pl.when(self.here)
        def _():
            sent(self.x4.at[0:3], self.s.at[3], self.axes.sibling)

        @pl.when(jnp.logical_not(self.here))
        def _():
            self.third_copy().wait_send()
            if self.halves:
                self.last_copy(1 - self.core).wait_recv()

        if self.halves:
            self.last_copy(self.core).wait_send()


def blocks(size):
    return [(b, min(b + 256, size)) for b in range(0, size, 256)]


def mirror(dst, lows):
    size = dst.shape[0]
    for low, (b, e) in zip(lows, blocks(size)):
        dst[b:size, b:e] = low
        if e < size:
            dst[b:e, e:size] = low[e - b :].T


def diagonal(rows, cols):
    shape = (rows, cols)
    return lax.broadcasted_iota(jnp.int32, shape, 0) == lax.broadcasted_iota(jnp.int32, shape, 1)


def newton_schulz_step(x_ref, a_ref, p_ref, first):
    size, total = x_ref.shape
    parts = blocks(size)
    gram = [
        lax.dot_general(x_ref[b:size, :], x_ref[b:e, :], NT, preferred_element_type=f32) for b, e in parts
    ]
    if first:
        squares = 0.0
        for g, (b, e) in zip(gram, parts):
            squares = squares + jnp.sum(jnp.where(diagonal(e - b, e - b), g[0 : e - b], 0.0))
        scale = 1.0 / (jnp.sqrt(squares) + 1e-07)
        gram = [g * (scale * scale) for g in gram]
    mirror(a_ref, [g.astype(bf16) for g in gram])
    poly = []
    for g, (b, e) in zip(gram, parts):
        value = poly_second * g + poly_third * dot(a_ref[b:size, :], a_ref[:, b:e])
        value = value + jnp.where(diagonal(size - b, e - b), poly_first, 0.0)
        poly.append((value * scale if first else value).astype(bf16))
    mirror(p_ref, poly)
    for at in range(0, total, 512):
        end = min(at + 512, total)
        x_ref[:, at:end] = dot(p_ref[...], x_ref[:, at:end]).astype(bf16)


class Muon:
    @staticmethod
    def scratch(count, rows, cols):
        return [
            pltpu.VMEM((count, rows, cols), bf16),
            pltpu.SemaphoreType.DMA((count,)),
            pltpu.SemaphoreType.DMA((1,)),
            pltpu.SemaphoreType.DMA((1,)),
            pltpu.SemaphoreType.DMA((count,)),
            pltpu.SemaphoreType.DMA((1,)),
            pltpu.SemaphoreType.DMA((1,)),
            pltpu.SemaphoreType.DMA((1,)),
        ]

    def __init__(self, owners, planes, out, t, work, halves, refs):
        self.t, self.halves, self.planes = t, halves, planes
        self.u, self.us, self.uv, self.os, self.ov, self.bs, self.ps, self.pv = refs
        _, self.rows, self.cols = self.u.shape
        x, a, p = work
        self.x = x.at[0 : self.cols, 0 : 16 * self.rows]
        self.a, self.p = a, p
        self.out = out
        self.dp, self.ctx, at_x, self.core = place()
        self.sibling = {"dp": self.dp + 1 - 2 * self.core, "ctx": self.ctx}
        self.owners = [pick(self.core, a, b) for a, b in zip(*owners)]
        self.count = len(planes)
        self.here = [at_x == plane for plane in planes]
        self.carries = [halves or self.core == m for m in range(self.count)]
        self.mine = False
        self.which = 0
        for m, owner in enumerate(self.owners):
            mine = self.here[m] & (self.ctx == owner) & self.carries[m]
            self.mine = self.mine | mine
            self.which = self.which + jnp.where(mine, m, 0)

    def up(self, m):
        return remote(
            self.u.at[m], self.t.at[self.ctx], self.us.at[m], self.uv.at[0],
            {"dp": self.dp, "ctx": self.owners[m]},
        )

    def send(self, m):
        @pl.when((self.ctx != self.owners[m]) & self.carries[m])
        def _():
            self.up(m).start()

        @pl.when((self.ctx == self.owners[m]) & self.carries[m])
        def _():
            self.t[self.ctx] = self.u[m]

    def part(self, ref, i, core):
        if self.halves:
            half = self.rows // 2
            return ref.at[i, pl.ds(pl.multiple_of(half * core, 16), half), :]
        return ref.at[i]

    def down(self, peer):
        return remote(
            self.part(self.t, peer, self.core), self.part(self.out, self.which, self.core),
            self.os.at[0], self.ov.at[self.which], {"dp": self.dp, "ctx": peer},
        )

    def pair_copy(self, m, core):
        part = self.part(self.out, m, core)
        return remote(part, part, self.ps.at[0], self.pv.at[0], self.sibling)

    def side_copy(self, m, d):
        part = self.part(self.out, m, self.core)
        peer = {"dp": lax.rem(self.dp + 2 * d, 8), "ctx": self.ctx}
        return remote(part, part, self.bs.at[0], self.ov.at[m], peer)

    def begin(self):
        @pl.when(self.mine)
        def _():
            came(self.t.at[0:15], self.uv.at[0], {"dp": self.dp, "ctx": self.ctx})
            self.x[...] = self.t[...].reshape(16 * self.rows, self.cols).T
            newton_schulz_step(self.x, self.a, self.p, True)

    def go_on(self, steps):
        @pl.when(self.mine)
        def _():
            def step(_, carry):
                newton_schulz_step(self.x, self.a, self.p, False)
                return carry

            lax.fori_loop(0, steps, step, 0)

    def end(self):
        @pl.when(self.mine)
        def _():
            self.t[...] = self.x[...].T.reshape(16, self.rows, self.cols)

            def leave(d, carry):
                self.down(lax.rem(self.ctx + d, 16)).start()
                return carry

            lax.fori_loop(1, 16, leave, 0)
            self.part(self.out, self.which, self.core)[...] = self.part(self.t, self.ctx, self.core)[...]


    def pass_on(self):
        for m, owner in enumerate(self.owners):
            @pl.when(self.here[m] & self.carries[m])
            def _():
                @pl.when(self.ctx != owner)
                def _():
                    self.side_copy(m, 1).wait_recv()

                for d in (2, 1, 3):
                    self.side_copy(m, d).start()
                self.pair_copy(m, self.core).start()

    def collect(self):
        for m in range(self.count):
            @pl.when(jnp.logical_not(self.here[m]) & self.carries[m])
            def _():
                self.side_copy(m, 1).wait_recv()
                self.pair_copy(m, self.core).start()

    def settle(self):
        if self.halves:
            every = self.part(self.out, pl.ds(0, self.count), 0)
        else:
            every = self.out.at[0]
        came(every, self.pv.at[0], self.sibling)
        sent(every, self.ps.at[0], self.sibling)

        @pl.when(self.mine)
        def _():
            sent(self.part(self.t, pl.ds(0, 15), self.core), self.os.at[0], self.sibling)

        for m, owner in enumerate(self.owners):
            @pl.when(self.here[m] & self.carries[m])
            def _():
                @pl.when(self.ctx != owner)
                def _():
                    self.up(m).wait_send()

                for d in (1, 2, 3):
                    self.side_copy(m, d).wait_send()


def update_of(momentum, gradient):
    return gradient + momentum_decay * (momentum_decay * momentum + gradient)


def dot(a, b):
    return jnp.dot(a, b, preferred_element_type=f32)


def rotated(u, cosine, sine):
    first, second = u[0:32], u[32:64]
    return first * cosine - second * sine, second * cosine + first * sine


def two_part(value):
    high = value.astype(bf16)
    return high, (value - high.astype(f32)).astype(bf16)


VALUE_AT = (128, 192, 64)


def layer_kernel(names, *refs):
    r = types.SimpleNamespace(**dict(zip(names, refs)))
    dp, ctx, x, core = place()
    axes = Axes()
    first, second, sa, sb = axes.first, axes.second, axes.sa, axes.sb
    barrier = greet_all(dp, ctx)
    K, QO, W = r.K, r.QO, r.W
    Q, O = QO.at[0], QO.at[1]
    gather_k = Gather(axes, K, r.gk)
    gather_qo = SideGather(axes, QO, r.gqo)
    gather_w = SplitGather(axes, W, r.gw)

    def lanes_at(p):
        return pl.ds(pl.multiple_of(128 * p, 128), 128)

    def spread(buffer, refs):
        return Along(
            axes, 0, lambda p: buffer.at[:, lanes_at(first)], lambda p: buffer.at[:, lanes_at(p)],
            buffer.at[:, 0:384], refs,
        )

    def deliver(source, target, refs):
        return Along(axes, 0, lambda p: source.at[p], lambda p: target.at[p], target.at[0:3], refs)

    N2, DY, DA, DQ, DKV = r.N2, r.DY, r.DA, r.DQ, r.DKV
    share_n2, share_dy = spread(N2, r.c_n2), spread(DY, r.c_dy)
    share_da, share_dq, share_dkv = spread(DA, r.c_da), spread(DQ, r.c_dq), spread(DKV, r.c_dkv)
    send_n1 = deliver(r.n1s, r.N1, r.c_n1)
    send_ob = deliver(r.obs, r.OB, r.c_ob)
    send_out = deliver(r.outs, r.outr, r.c_out)
    send_dn = deliver(r.dns, r.dnr, r.c_dn)
    send_gain = deliver(r.gps, r.gpr, r.c_gain)

    fin_f = r.fin_f
    ff = [Reduce(axes, r.fg.at[m], fin_f.at[m], True, PLANES_FF[m], r.rf[m]) for m in range(3)]
    sum_q = Reduce(axes, r.qg, r.fin_q, False, 3, r.rq)
    sum_o = Reduce(axes, r.og, r.fin_o, False, 3, r.ro)
    sum_k = Reduce(axes, r.kg, r.fin_k, False, 3, r.rk)
    work = (r.nx, r.na, r.np)
    m_ff = Muon(OWNERS_FF, PLANES_FF, r.o_ff, r.whole, work, True, r.mf)
    m_sq = Muon(OWNERS_SQ, PLANES_SQ, r.o_sq, r.whole.at[:, 0:48], work, False, r.ms)
    m_kv = Muon(OWNERS_KV, PLANES_KV, r.o_kv, r.kv_whole, (r.nx, r.ka, r.kp), False, r.mk)

    def grouped(buffer, value):
        for s in range(16):
            a, b = pick(core, s % 4, s // 4), pick(core, s // 4, s % 4)
            buffer[a, pl.ds(pl.multiple_of(48 * b, 16), 48), :] = value[48 * s : 48 * s + 48]

    pad_sq, pad_kv, tile = r.pad_sq, r.pad_kv, r.tile
    pad_sq[...] = jnp.zeros_like(pad_sq)
    pad_kv[...] = jnp.zeros_like(pad_kv)
    tile[...] = jnp.zeros_like(tile)
    tile[64:66, 0:36] = r.gains[...]
    pad_kv[0, 0:36, 128:256] = tile[...].T[0:36, :]
    for m in range(2):
        pad_sq[m, 0:36, 0:576] = r.w_square[:, m, :]
        pad_kv[m, 0:36, 0:192] = r.w_kv[:, m, :]
        K[m, ctx] = pad_kv[m].astype(bf16)
    for half in range(2):
        for m in range(2):
            QO[m, half, ctx] = pad_sq[m, :, 384 * half : 384 * half + 384].astype(bf16)
    W[0, second] = r.w_gate_up[0].astype(bf16)
    W[1, second] = r.w_gate_up[1].astype(bf16)
    W[2, second] = r.w_down[...].astype(bf16)
    pl.semaphore_wait(barrier, 19)
    gather_k.start()
    gather_qo.start()
    gather_w.start(1)
    DY[:, lanes_at(first)] = r.cotangent[...]

    spread_in, spread_out = r.E, r.ET
    row = lax.broadcasted_iota(jnp.int32, (768, 1), 0)
    step = jnp.zeros((768, 1), jnp.int32)
    for t in range(1, 16):
        step = step + (row >= 48 * t).astype(jnp.int32)
    home = jnp.where(row - 48 * step < 36, row - 12 * step, -1)
    col = lax.broadcasted_iota(jnp.int32, (768, 576), 1)
    spread_out[...] = (col == home).astype(f32).astype(bf16)

    xT = r.tokens[...].astype(f32)
    r1 = lax.rsqrt(jnp.sum(xT * xT, axis=0, keepdims=True) * (1.0 / 576) + norm_eps)
    hat1 = xT * r1
    r.hat1[...] = hat1
    high, low = two_part(hat1)
    hat1_wide = dot(spread_out[...], high) + dot(spread_out[...], low)
    gather_k.forward()
    gather_qo.forward()
    gather_w.start(0)
    row = lax.broadcasted_iota(jnp.int32, (576, 1), 0)
    step = jnp.zeros((576, 1), jnp.int32)
    for t in range(1, 16):
        step = step + (row >= 36 * t).astype(jnp.int32)
    col = lax.broadcasted_iota(jnp.int32, (576, 768), 1)
    spread_in[...] = (col == row + 12 * step).astype(f32).astype(bf16)
    pos = r.positions[...]
    row = lax.broadcasted_iota(jnp.int32, (32, 128), 0)
    freqs = jnp.zeros((32, 128), f32)
    for i in range(32):
        freqs = jnp.where(row == i, rope_base ** (-2.0 * i / HEAD_WIDTH), freqs)
    angle = freqs * pos.astype(f32)
    cosine, sine = jnp.cos(angle), jnp.sin(angle)
    r.cos[...] = cosine
    r.sin[...] = sine
    gather_k.swap()
    gather_k.finish()

    n1_wide = (hat1_wide * K[0, :, :, 192:193].reshape(768, 1).astype(f32)).astype(bf16)
    n1 = n1_wide.T
    kT = dot(n1, K[0].reshape(768, 256)).T
    vT = dot(n1, K[1].reshape(768, 256)).T
    kv, kvT, QT = r.kv, r.kvT, r.QT
    own = []
    for c in range(3):
        own += rotated(kT[64 * c : 64 * c + 64], cosine, sine)
    own += [vT[128:192], vT[0:128]]
    kv[ctx] = jnp.concatenate(own, axis=0).T.astype(bf16)

    def slice_of(a, b):
        return a * sa + b * sb

    def reach(a):
        return a * sa + 3 * sb

    def kv_near(d):
        return remote(kv.at[ctx], kv.at[ctx], r.ks.at[0], r.kr.at[ctx], axes.near(d))

    def kv_far(src, e, d):
        return remote(kv.at[src], kv.at[src], r.ks.at[0], r.kr.at[src], axes.far(d))

    def kv_arrive(src):
        remote(kv.at[src], kv.at[src], r.ks.at[0], r.kr.at[src], axes.sibling).wait_recv()

    def near_wanted(d):
        return reach(lax.rem(first + d, 4)) > ctx

    def far_wanted(src, d):
        return slice_of(first, lax.rem(second + d, 4)) > src

    for d in (2, 1, 3):
        @pl.when(near_wanted(d))
        def _():
            kv_near(d).start()

    for d in (2, 1, 3):
        @pl.when(far_wanted(ctx, d))
        def _():
            kv_far(ctx, 0, d).start()

    for i in range(1, 4):
        @pl.when((lax.rem(ctx, 4) + i < 4) & ((core == 1) | (ctx >= 12)))
        def _():
            kv[ctx + i] = jnp.zeros((128, 384), bf16)

    gather_qo.swap()
    for e in (1, 3, 2):
        src = axes.slice_at(e, 0)

        @pl.when(reach(first) > src)
        def _():
            kv_arrive(src)
            for d in (2, 1, 3):
                @pl.when(far_wanted(src, d))
                def _():
                    kv_far(src, e, d).start()

    gather_w.forward()
    gather_qo.side()
    gather_qo.finish()
    QT[...] = jnp.zeros_like(QT)
    qT = [dot(n1, Q[half].reshape(768, 384)).T for half in range(2)]
    for h in range(9):
        c = h // 3
        part = qT[h // 6][64 * (h % 6) : 64 * (h % 6) + 64]
        a, b = rotated(part, cosine, sine)
        lanes = slice(128 * h, 128 * h + 128)
        QT[64 * c : 64 * c + 32, lanes] = (a.astype(bf16).astype(f32) * 0.125).astype(bf16)
        QT[64 * c + 32 : 64 * c + 64, lanes] = (b.astype(bf16).astype(f32) * 0.125).astype(bf16)

    @pl.when(core == 0)
    def _():
        share_dy.start()

    S, eb, tops, top, total, fade, oT = r.S, r.eb, r.tops, r.top, r.total, r.fade, r.oT
    top[...] = jnp.full_like(top, HIDDEN)
    total[...] = jnp.zeros_like(total)
    oT[...] = jnp.zeros_like(oT)
    groups = lax.div(ctx, 4) + 1

    def attend(g, carry):
        for i in range(4):
            j = 4 * g + i

            @pl.when((j < ctx) & (pick(core, g, i) != second))
            def _():
                kv_arrive(j)

        block = kv[pl.ds(4 * g, 4)].reshape(512, 384)
        kvT[g] = block.T
        S[...] = dot(block[:, 0:256], QT[...])
        key = 512 * g + lax.broadcasted_iota(jnp.int32, (512, 128), 0)
        query = 128 * ctx + lax.broadcasted_iota(jnp.int32, (512, 128), 1)
        allowed = (key <= query) & (key >= query - pos)
        for h in range(9):
            lanes = slice(128 * h, 128 * h + 128)
            s = jnp.where(allowed, S[:, lanes], HIDDEN)
            before = top[:, lanes]
            now = jnp.maximum(before, jnp.max(s, axis=0, keepdims=True))
            weights = jnp.exp(s - now)
            damping = jnp.exp(before - now)
            total[:, lanes] = total[:, lanes] * damping + jnp.sum(weights, axis=0, keepdims=True)
            fade[:, lanes] = damping
            top[:, lanes] = now
            tops[g, :, lanes] = now
            eb[g, :, lanes] = weights.astype(bf16)
        oT[...] = oT[...] * fade[...] + dot(kvT[g, 128:384, :], eb[g])
        return carry

    lax.fori_loop(0, groups, attend, 0)
    @pl.when(core == 1)
    def _():
        share_dy.start()

    share = 1.0 / total[...]
    o = r.o
    for h in range(9):
        at_row = VALUE_AT[h // 3]
        lanes = slice(128 * h, 128 * h + 128)
        o[64 * h : 64 * h + 64, :] = oT[at_row : at_row + 64, lanes] * share[:, lanes]
    ob_wide = dot(spread_out[...], o[...].astype(bf16)).astype(bf16)
    ob = ob_wide.T
    mixed = [dot(ob, O[half].reshape(768, 384)).T for half in range(2)]
    hT = r.tokens[...].astype(f32) + jnp.concatenate([mixed[0], mixed[1][0:192]], axis=0)
    r2 = lax.rsqrt(jnp.sum(hT * hT, axis=0, keepdims=True) * (1.0 / 576) + norm_eps)
    hat2 = hT * r2
    gain_cols = dot(spread_in[...], K[0, :, :, 128:256].reshape(768, 128))
    N2[:, lanes_at(first)] = (hat2 * gain_cols[:, 65:66]).astype(bf16)
    share_n2.start()
    r.h[...] = hT
    r.hat2[...] = hat2
    grouped(r.obs, ob_wide)
    r.OB[first] = r.obs[first]
    grouped(r.n1s, n1_wide)
    r.N1[first] = r.n1s[first]
    gather_w.wait()
    share_dy.wait()
    dhid = dot(W[2].reshape(384, 576), DY[...])
    share_n2.wait()

    gate = dot(W[0].reshape(384, 576), N2[...])
    up = dot(W[1].reshape(384, 576), N2[...])
    sig = jax.nn.sigmoid(gate)
    silu = gate * sig
    hid, dgate, dup = r.hid, r.dgate, r.dup
    dgate[...] = (dhid * up * sig * (1.0 + gate * (1.0 - sig))).astype(bf16)
    dup[...] = (dhid * silu).astype(bf16)
    hid[...] = (silu * up).astype(bf16)
    part = lax.dot_general(W[0].reshape(384, 576), dgate[...], TN, preferred_element_type=f32)
    part = part + lax.dot_general(W[1].reshape(384, 576), dup[...], TN, preferred_element_type=f32)
    for p in range(4):
        r.dns[p] = part[:, 128 * p : 128 * p + 128].astype(bf16)
    send_dn.start()
    for m, left, right in ((2, hid, DY), (0, dgate, N2), (1, dup, N2)):
        part = lax.dot_general(left[...], right[...], NT, preferred_element_type=f32).astype(bf16)
        for p in range(4):
            r.fg[m, p] = part[96 * p : 96 * p + 96]
        ff[m].start()
    part = lax.dot_general(W[2].reshape(384, 576), hid[...], TN, preferred_element_type=f32)
    for p in range(4):
        r.outs[p] = part[:, 128 * p : 128 * p + 128].astype(bf16)

    send_dn.wait()
    dn2T = r.dns[first].astype(f32)
    for d in range(1, 4):
        dn2T = dn2T + r.dnr[lax.rem(first + d, 4)].astype(f32)
    hat2 = r.hat2[...]
    shaped = dn2T * gain_cols[:, 65:66]
    mean = jnp.sum(shaped * hat2, axis=0, keepdims=True) * (1.0 / 576)
    dhT = r.cotangent[...].astype(f32) + r2 * (shaped - hat2 * mean)
    r.dhT[...] = dhT
    gain_two = jnp.sum(dn2T * hat2, axis=1, keepdims=True)
    daT = dhT.astype(bf16)
    DA[:, lanes_at(first)] = daT
    send_ob.start()
    share_da.start()
    send_n1.start()
    dob_wide = dot(O[0].reshape(768, 384), daT[0:384]) + dot(O[1, :, :, 0:192].reshape(768, 192), daT[384:576])
    dobT = dot(spread_in[...], dob_wide.astype(bf16))
    dO, dQ, delta = r.dO, oT, r.delta
    dO[...] = jnp.zeros_like(dO)
    dQ[...] = jnp.zeros_like(dQ)
    for h in range(9):
        at_row = VALUE_AT[h // 3]
        lanes = slice(128 * h, 128 * h + 128)
        part = dobT[64 * h : 64 * h + 64]
        dO[at_row : at_row + 64, lanes] = part.astype(bf16)
        delta[:, lanes] = jnp.sum(part * o[64 * h : 64 * h + 64, :], axis=0, keepdims=True)

    dkv_out, dkv_in, dOg = r.dkv_out, r.dkv_in, r.dOg

    def dkv_far(j, a, b):
        device = {"dp": dp, "ctx": ctx + (b - second) * sb}
        return remote(dkv_out.at[j], dkv_in.at[second, a], r.ds1.at[0], r.dr1.at[second, a], device)

    def attend_back(g, carry):
        factor = jnp.exp(tops[g] - top[...]) / total[...]
        dOg[...] = (dO[...].astype(f32) * factor).astype(bf16)
        block = kv[pl.ds(4 * g, 4)].reshape(512, 384)
        S[...] = dot(block[:, 128:384], dOg[...])
        inner = delta[...] * factor
        dv = lax.dot_general(eb[g], dOg[...], NT, preferred_element_type=f32)
        for h in range(9):
            lanes = slice(128 * h, 128 * h + 128)
            eb[g, :, lanes] = (eb[g, :, lanes].astype(f32) * (S[:, lanes] - inner[:, lanes])).astype(bf16)
        dk = lax.dot_general(eb[g], QT[...], NT, preferred_element_type=f32)
        dQ[...] = dQ[...] + dot(kvT[g, 0:256, :], eb[g])
        out = jnp.concatenate([dk[:, 0:128], dk[:, 128:256] + dv[:, 0:128], dv[:, 128:256]], axis=1)
        dkv_out[pl.ds(4 * g, 4)] = out.astype(bf16).reshape(4, 128, 384)
        for i in range(4):
            j = 4 * g + i
            a, b = pick(core, i, g), pick(core, g, i)

            @pl.when((j < ctx) & (b != second))
            def _():
                dkv_far(j, a, b).start()

        return carry

    lax.fori_loop(0, groups, attend_back, 0)
    cosine, sine = r.cos[...], r.sin[...]
    dqT = r.dqT
    for h in range(9):
        c = h // 3
        lanes = slice(128 * h, 128 * h + 128)
        a, b = rotated(dQ[64 * c : 64 * c + 64, lanes] * 0.125, cosine, -sine)
        dqT[64 * h : 64 * h + 32, :] = a.astype(bf16)
        dqT[64 * h + 32 : 64 * h + 64, :] = b.astype(bf16)
    DQ[:, lanes_at(first)] = dqT[...]
    share_dq.start()
    dn1_wide = dot(Q[0].reshape(768, 384), dqT[0:384]) + dot(Q[1, :, :, 0:192].reshape(768, 192), dqT[384:576])
    def gathered_rows(buffer):
        return jnp.concatenate([buffer[p] for p in range(4)], axis=1)

    def gradient(rows, columns):
        return lax.dot_general(rows, columns, NT, preferred_element_type=f32)

    ff[2].second_sum()
    ff[0].second_sum()
    ff[2].pair_sum()
    ff[1].second_sum()
    ff[0].pair_sum()
    ff[1].pair_sum()

    def send_ff(m, momentum):
        @pl.when(ff[m].here)
        def _():
            ff[m].third_sum()
            ff[m].finish()
            for half in range(2):
                rows = slice(48 * half, 48 * half + 48)
                m_ff.u[m, rows] = update_of(momentum[rows, :], fin_f[m, half].astype(f32)).astype(bf16)
            m_ff.send(m)

    send_ff(2, r.mom_down)
    send_ff(0, r.mom_gate_up.at[0])
    send_ff(1, r.mom_gate_up.at[1])
    mid, mid_in, own_sum = r.mid, r.mid_in, r.own_sum

    def dkv_near(d):
        return remote(mid.at[d - 1], mid_in.at[d - 1], r.ds2.at[0], r.dr2.at[d - 1], axes.near(d))

    for e in (2, 1, 3, 0):
        a = lax.rem(first + e, 4)
        target = slice_of(a, second)
        own_sum[...] = jnp.zeros_like(own_sum)

        @pl.when(target <= ctx)
        def _():
            own_sum[...] = dkv_out[target].astype(f32)

        for k in range(1, 4):
            b = lax.rem(second + k, 4)

            @pl.when(target < slice_of(first, b))
            def _():
                remote(
                    dkv_in.at[b, a], dkv_in.at[b, a], r.ds1.at[0], r.dr1.at[b, a], axes.sibling
                ).wait_recv()
                own_sum[...] += dkv_in[b, a].astype(f32)

        if e:
            @pl.when(reach(first) > target)
            def _():
                mid[e - 1] = own_sum[...].astype(bf16)
                dkv_near(e).start()

    send_ob.wait()
    share_da.wait()
    part = gradient(gathered_rows(r.OB), DA[...]).astype(bf16)
    for p in range(4):
        r.og[p] = part[48 * p : 48 * p + 48]
    sum_o.start()
    send_n1.wait()
    share_dq.wait()
    n1_rows = gathered_rows(r.N1)
    part = gradient(n1_rows, DQ[...]).astype(bf16)
    for p in range(4):
        r.qg[p] = part[48 * p : 48 * p + 48]
    sum_q.start()
    for d in range(1, 4):
        @pl.when(reach(lax.rem(first + 4 - d, 4)) > ctx)
        def _():
            dkv_near(d).wait_recv()
            own_sum[...] += mid_in[d - 1].astype(f32)

    dkvT = own_sum[...].T
    dk = []
    for c in range(3):
        dk += rotated(dkvT[64 * c : 64 * c + 64], cosine, -sine)
    dkT = jnp.concatenate(dk, axis=0).astype(bf16)
    dvT = jnp.concatenate([dkvT[256:384], dkvT[192:256]], axis=0).astype(bf16)
    DKV[0:192, lanes_at(first)] = dkT
    DKV[192:384, lanes_at(first)] = dvT
    share_dkv.start()
    dn1_wide = dn1_wide + dot(K[0, :, :, 0:192].reshape(768, 192), dkT) + dot(
        K[1, :, :, 0:192].reshape(768, 192), dvT
    )
    high, low = two_part(dn1_wide)
    dn1T = dot(spread_in[...], high) + dot(spread_in[...], low)
    hat1 = r.hat1[...]
    gain_one = jnp.sum(dn1T * hat1, axis=1, keepdims=True)
    lane = lax.broadcasted_iota(jnp.int32, (576, 128), 1)
    columns = jnp.where(lane == 64, gain_one, jnp.where(lane == 65, gain_two, 0.0)).astype(bf16)
    grouped(r.gps, dot(spread_out[...], columns).astype(bf16))
    send_gain.start()
    shaped = dn1T * gain_cols[:, 64:65]
    mean = jnp.sum(shaped * hat1, axis=0, keepdims=True) * (1.0 / 576)
    r.ginT[...] = (r.dhT[...] + r1 * (shaped - hat1 * mean)).astype(bf16)

    sum_o.second_sum()
    sum_o.pair_sum()
    sum_q.second_sum()
    sum_q.pair_sum()
    pad_kv[0, 0:36, 192:256] = jnp.zeros((36, 64), f32)
    for m in range(2):
        pad_sq[m, 0:36, 0:576] = r.mom_square[:, m, :]
        pad_kv[m, 0:36, 0:192] = r.mom_kv[:, m, :]

    def send_sq(m, reduced):
        @pl.when(reduced.here)
        def _():
            reduced.third_sum()
            m_sq.u[m] = update_of(pad_sq[m, :, 0:576], reduced.fin[...].astype(f32)).astype(bf16)
            m_sq.send(m)

    send_sq(1, sum_o)
    send_sq(0, sum_q)
    share_dkv.wait()
    part_k = gradient(n1_rows, DKV[0:192, :])
    part_v = gradient(n1_rows, DKV[192:384, :]).astype(bf16)
    send_gain.wait()
    gains_sum = r.gps[first].astype(f32)
    for d in range(1, 4):
        gains_sum = gains_sum + r.gpr[lax.rem(first + d, 4)].astype(f32)
    edge = (jnp.concatenate([part_k[:, 128:192], jnp.zeros((192, 64), f32)], axis=1) + gains_sum).astype(bf16)
    part_k = part_k.astype(bf16)
    kg = r.kg
    for p in range(4):
        rows = slice(48 * p, 48 * p + 48)
        kg[p, :, 0:128] = part_k[rows, 0:128]
        kg[p, :, 128:256] = edge[rows]
        kg[p, :, 256:448] = part_v[rows]
        kg[p, :, 448:512] = jnp.zeros((48, 64), bf16)
    sum_k.start()

    m_ff.begin()
    sum_k.second_sum()
    sum_k.pair_sum()
    m_ff.go_on(2)
    fin_k, gsend, gain_sums, gain_total = r.fin_k, r.gsend, r.gain_sums, r.gain_total

    @pl.when(sum_k.here)
    def _():
        sum_k.third_sum()
        for m in range(2):
            part = fin_k[:, 256 * m : 256 * m + 192].astype(f32)
            m_kv.u[m] = update_of(pad_kv[m, :, 0:192], part).astype(bf16)
            m_kv.send(m)

        gain_grads = fin_k[:, 128:256].astype(f32).T[64:66, 0:36]
        gain_next = momentum_decay * r.mom_gains[...] + gain_grads
        sums = jnp.sum(gain_next * gain_next, axis=1, keepdims=True)
        gsend[0:2, :] = jnp.broadcast_to(sums, (2, 128))
        gsend[2:8, :] = jnp.zeros((6, 128), f32)
        gain_sums[ctx] = gsend[...]
        for d in range(1, 16):
            remote(
                gsend, gain_sums.at[ctx], r.gs.at[0], r.gv.at[0], {"dp": dp, "ctx": lax.rem(ctx + d, 16)}
            ).start()

    send_out.start()
    m_sq.begin()
    m_sq.go_on(2)
    m_ff.go_on(NS_ITERS - 3)
    m_ff.end()
    m_kv.begin()
    m_kv.go_on(NS_ITERS - 1)
    m_kv.end()
    m_sq.go_on(NS_ITERS - 3)
    m_sq.end()
    def gains_copy(d):
        peer = {"dp": lax.rem(dp + 2 * d, 8), "ctx": ctx}
        return remote(gain_total, gain_total, r.gs.at[1], r.gv.at[1], peer)

    @pl.when(sum_k.here)
    def _():
        came(gain_sums.at[0:15], r.gv.at[0], axes.sibling)
        total_gains = gain_sums[0]
        for k in range(1, 16):
            total_gains = total_gains + gain_sums[k]
        gain_total[...] = total_gains
        for d in (2, 1, 3):
            gains_copy(d).start()
    send_out.wait()
    total_out = r.h[...] + r.outs[first].astype(f32)
    for d in range(1, 4):
        total_out = total_out + r.outr[lax.rem(first + d, 4)].astype(f32)
    r.outT[...] = total_out.astype(bf16)
    for each in (*ff, sum_o, sum_q, sum_k):
        each.collect()
    m_kv.pass_on()
    m_sq.pass_on()
    m_ff.pass_on()
    m_sq.collect()
    m_kv.collect()
    m_ff.collect()

    @pl.when(sum_k.here)
    def _():
        for d in (2, 1, 3):
            gains_copy(d).wait_send()
        sent(gain_sums.at[0:15], r.gs.at[0], axes.sibling)

    @pl.when(jnp.logical_not(sum_k.here))
    def _():
        gains_copy(1).wait_recv()

    m_kv.settle()
    m_sq.settle()
    m_ff.settle()
    for d in range(1, 4):
        @pl.when(near_wanted(d))
        def _():
            kv_near(d).wait_send()

        @pl.when(reach(first) > slice_of(lax.rem(first + d, 4), second))
        def _():
            dkv_near(d).wait_send()

        for e in range(4):
            src = axes.slice_at(e, 0)
            held = True if e == 0 else reach(first) > src

            @pl.when(far_wanted(src, d) & held)
            def _():
                kv_far(src, e, d).wait_send()

    def dkv_gone(j, carry):
        y, z = lax.div(j, 4), lax.rem(j, 4)
        a, b = pick(core, z, y), pick(core, y, z)

        @pl.when(b != second)
        def _():
            dkv_far(j, a, b).wait_send()

        return carry

    lax.fori_loop(0, ctx, dkv_gone, 0)
    for each in (
        *ff, sum_o, sum_q, sum_k, gather_k, gather_qo, gather_w, share_n2, share_dy, share_da, share_dq,
        share_dkv, send_n1, send_ob, send_out, send_dn, send_gain,
    ):
        each.drain()


def whole(memory=pltpu.VMEM):
    return pl.BlockSpec(memory_space=memory)


def run_layer(inputs):
    outs = dict(
        outT=((576, 128), bf16),
        ginT=((576, 128), bf16),
        fin_f=((3, 2, 48, 576), bf16),
        fin_q=((48, 576), bf16),
        fin_o=((48, 576), bf16),
        fin_k=((48, 512), bf16),
        o_ff=((3, 96, 576), bf16),
        o_sq=((2, 48, 576), bf16),
        o_kv=((2, 48, 192), bf16),
        gain_total=((8, 128), f32),
    )
    dma = pltpu.SemaphoreType.DMA
    scratch = dict(
        K=pltpu.VMEM((2, 16, 48, 256), bf16),
        QO=pltpu.VMEM((2, 2, 16, 48, 384), bf16),
        W=pltpu.VMEM((3, 4, 96, 576), bf16),
        pad_sq=pltpu.VMEM((2, 48, 768), f32),
        pad_kv=pltpu.VMEM((2, 48, 256), f32),
        tile=pltpu.VMEM((128, 128), f32),
        E=pltpu.VMEM((576, 768), bf16),
        ET=pltpu.VMEM((768, 576), bf16),
        cos=pltpu.VMEM((32, 128), f32),
        sin=pltpu.VMEM((32, 128), f32),
        kv=pltpu.VMEM((16, 128, 384), bf16),
        kvT=pltpu.VMEM((4, 384, 512), bf16),
        QT=pltpu.VMEM((256, 1152), bf16),
        S=pltpu.VMEM((512, 1152), f32),
        eb=pltpu.VMEM((4, 512, 1152), bf16),
        tops=pltpu.VMEM((4, 1, 1152), f32),
        oT=pltpu.VMEM((256, 1152), f32),
        dO=pltpu.VMEM((256, 1152), bf16),
        dOg=pltpu.VMEM((256, 1152), bf16),
        dkv_out=pltpu.VMEM((16, 128, 384), bf16),
        dkv_in=pltpu.VMEM((4, 4, 128, 384), bf16),
        mid=pltpu.VMEM((3, 128, 384), bf16),
        mid_in=pltpu.VMEM((3, 128, 384), bf16),
        own_sum=pltpu.VMEM((128, 384), f32),
        dqT=pltpu.VMEM((576, 128), bf16),
        DKV=pltpu.VMEM((384, 512), bf16),
        fg=pltpu.VMEM((3, 4, 96, 576), bf16),
        qg=pltpu.VMEM((4, 48, 576), bf16),
        og=pltpu.VMEM((4, 48, 576), bf16),
        kg=pltpu.VMEM((4, 48, 512), bf16),
        gsend=pltpu.VMEM((8, 128), f32),
        nx=pltpu.VMEM((576, 1536), bf16),
        na=pltpu.VMEM((576, 576), bf16),
        np=pltpu.VMEM((576, 576), bf16),
        ka=pltpu.VMEM((192, 192), bf16),
        kp=pltpu.VMEM((192, 192), bf16),
        whole=pltpu.VMEM((16, 96, 576), bf16),
        kv_whole=pltpu.VMEM((16, 48, 192), bf16),
        gain_sums=pltpu.VMEM((16, 8, 128), f32),
        gs=dma((2,)),
        gv=dma((2,)),
        ks=dma((1,)),
        kr=dma((16,)),
        ds1=dma((1,)),
        dr1=dma((4, 4)),
        ds2=dma((1,)),
        dr2=dma((3,)),
        gk=Gather.scratch(),
        gqo=SideGather.scratch(),
        gw=SplitGather.scratch(),
        rf=[Reduce.scratch(96, 576, True) for _ in range(3)],
        rq=Reduce.scratch(48, 576, False),
        ro=Reduce.scratch(48, 576, False),
        rk=Reduce.scratch(48, 512, False),
        mf=Muon.scratch(3, 96, 576),
        ms=Muon.scratch(2, 48, 576),
        mk=Muon.scratch(2, 48, 192),
        top=pltpu.VMEM((1, 1152), f32),
        total=pltpu.VMEM((1, 1152), f32),
        fade=pltpu.VMEM((1, 1152), f32),
        delta=pltpu.VMEM((1, 1152), f32),
        hat1=pltpu.VMEM((576, 128), f32),
        hat2=pltpu.VMEM((576, 128), f32),
        h=pltpu.VMEM((576, 128), f32),
        o=pltpu.VMEM((576, 128), f32),
        dhT=pltpu.VMEM((576, 128), f32),
        N2=pltpu.VMEM((576, 512), bf16),
        DY=pltpu.VMEM((576, 512), bf16),
        DA=pltpu.VMEM((576, 512), bf16),
        DQ=pltpu.VMEM((576, 512), bf16),
        hid=pltpu.VMEM((384, 512), bf16),
        dgate=pltpu.VMEM((384, 512), bf16),
        dup=pltpu.VMEM((384, 512), bf16),
        outs=pltpu.VMEM((4, 576, 128), bf16),
        outr=pltpu.VMEM((4, 576, 128), bf16),
        dns=pltpu.VMEM((4, 576, 128), bf16),
        dnr=pltpu.VMEM((4, 576, 128), bf16),
        n1s=pltpu.VMEM((4, 192, 128), bf16),
        N1=pltpu.VMEM((4, 192, 128), bf16),
        obs=pltpu.VMEM((4, 192, 128), bf16),
        OB=pltpu.VMEM((4, 192, 128), bf16),
        gps=pltpu.VMEM((4, 192, 128), bf16),
        gpr=pltpu.VMEM((4, 192, 128), bf16),
        c_n2=Along.scratch(),
        c_dy=Along.scratch(),
        c_da=Along.scratch(),
        c_dq=Along.scratch(),
        c_dkv=Along.scratch(),
        c_n1=Along.scratch(),
        c_ob=Along.scratch(),
        c_out=Along.scratch(),
        c_dn=Along.scratch(),
        c_gain=Along.scratch(),
    )
    names = [*inputs, *outs, *scratch]
    scratch_list = list(scratch.values())

    def kernel(*refs):
        layer_kernel(names, *refs)

    return pl.pallas_call(
        kernel,
        out_shape=tuple(jax.ShapeDtypeStruct(*o) for o in outs.values()),
        in_specs=[whole()] * len(inputs),
        out_specs=[whole()] * len(outs),
        scratch_shapes=scratch_list,
        compiler_params=pltpu.CompilerParams(
            collective_id=3, has_side_effects=True, vmem_limit_bytes=VMEM_LIMIT
        ),
    )(*inputs.values())


VMEM_LIMIT = 63 * 2**20


def finish_kernel(
    outT, ginT, fin_f, fin_q, fin_o, fin_k, o_ff, o_sq, o_kv, gain_total, w_square, w_kv, w_gate_up, w_down, gains,
    mom_square, mom_kv, mom_gate_up, mom_down, mom_gains,
    out, gin, grad_square, grad_kv, grad_gate_up, grad_down, grad_gains,
    next_square, next_kv, next_gate_up, next_down, next_gains,
    new_square, new_kv, new_gate_up, new_down, new_gains,
):
    shrink = 1.0 - learn_rate * weight_decay
    out[...] = outT[...]
    gin[...] = ginT[...]

    def one(at, grad, width, weight, momentum, ortho, grad_out, next_out, new_out):
        grad_out[at] = grad
        next_out[at] = momentum_decay * momentum[at] + grad
        new_out[at] = shrink * weight[at] - learn_rate * (0.2 * math.sqrt(width)) * ortho

    everything = slice(None)
    for m, fin in enumerate((fin_q, fin_o)):
        one((everything, m, everything), fin[...].astype(f32)[0:36], 576, w_square, mom_square,
            o_sq[m].astype(f32)[0:36], grad_square, next_square, new_square)
    for m in range(2):
        one((everything, m, everything), fin_k[:, 256 * m : 256 * m + 192].astype(f32)[0:36], 576, w_kv, mom_kv,
            o_kv[m].astype(f32)[0:36], grad_kv, next_kv, new_kv)
    for half in range(2):
        rows = slice(48 * half, 48 * half + 48)
        for m in range(2):
            one((m, rows), fin_f[m, half].astype(f32), 1536, w_gate_up, mom_gate_up,
                o_ff[m, rows].astype(f32), grad_gate_up, next_gate_up, new_gate_up)
        one(rows, fin_f[2, half].astype(f32), 1536, w_down, mom_down,
            o_ff[2, rows].astype(f32), grad_down, next_down, new_down)
    gain_grads = fin_k[:, 128:256].astype(f32).T[64:66, 0:36]
    gain_next = momentum_decay * mom_gains[...] + gain_grads
    mean = gain_total[0:2, 0:1] * (1.0 / 576)
    grad_gains[...] = gain_grads
    next_gains[...] = gain_next
    new_gains[...] = gains[...] - gain_rate * gain_next / jnp.sqrt(mean + 1e-06)


def finish(packed, weights, momenta):
    shapes = [jax.ShapeDtypeStruct((576, 128), bf16)] * 2
    shapes += [jax.ShapeDtypeStruct(a.shape, f32) for a in weights] * 3
    return pl.pallas_call(
        finish_kernel,
        out_shape=tuple(shapes),
        in_specs=[whole()] * 20,
        out_specs=[whole()] * 17,
        compiler_params=pltpu.CompilerParams(vmem_limit_bytes=VMEM_LIMIT),
    )(*packed, *weights, *momenta)


def swapped(a):
    return jnp.transpose(a, (1, 0, 2))


def shards(
    tokens, positions, cotangent, w_square, w_kv, w_gate_up, w_down, gains,
    mom_square, mom_kv, mom_gate_up, mom_down, mom_gains,
):
    weights = (swapped(w_square), swapped(w_kv), w_gate_up, w_down, gains)
    momenta = (swapped(mom_square), swapped(mom_kv), mom_gate_up, mom_down, mom_gains)
    inputs = dict(
        tokens=tokens[0].T,
        positions=positions,
        cotangent=cotangent[0].T,
        w_square=weights[0],
        w_kv=weights[1],
        w_gate_up=weights[2],
        w_down=weights[3],
        gains=weights[4],
        mom_square=momenta[0],
        mom_kv=momenta[1],
        mom_gate_up=momenta[2],
        mom_down=momenta[3],
        mom_gains=momenta[4],
    )
    outs = list(finish(run_layer(inputs), weights, momenta))
    outs[0] = outs[0].T[None]
    outs[1] = outs[1].T[None]
    for i in (2, 3, 7, 8, 12, 13):
        outs[i] = swapped(outs[i])
    return tuple(outs)


def solution(mesh):
    return jax.shard_map(
        shards,
        mesh=mesh,
        in_specs=(
            P("dp", "ctx", None),
            P("dp", "ctx"),
            P("dp", "ctx", None),
            P(None, "ctx", None),
            P(None, "ctx", None),
            P(None, "ctx", None),
            P("ctx", None),
            P(None, "ctx"),
            P(None, "ctx", None),
            P(None, "ctx", None),
            P(None, "ctx", None),
            P("ctx", None),
            P(None, "ctx"),
        ),
        out_specs=(
            P("dp", "ctx", None),
            P("dp", "ctx", None),
            *(P(None, "ctx", None), P(None, "ctx", None), P(None, "ctx", None), P("ctx", None), P(None, "ctx")) * 3,
        ),
        check_vma=False,
    )
```

```python
import math
import types

import jax
import jax.numpy as jnp
from jax import lax
from jax.experimental import pallas as pl
from jax.experimental.pallas import tpu as pltpu
from jax.sharding import PartitionSpec as P

HEAD_WIDTH = 64
NS_ITERS = 5

norm_eps = 1e-05
rope_base = 100000.0
momentum_decay = 0.95
learn_rate = 0.2
weight_decay = 0.1
gain_rate = 0.25
poly_first = 3.4445
poly_second = -4.775
poly_third = 2.0315

MESH = pl.DeviceIdType.MESH
bf16 = jnp.bfloat16
f32 = jnp.float32
NT = (((1,), (1,)), ((), ()))
TN = (((0,), (0,)), ((), ()))
HIDDEN = -1e30

OWNERS_FF = ((0, 5, 10), (15, 2, 8))
OWNERS_SQ = ((3, 12), (7, 13))
OWNERS_KV = ((6, 9), (4, 1))
PLANES_FF = (1, 2, 0)
PLANES_SQ = (None, None)
PLANES_KV = (None, None)


def place():
    dp = lax.axis_index("dp")
    ctx = lax.axis_index("ctx")
    core = lax.rem(dp, 2)
    return dp, ctx, lax.div(dp, 2), core


def pick(core, first, second):
    return first + core * (second - first)


def remote(src, dst, send_sem, recv_sem, device):
    return pltpu.make_async_remote_copy(
        src_ref=src, dst_ref=dst, send_sem=send_sem, recv_sem=recv_sem, device_id=device, device_id_type=MESH
    )


def greet_all(dp, ctx):
    barrier = pltpu.get_barrier_semaphore()
    for d in range(1, 16):
        pl.semaphore_signal(
            barrier, inc=1, device_id={"dp": dp, "ctx": lax.rem(ctx + d, 16)}, device_id_type=MESH
        )
    for d in range(1, 4):
        pl.semaphore_signal(
            barrier, inc=1, device_id={"dp": lax.rem(dp + 2 * d, 8), "ctx": ctx}, device_id_type=MESH
        )
    pl.semaphore_signal(
        barrier, inc=1, device_id={"dp": dp + 1 - 2 * lax.rem(dp, 2), "ctx": ctx}, device_id_type=MESH
    )
    return barrier


def sent(bytes_like, sem, device):
    remote(bytes_like, bytes_like, sem, sem, device).wait_send()


def came(bytes_like, sem, device):
    remote(bytes_like, bytes_like, sem, sem, device).wait_recv()


class Axes:
    def __init__(self):
        self.dp, self.ctx, self.x, self.core = place()
        y, z = lax.div(self.ctx, 4), lax.rem(self.ctx, 4)
        self.first = pick(self.core, z, y)
        self.second = pick(self.core, y, z)
        self.sa = pick(self.core, 1, 4)
        self.sb = pick(self.core, 4, 1)
        self.sibling = {"dp": self.dp + 1 - 2 * self.core, "ctx": self.ctx}

    def near(self, d):
        a = lax.rem(self.first + d, 4)
        return {"dp": self.dp, "ctx": self.ctx + (a - self.first) * self.sa}

    def far(self, d):
        b = lax.rem(self.second + d, 4)
        return {"dp": self.dp, "ctx": self.ctx + (b - self.second) * self.sb}

    def beside(self, before):
        return {"dp": lax.rem(self.dp + pick(before, 2, 6), 8), "ctx": self.ctx}

    def slice_at(self, back_first, back_second):
        a = lax.rem(self.first + 4 - back_first, 4)
        b = lax.rem(self.second + 4 - back_second, 4)
        return a * self.sa + b * self.sb


class Gather:
    @staticmethod
    def scratch():
        dma = pltpu.SemaphoreType.DMA
        return [dma((2,)), dma((3,)), dma((4, 3)), dma((1,))]

    def __init__(self, axes, pack, refs):
        self.axes, self.pack = axes, pack
        self.s, self.v1, self.v2, self.vp = refs

    def move(self, s, ssem, vsem, device):
        part = self.pack.at[self.axes.core, s]
        return remote(part, part, self.s.at[ssem], vsem, device)

    def first_copy(self, d, s):
        return self.move(s, 0, self.v1.at[d - 1], self.axes.near(d))

    def second_copy(self, e, d, s):
        return self.move(s, 0, self.v2.at[e, d - 1], self.axes.far(d))

    def pair_copy(self, s):
        return self.move(s, 1, self.vp.at[0], self.axes.sibling)

    def start(self):
        for d in (2, 1, 3):
            self.first_copy(d, self.axes.ctx).start()

    def forward(self):
        for d in (2, 1, 3):
            self.second_copy(0, d, self.axes.ctx).start()
        for e in (1, 3, 2):
            s = self.axes.slice_at(e, 0)
            self.first_copy(e, s).wait_recv()
            for d in (2, 1, 3):
                self.second_copy(e, d, s).start()
            self.pair_copy(s).start()

    def swap(self):
        for e in (0, 1, 3, 2):
            for d in (1, 3, 2):
                s = self.axes.slice_at(e, d)
                self.second_copy(e, d, s).wait_recv()
                self.pair_copy(s).start()

    def finish(self):
        came(self.pack.at[0, 0:15], self.vp.at[0], self.axes.sibling)

    def drain(self):
        for i in range(2):
            sent(self.pack.at[0, 0:15], self.s.at[i], self.axes.sibling)


class SideGather:
    @staticmethod
    def scratch():
        dma = pltpu.SemaphoreType.DMA
        return [dma((4,)), dma((3,)), dma((4, 3)), dma((4,)), dma((2,))]

    def __init__(self, axes, pack, refs):
        self.axes, self.pack = axes, pack
        self.s, self.v1, self.v2, self.vx, self.vp = refs
        self.fetched = lax.rem(axes.x, 2)
        self.missing = 1 - self.fetched

    def move(self, m, s, ssem, vsem, device):
        part = self.pack.at[m, self.axes.core, s]
        return remote(part, part, self.s.at[ssem], vsem, device)

    def first_copy(self, d, s):
        return self.move(self.fetched, s, 0, self.v1.at[d - 1], self.axes.near(d))

    def second_copy(self, e, d, s):
        return self.move(self.fetched, s, 0, self.v2.at[e, d - 1], self.axes.far(d))

    def side_copy(self, s, d):
        return self.move(self.fetched, s, 1, self.vx.at[d], self.axes.beside(self.axes.core))

    def pair_copy(self, m, s):
        return self.move(m, s, 2 + m, self.vp.at[m], self.axes.sibling)

    def start(self):
        for d in (2, 1, 3):
            self.first_copy(d, self.axes.ctx).start()

    def arrived(self, s, d):
        self.side_copy(s, d).start()
        self.pair_copy(self.fetched, s).start()

    def forward(self):
        for d in (2, 1, 3):
            self.second_copy(0, d, self.axes.ctx).start()
        for e in (1, 3, 2):
            s = self.axes.slice_at(e, 0)
            self.first_copy(e, s).wait_recv()
            for d in (2, 1, 3):
                self.second_copy(e, d, s).start()
            self.arrived(s, 0)

    def swap(self):
        for e in (0, 1, 3, 2):
            for d in (1, 3, 2):
                s = self.axes.slice_at(e, d)
                self.second_copy(e, d, s).wait_recv()
                self.arrived(s, d)

    def side(self):
        for d in (0, 1, 3, 2):
            came(self.pack.at[0, 0, 0 : 4 if d else 3], self.vx.at[d], self.axes.sibling)
            for e in (1, 3, 2, 0):
                if d or e:
                    self.pair_copy(self.missing, self.axes.slice_at(e, d)).start()

    def finish(self):
        for m in range(2):
            came(self.pack.at[0, 0, 0:15], self.vp.at[m], self.axes.sibling)

    def drain(self):
        for i in range(4):
            sent(self.pack.at[0, 0, 0:15], self.s.at[i], self.axes.sibling)


class SplitGather:
    @staticmethod
    def scratch():
        dma = pltpu.SemaphoreType.DMA
        return [dma((2,)), dma((2, 3)), dma((2,)), dma((2,))]

    def __init__(self, axes, whole_ref, refs):
        self.axes, self.whole = axes, whole_ref
        self.s, self.v, self.sx, self.vx = refs
        self.odd = lax.rem(axes.x, 2)

    def region(self, k, odd, p):
        if k == 0:
            return self.whole.at[2 * odd, p]
        return self.whole.at[1, p, pl.ds(pl.multiple_of(48 * odd, 16), 48), :]

    def far_copy(self, k, d, p):
        part = self.region(k, self.odd, p)
        return remote(part, part, self.s.at[k], self.v.at[k, d - 1], self.axes.far(d))

    def side_copy(self, k, d, p, odd):
        part = self.region(k, odd, p)
        side = self.axes.core if k == 0 else 1 - self.axes.core
        return remote(part, part, self.sx.at[k], self.vx.at[k], self.axes.beside(side))

    def place(self, d):
        return lax.rem(self.axes.second + 4 - d, 4)

    def start(self, k):
        for d in (2, 1, 3):
            self.far_copy(k, d, self.axes.second).start()

    def forward(self):
        for k in (1, 0):
            for d in (1, 3, 2):
                p = self.place(d)
                self.far_copy(k, d, p).wait_recv()
                self.side_copy(k, d, p, self.odd).start()

    def three(self, k):
        return self.whole.at[0, 0:3] if k == 0 else self.whole.at[1, 0:3, 0:48]

    def wait(self):
        for k in range(2):
            came(self.three(k), self.vx.at[k], self.axes.sibling)

    def drain(self):
        for k in range(2):
            sent(self.three(k), self.s.at[k], self.axes.sibling)
            sent(self.three(k), self.sx.at[k], self.axes.sibling)


class Along:
    @staticmethod
    def scratch():
        return [pltpu.SemaphoreType.DMA((1,)), pltpu.SemaphoreType.DMA((1,))]

    def __init__(self, axes, axis, src, dst, three, refs):
        self.axes, self.src, self.dst, self.three = axes, src, dst, three
        self.ssem, self.vsem = refs
        self.me = axes.second if axis else axes.first
        self.peer = axes.far if axis else axes.near

    def start(self):
        for d in (2, 1, 3):
            remote(
                self.src(lax.rem(self.me + d, 4)), self.dst(self.me), self.ssem.at[0], self.vsem.at[0], self.peer(d)
            ).start()

    def wait(self):
        came(self.three, self.vsem.at[0], self.axes.sibling)

    def drain(self):
        sent(self.three, self.ssem.at[0], self.axes.sibling)


class Reduce:
    @staticmethod
    def scratch(rows, cols, halves):
        dma = pltpu.SemaphoreType.DMA
        part = (rows // 2, cols) if halves else (rows, cols)
        return [
            pltpu.VMEM((4, rows, cols), bf16),
            pltpu.VMEM((2, *part), bf16),
            pltpu.VMEM(part, bf16),
            pltpu.VMEM((4, *part), bf16),
            Along.scratch(),
            dma((4,)),
            dma((4,)),
        ]

    def __init__(self, axes, g, fin, halves, plane, refs):
        self.axes, self.g, self.fin, self.halves = axes, g, fin, halves
        self.plane, self.here = plane, True if plane is None else axes.x == plane
        self.r2, self.h, self.hx, self.x4, along, self.s, self.v = refs
        self.core, self.x = axes.core, axes.x
        self.second = Along(axes, 1, lambda p: g.at[p], lambda p: self.r2.at[p], self.r2.at[0:3], along)

    def pair_copy(self):
        other = 1 - self.core if self.halves else 0
        return remote(self.h.at[other], self.hx, self.s.at[0], self.v.at[0], self.axes.sibling)

    def third_copy(self, d=0):
        slot = self.x4.at[self.x]
        to = lax.rem(self.axes.dp + 2 * d, 8) if self.plane is None else 2 * self.plane + self.core
        return remote(slot, slot, self.s.at[1], self.v.at[1], {"dp": to, "ctx": self.axes.ctx})

    def tell_copy(self, d):
        part = self.fin.at[self.core] if self.halves else self.fin
        peer = {"dp": lax.rem(self.axes.dp + 2 * d, 8), "ctx": self.axes.ctx}
        return remote(part, part, self.s.at[3], self.v.at[3], peer)

    def last_copy(self, half):
        return remote(self.fin.at[half], self.fin.at[half], self.s.at[2], self.v.at[2], self.axes.sibling)

    def start(self):
        self.second.start()

    def second_sum(self):
        self.second.wait()
        me = self.axes.second
        total = self.g[me].astype(f32)
        for d in range(1, 4):
            total = total + self.r2[lax.rem(me + d, 4)].astype(f32)
        total = total.astype(bf16)
        rows = total.shape[0] // 2
        if self.halves:
            self.h[0] = total[0:rows]
            self.h[1] = total[rows:]
        else:
            self.h[0] = total
        self.pair_copy().start()

    def pair_sum(self):
        self.pair_copy().wait_recv()
        mine = self.h[self.core if self.halves else 0]
        self.x4[self.x] = (mine.astype(f32) + self.hx[...].astype(f32)).astype(bf16)

        if self.plane is None:
            for d in (2, 1, 3):
                self.third_copy(d).start()
        else:
            @pl.when(jnp.logical_not(self.here))
            def _():
                self.third_copy().start()

    def third_sum(self):
        came(self.x4.at[0:3], self.v.at[1], self.axes.sibling)
        total = self.x4[0].astype(f32)
        for k in range(1, 4):
            total = total + self.x4[k].astype(f32)
        if self.halves:
            self.fin[self.core] = total.astype(bf16)
            self.last_copy(self.core).start()
        else:
            self.fin[...] = total.astype(bf16)
        if self.plane is not None:
            for d in (2, 1, 3):
                self.tell_copy(d).start()

    def finish(self):
        if self.halves:
            self.last_copy(1 - self.core).wait_recv()

    def collect(self):
        if self.plane is None:
            return

        @pl.when(jnp.logical_not(self.here))
        def _():
            self.tell_copy(1).wait_recv()
            if self.halves:
                self.last_copy(self.core).start()

    def drain(self):
        self.second.drain()
        self.pair_copy().wait_send()
        if self.plane is None:
            sent(self.x4.at[0:3], self.s.at[1], self.axes.sibling)
            return

        @pl.when(self.here)
        def _():
            sent(self.x4.at[0:3], self.s.at[3], self.axes.sibling)

        @pl.when(jnp.logical_not(self.here))
        def _():
            self.third_copy().wait_send()
            if self.halves:
                self.last_copy(1 - self.core).wait_recv()

        if self.halves:
            self.last_copy(self.core).wait_send()


def blocks(size):
    return [(b, min(b + 256, size)) for b in range(0, size, 256)]


def mirror(dst, lows):
    size = dst.shape[0]
    for low, (b, e) in zip(lows, blocks(size)):
        dst[b:size, b:e] = low
        if e < size:
            dst[b:e, e:size] = low[e - b :].T


def diagonal(rows, cols):
    shape = (rows, cols)
    return lax.broadcasted_iota(jnp.int32, shape, 0) == lax.broadcasted_iota(jnp.int32, shape, 1)


def newton_schulz_step(x_ref, a_ref, p_ref, first):
    size, total = x_ref.shape
    parts = blocks(size)
    gram = [
        lax.dot_general(x_ref[b:size, :], x_ref[b:e, :], NT, preferred_element_type=f32) for b, e in parts
    ]
    if first:
        squares = 0.0
        for g, (b, e) in zip(gram, parts):
            squares = squares + jnp.sum(jnp.where(diagonal(e - b, e - b), g[0 : e - b], 0.0))
        scale = 1.0 / (jnp.sqrt(squares) + 1e-07)
        gram = [g * (scale * scale) for g in gram]
    mirror(a_ref, [g.astype(bf16) for g in gram])
    poly = []
    for g, (b, e) in zip(gram, parts):
        value = poly_second * g + poly_third * dot(a_ref[b:size, :], a_ref[:, b:e])
        value = value + jnp.where(diagonal(size - b, e - b), poly_first, 0.0)
        poly.append((value * scale if first else value).astype(bf16))
    mirror(p_ref, poly)
    for at in range(0, total, 512):
        end = min(at + 512, total)
        x_ref[:, at:end] = dot(p_ref[...], x_ref[:, at:end]).astype(bf16)


class Muon:
    @staticmethod
    def scratch(count, rows, cols):
        return [
            pltpu.VMEM((count, rows, cols), bf16),
            pltpu.SemaphoreType.DMA((count,)),
            pltpu.SemaphoreType.DMA((1,)),
            pltpu.SemaphoreType.DMA((1,)),
            pltpu.SemaphoreType.DMA((count,)),
            pltpu.SemaphoreType.DMA((1,)),
            pltpu.SemaphoreType.DMA((1,)),
            pltpu.SemaphoreType.DMA((1,)),
        ]

    def __init__(self, owners, planes, out, t, work, halves, refs):
        self.t, self.halves, self.planes = t, halves, planes
        self.u, self.us, self.uv, self.os, self.ov, self.bs, self.ps, self.pv = refs
        _, self.rows, self.cols = self.u.shape
        x, a, p = work
        self.x = x.at[0 : self.cols, 0 : 16 * self.rows]
        self.a, self.p = a, p
        self.out = out
        self.dp, self.ctx, at_x, self.core = place()
        self.sibling = {"dp": self.dp + 1 - 2 * self.core, "ctx": self.ctx}
        self.owners = [pick(self.core, a, b) for a, b in zip(*owners)]
        self.count = len(planes)
        self.everywhere = planes[0] is None
        self.here = [True if plane is None else at_x == plane for plane in planes]
        self.carries = [halves or self.core == m for m in range(self.count)]
        self.mine = False
        self.which = 0
        for m, owner in enumerate(self.owners):
            mine = self.here[m] & (self.ctx == owner) & self.carries[m]
            self.mine = self.mine | mine
            self.which = self.which + jnp.where(mine, m, 0)

    def up(self, m):
        return remote(
            self.u.at[m], self.t.at[self.ctx], self.us.at[m], self.uv.at[0],
            {"dp": self.dp, "ctx": self.owners[m]},
        )

    def send(self, m):
        @pl.when((self.ctx != self.owners[m]) & self.carries[m])
        def _():
            self.up(m).start()

        @pl.when((self.ctx == self.owners[m]) & self.carries[m])
        def _():
            self.t[self.ctx] = self.u[m]

    def part(self, ref, i, core):
        if self.halves:
            half = self.rows // 2
            return ref.at[i, pl.ds(pl.multiple_of(half * core, 16), half), :]
        return ref.at[i]

    def down(self, peer):
        return remote(
            self.part(self.t, peer, self.core), self.part(self.out, self.which, self.core),
            self.os.at[0], self.ov.at[self.which], {"dp": self.dp, "ctx": peer},
        )

    def pair_copy(self, m, core):
        part = self.part(self.out, m, core)
        return remote(part, part, self.ps.at[0], self.pv.at[0], self.sibling)

    def side_copy(self, m, d):
        part = self.part(self.out, m, self.core)
        peer = {"dp": lax.rem(self.dp + 2 * d, 8), "ctx": self.ctx}
        return remote(part, part, self.bs.at[0], self.ov.at[m], peer)

    def begin(self):
        @pl.when(self.mine)
        def _():
            came(self.t.at[0:15], self.uv.at[0], {"dp": self.dp, "ctx": self.ctx})
            self.x[...] = self.t[...].reshape(16 * self.rows, self.cols).T
            newton_schulz_step(self.x, self.a, self.p, True)

    def go_on(self, steps):
        @pl.when(self.mine)
        def _():
            def step(_, carry):
                newton_schulz_step(self.x, self.a, self.p, False)
                return carry

            lax.fori_loop(0, steps, step, 0)

    def end(self):
        @pl.when(self.mine)
        def _():
            self.t[...] = self.x[...].T.reshape(16, self.rows, self.cols)

            def leave(d, carry):
                self.down(lax.rem(self.ctx + d, 16)).start()
                return carry

            lax.fori_loop(1, 16, leave, 0)
            self.part(self.out, self.which, self.core)[...] = self.part(self.t, self.ctx, self.core)[...]


    def pass_on(self):
        for m, owner in enumerate(self.owners):
            @pl.when(self.here[m] & self.carries[m])
            def _():
                @pl.when(self.ctx != owner)
                def _():
                    self.side_copy(m, 1).wait_recv()

                if not self.everywhere:
                    for d in (2, 1, 3):
                        self.side_copy(m, d).start()
                self.pair_copy(m, self.core).start()

    def collect(self):
        if self.everywhere:
            return
        for m in range(self.count):
            @pl.when(jnp.logical_not(self.here[m]) & self.carries[m])
            def _():
                self.side_copy(m, 1).wait_recv()
                self.pair_copy(m, self.core).start()

    def settle(self):
        if self.halves:
            every = self.part(self.out, pl.ds(0, self.count), 0)
        else:
            every = self.out.at[0]
        came(every, self.pv.at[0], self.sibling)
        sent(every, self.ps.at[0], self.sibling)

        @pl.when(self.mine)
        def _():
            sent(self.part(self.t, pl.ds(0, 15), self.core), self.os.at[0], self.sibling)

        for m, owner in enumerate(self.owners):
            @pl.when(self.here[m] & self.carries[m])
            def _():
                @pl.when(self.ctx != owner)
                def _():
                    self.up(m).wait_send()

                if not self.everywhere:
                    for d in (1, 2, 3):
                        self.side_copy(m, d).wait_send()


def update_of(momentum, gradient):
    return gradient + momentum_decay * (momentum_decay * momentum + gradient)


def dot(a, b):
    return jnp.dot(a, b, preferred_element_type=f32)


def rotated(u, cosine, sine):
    first, second = u[0:32], u[32:64]
    return first * cosine - second * sine, second * cosine + first * sine


def two_part(value):
    high = value.astype(bf16)
    return high, (value - high.astype(f32)).astype(bf16)


VALUE_AT = (128, 192, 64)


def layer_kernel(names, *refs):
    r = types.SimpleNamespace(**dict(zip(names, refs)))
    dp, ctx, x, core = place()
    axes = Axes()
    first, second, sa, sb = axes.first, axes.second, axes.sa, axes.sb
    barrier = greet_all(dp, ctx)
    K, QO, W = r.K, r.QO, r.W
    Q, O = QO.at[0], QO.at[1]
    gather_k = Gather(axes, K, r.gk)
    gather_qo = SideGather(axes, QO, r.gqo)
    gather_w = SplitGather(axes, W, r.gw)

    def lanes_at(p):
        return pl.ds(pl.multiple_of(128 * p, 128), 128)

    def spread(buffer, refs):
        return Along(
            axes, 0, lambda p: buffer.at[:, lanes_at(first)], lambda p: buffer.at[:, lanes_at(p)],
            buffer.at[:, 0:384], refs,
        )

    def deliver(source, target, refs):
        return Along(axes, 0, lambda p: source.at[p], lambda p: target.at[p], target.at[0:3], refs)

    N2, DY, DA, DQ, DKV = r.N2, r.DY, r.DA, r.DQ, r.DKV
    share_n2, share_dy = spread(N2, r.c_n2), spread(DY, r.c_dy)
    share_da, share_dq, share_dkv = spread(DA, r.c_da), spread(DQ, r.c_dq), spread(DKV, r.c_dkv)
    send_n1 = deliver(r.n1s, r.N1, r.c_n1)
    send_ob = deliver(r.obs, r.OB, r.c_ob)
    send_out = deliver(r.outs, r.outr, r.c_out)
    send_dn = deliver(r.dns, r.dnr, r.c_dn)
    send_gain = deliver(r.gps, r.gpr, r.c_gain)

    fin_f = r.fin_f
    ff = [Reduce(axes, r.fg.at[m], fin_f.at[m], True, PLANES_FF[m], r.rf[m]) for m in range(3)]
    sum_q = Reduce(axes, r.qg, r.fin_q, False, None, r.rq)
    sum_o = Reduce(axes, r.og, r.fin_o, False, None, r.ro)
    sum_k = Reduce(axes, r.kg, r.fin_k, False, None, r.rk)
    work = (r.nx, r.na, r.np)
    m_ff = Muon(OWNERS_FF, PLANES_FF, r.o_ff, r.whole, work, True, r.mf)
    m_sq = Muon(OWNERS_SQ, PLANES_SQ, r.o_sq, r.whole.at[:, 0:48], work, False, r.ms)
    m_kv = Muon(OWNERS_KV, PLANES_KV, r.o_kv, r.kv_whole, (r.nx, r.ka, r.kp), False, r.mk)

    def grouped(buffer, value):
        for s in range(16):
            a, b = pick(core, s % 4, s // 4), pick(core, s // 4, s % 4)
            buffer[a, pl.ds(pl.multiple_of(48 * b, 16), 48), :] = value[48 * s : 48 * s + 48]

    pad_sq, pad_kv, tile = r.pad_sq, r.pad_kv, r.tile
    pad_sq[...] = jnp.zeros_like(pad_sq)
    pad_kv[...] = jnp.zeros_like(pad_kv)
    tile[...] = jnp.zeros_like(tile)
    tile[64:66, 0:36] = r.gains[...]
    pad_kv[0, 0:36, 128:256] = tile[...].T[0:36, :]
    for m in range(2):
        pad_sq[m, 0:36, 0:576] = r.w_square[:, m, :]
        pad_kv[m, 0:36, 0:192] = r.w_kv[:, m, :]
        K[m, ctx] = pad_kv[m].astype(bf16)
    for half in range(2):
        for m in range(2):
            QO[m, half, ctx] = pad_sq[m, :, 384 * half : 384 * half + 384].astype(bf16)
    W[0, second] = r.w_gate_up[0].astype(bf16)
    W[1, second] = r.w_gate_up[1].astype(bf16)
    W[2, second] = r.w_down[...].astype(bf16)
    pl.semaphore_wait(barrier, 19)
    gather_k.start()
    gather_qo.start()
    gather_w.start(1)
    DY[:, lanes_at(first)] = r.cotangent[...]

    spread_in, spread_out = r.E, r.ET
    row = lax.broadcasted_iota(jnp.int32, (768, 1), 0)
    step = jnp.zeros((768, 1), jnp.int32)
    for t in range(1, 16):
        step = step + (row >= 48 * t).astype(jnp.int32)
    home = jnp.where(row - 48 * step < 36, row - 12 * step, -1)
    col = lax.broadcasted_iota(jnp.int32, (768, 576), 1)
    spread_out[...] = (col == home).astype(f32).astype(bf16)

    xT = r.tokens[...].astype(f32)
    r1 = lax.rsqrt(jnp.sum(xT * xT, axis=0, keepdims=True) * (1.0 / 576) + norm_eps)
    hat1 = xT * r1
    r.hat1[...] = hat1
    high, low = two_part(hat1)
    hat1_wide = dot(spread_out[...], high) + dot(spread_out[...], low)
    gather_k.forward()
    gather_qo.forward()
    gather_w.start(0)
    row = lax.broadcasted_iota(jnp.int32, (576, 1), 0)
    step = jnp.zeros((576, 1), jnp.int32)
    for t in range(1, 16):
        step = step + (row >= 36 * t).astype(jnp.int32)
    col = lax.broadcasted_iota(jnp.int32, (576, 768), 1)
    spread_in[...] = (col == row + 12 * step).astype(f32).astype(bf16)
    pos = r.positions[...]
    row = lax.broadcasted_iota(jnp.int32, (32, 128), 0)
    freqs = jnp.zeros((32, 128), f32)
    for i in range(32):
        freqs = jnp.where(row == i, rope_base ** (-2.0 * i / HEAD_WIDTH), freqs)
    angle = freqs * pos.astype(f32)
    cosine, sine = jnp.cos(angle), jnp.sin(angle)
    r.cos[...] = cosine
    r.sin[...] = sine
    gather_k.swap()
    gather_k.finish()

    n1_wide = (hat1_wide * K[0, :, :, 192:193].reshape(768, 1).astype(f32)).astype(bf16)
    n1 = n1_wide.T
    kT = dot(n1, K[0].reshape(768, 256)).T
    vT = dot(n1, K[1].reshape(768, 256)).T
    kv, kvT, QT = r.kv, r.kvT, r.QT
    own = []
    for c in range(3):
        own += rotated(kT[64 * c : 64 * c + 64], cosine, sine)
    own += [vT[128:192], vT[0:128]]
    kv[ctx] = jnp.concatenate(own, axis=0).T.astype(bf16)

    def slice_of(a, b):
        return a * sa + b * sb

    def reach(a):
        return a * sa + 3 * sb

    def kv_near(d):
        return remote(kv.at[ctx], kv.at[ctx], r.ks.at[0], r.kr.at[ctx], axes.near(d))

    def kv_far(src, e, d):
        return remote(kv.at[src], kv.at[src], r.ks.at[0], r.kr.at[src], axes.far(d))

    def kv_arrive(src):
        remote(kv.at[src], kv.at[src], r.ks.at[0], r.kr.at[src], axes.sibling).wait_recv()

    def near_wanted(d):
        return reach(lax.rem(first + d, 4)) > ctx

    def far_wanted(src, d):
        return slice_of(first, lax.rem(second + d, 4)) > src

    for d in (2, 1, 3):
        @pl.when(near_wanted(d))
        def _():
            kv_near(d).start()

    for d in (2, 1, 3):
        @pl.when(far_wanted(ctx, d))
        def _():
            kv_far(ctx, 0, d).start()

    for i in range(1, 4):
        @pl.when((lax.rem(ctx, 4) + i < 4) & ((core == 1) | (ctx >= 12)))
        def _():
            kv[ctx + i] = jnp.zeros((128, 384), bf16)

    gather_qo.swap()
    for e in (1, 3, 2):
        src = axes.slice_at(e, 0)

        @pl.when(reach(first) > src)
        def _():
            kv_arrive(src)
            for d in (2, 1, 3):
                @pl.when(far_wanted(src, d))
                def _():
                    kv_far(src, e, d).start()

    gather_w.forward()
    gather_qo.side()
    gather_qo.finish()
    QT[...] = jnp.zeros_like(QT)
    qT = [dot(n1, Q[half].reshape(768, 384)).T for half in range(2)]
    for h in range(9):
        c = h // 3
        part = qT[h // 6][64 * (h % 6) : 64 * (h % 6) + 64]
        a, b = rotated(part, cosine, sine)
        lanes = slice(128 * h, 128 * h + 128)
        QT[64 * c : 64 * c + 32, lanes] = (a.astype(bf16).astype(f32) * 0.125).astype(bf16)
        QT[64 * c + 32 : 64 * c + 64, lanes] = (b.astype(bf16).astype(f32) * 0.125).astype(bf16)

    @pl.when(core == 0)
    def _():
        share_dy.start()

    S, eb, tops, top, total, fade, oT = r.S, r.eb, r.tops, r.top, r.total, r.fade, r.oT
    top[...] = jnp.full_like(top, HIDDEN)
    total[...] = jnp.zeros_like(total)
    oT[...] = jnp.zeros_like(oT)
    groups = lax.div(ctx, 4) + 1

    def attend(g, carry):
        for i in range(4):
            j = 4 * g + i

            @pl.when((j < ctx) & (pick(core, g, i) != second))
            def _():
                kv_arrive(j)

        block = kv[pl.ds(4 * g, 4)].reshape(512, 384)
        kvT[g] = block.T
        S[...] = dot(block[:, 0:256], QT[...])
        key = 512 * g + lax.broadcasted_iota(jnp.int32, (512, 128), 0)
        query = 128 * ctx + lax.broadcasted_iota(jnp.int32, (512, 128), 1)
        allowed = (key <= query) & (key >= query - pos)
        for h in range(9):
            lanes = slice(128 * h, 128 * h + 128)
            s = jnp.where(allowed, S[:, lanes], HIDDEN)
            before = top[:, lanes]
            now = jnp.maximum(before, jnp.max(s, axis=0, keepdims=True))
            weights = jnp.exp(s - now)
            damping = jnp.exp(before - now)
            total[:, lanes] = total[:, lanes] * damping + jnp.sum(weights, axis=0, keepdims=True)
            fade[:, lanes] = damping
            top[:, lanes] = now
            tops[g, :, lanes] = now
            eb[g, :, lanes] = weights.astype(bf16)
        oT[...] = oT[...] * fade[...] + dot(kvT[g, 128:384, :], eb[g])
        return carry

    lax.fori_loop(0, groups, attend, 0)
    @pl.when(core == 1)
    def _():
        share_dy.start()

    share = 1.0 / total[...]
    o = r.o
    for h in range(9):
        at_row = VALUE_AT[h // 3]
        lanes = slice(128 * h, 128 * h + 128)
        o[64 * h : 64 * h + 64, :] = oT[at_row : at_row + 64, lanes] * share[:, lanes]
    ob_wide = dot(spread_out[...], o[...].astype(bf16)).astype(bf16)
    ob = ob_wide.T
    mixed = [dot(ob, O[half].reshape(768, 384)).T for half in range(2)]
    hT = r.tokens[...].astype(f32) + jnp.concatenate([mixed[0], mixed[1][0:192]], axis=0)
    r2 = lax.rsqrt(jnp.sum(hT * hT, axis=0, keepdims=True) * (1.0 / 576) + norm_eps)
    hat2 = hT * r2
    gain_cols = dot(spread_in[...], K[0, :, :, 128:256].reshape(768, 128))
    N2[:, lanes_at(first)] = (hat2 * gain_cols[:, 65:66]).astype(bf16)
    share_n2.start()
    r.h[...] = hT
    r.hat2[...] = hat2
    grouped(r.obs, ob_wide)
    r.OB[first] = r.obs[first]
    grouped(r.n1s, n1_wide)
    r.N1[first] = r.n1s[first]
    gather_w.wait()
    share_dy.wait()
    dhid = dot(W[2].reshape(384, 576), DY[...])
    share_n2.wait()

    gate = dot(W[0].reshape(384, 576), N2[...])
    up = dot(W[1].reshape(384, 576), N2[...])
    sig = jax.nn.sigmoid(gate)
    silu = gate * sig
    hid, dgate, dup = r.hid, r.dgate, r.dup
    dgate[...] = (dhid * up * sig * (1.0 + gate * (1.0 - sig))).astype(bf16)
    dup[...] = (dhid * silu).astype(bf16)
    hid[...] = (silu * up).astype(bf16)
    part = lax.dot_general(W[0].reshape(384, 576), dgate[...], TN, preferred_element_type=f32)
    part = part + lax.dot_general(W[1].reshape(384, 576), dup[...], TN, preferred_element_type=f32)
    for p in range(4):
        r.dns[p] = part[:, 128 * p : 128 * p + 128].astype(bf16)
    send_dn.start()
    for m, left, right in ((2, hid, DY), (0, dgate, N2), (1, dup, N2)):
        part = lax.dot_general(left[...], right[...], NT, preferred_element_type=f32).astype(bf16)
        for p in range(4):
            r.fg[m, p] = part[96 * p : 96 * p + 96]
        ff[m].start()
    part = lax.dot_general(W[2].reshape(384, 576), hid[...], TN, preferred_element_type=f32)
    for p in range(4):
        r.outs[p] = part[:, 128 * p : 128 * p + 128].astype(bf16)

    send_dn.wait()
    dn2T = r.dns[first].astype(f32)
    for d in range(1, 4):
        dn2T = dn2T + r.dnr[lax.rem(first + d, 4)].astype(f32)
    hat2 = r.hat2[...]
    shaped = dn2T * gain_cols[:, 65:66]
    mean = jnp.sum(shaped * hat2, axis=0, keepdims=True) * (1.0 / 576)
    dhT = r.cotangent[...].astype(f32) + r2 * (shaped - hat2 * mean)
    r.dhT[...] = dhT
    gain_two = jnp.sum(dn2T * hat2, axis=1, keepdims=True)
    daT = dhT.astype(bf16)
    DA[:, lanes_at(first)] = daT
    send_ob.start()
    share_da.start()
    send_n1.start()
    dob_wide = dot(O[0].reshape(768, 384), daT[0:384]) + dot(O[1, :, :, 0:192].reshape(768, 192), daT[384:576])
    dobT = dot(spread_in[...], dob_wide.astype(bf16))
    dO, dQ, delta = r.dO, oT, r.delta
    dO[...] = jnp.zeros_like(dO)
    dQ[...] = jnp.zeros_like(dQ)
    for h in range(9):
        at_row = VALUE_AT[h // 3]
        lanes = slice(128 * h, 128 * h + 128)
        part = dobT[64 * h : 64 * h + 64]
        dO[at_row : at_row + 64, lanes] = part.astype(bf16)
        delta[:, lanes] = jnp.sum(part * o[64 * h : 64 * h + 64, :], axis=0, keepdims=True)

    dkv_out, dkv_in, dOg = r.dkv_out, r.dkv_in, r.dOg

    def dkv_far(j, a, b):
        device = {"dp": dp, "ctx": ctx + (b - second) * sb}
        return remote(dkv_out.at[j], dkv_in.at[second, a], r.ds1.at[0], r.dr1.at[second, a], device)

    def attend_back(g, carry):
        factor = jnp.exp(tops[g] - top[...]) / total[...]
        dOg[...] = (dO[...].astype(f32) * factor).astype(bf16)
        block = kv[pl.ds(4 * g, 4)].reshape(512, 384)
        S[...] = dot(block[:, 128:384], dOg[...])
        inner = delta[...] * factor
        dv = lax.dot_general(eb[g], dOg[...], NT, preferred_element_type=f32)
        for h in range(9):
            lanes = slice(128 * h, 128 * h + 128)
            eb[g, :, lanes] = (eb[g, :, lanes].astype(f32) * (S[:, lanes] - inner[:, lanes])).astype(bf16)
        dk = lax.dot_general(eb[g], QT[...], NT, preferred_element_type=f32)
        dQ[...] = dQ[...] + dot(kvT[g, 0:256, :], eb[g])
        out = jnp.concatenate([dk[:, 0:128], dk[:, 128:256] + dv[:, 0:128], dv[:, 128:256]], axis=1)
        dkv_out[pl.ds(4 * g, 4)] = out.astype(bf16).reshape(4, 128, 384)
        for i in range(4):
            j = 4 * g + i
            a, b = pick(core, i, g), pick(core, g, i)

            @pl.when((j < ctx) & (b != second))
            def _():
                dkv_far(j, a, b).start()

        return carry

    lax.fori_loop(0, groups, attend_back, 0)
    def gathered_rows(buffer):
        return jnp.concatenate([buffer[p] for p in range(4)], axis=1)

    def gradient(rows, columns):
        return lax.dot_general(rows, columns, NT, preferred_element_type=f32)

    def send_ff(m, momentum):
        @pl.when(ff[m].here)
        def _():
            ff[m].third_sum()
            ff[m].finish()
            for half in range(2):
                rows = slice(48 * half, 48 * half + 48)
                m_ff.u[m, rows] = update_of(momentum[rows, :], fin_f[m, half].astype(f32)).astype(bf16)
            m_ff.send(m)

    def send_sq(m, reduced):
        @pl.when(reduced.here)
        def _():
            reduced.third_sum()
            m_sq.u[m] = update_of(pad_sq[m, :, 0:576], reduced.fin[...].astype(f32)).astype(bf16)
            m_sq.send(m)

    cosine, sine = r.cos[...], r.sin[...]
    dqT = r.dqT
    for h in range(9):
        c = h // 3
        lanes = slice(128 * h, 128 * h + 128)
        a, b = rotated(dQ[64 * c : 64 * c + 64, lanes] * 0.125, cosine, -sine)
        dqT[64 * h : 64 * h + 32, :] = a.astype(bf16)
        dqT[64 * h + 32 : 64 * h + 64, :] = b.astype(bf16)
    DQ[:, lanes_at(first)] = dqT[...]
    share_dq.start()
    dn1_wide = dot(Q[0].reshape(768, 384), dqT[0:384]) + dot(Q[1, :, :, 0:192].reshape(768, 192), dqT[384:576])
    ff[2].second_sum()
    ff[0].second_sum()
    ff[2].pair_sum()
    ff[1].second_sum()
    ff[0].pair_sum()
    ff[1].pair_sum()
    send_ff(2, r.mom_down)
    send_ff(0, r.mom_gate_up.at[0])
    send_ff(1, r.mom_gate_up.at[1])
    mid, mid_in, own_sum = r.mid, r.mid_in, r.own_sum

    def dkv_near(d):
        return remote(mid.at[d - 1], mid_in.at[d - 1], r.ds2.at[0], r.dr2.at[d - 1], axes.near(d))

    for e in (2, 1, 3, 0):
        a = lax.rem(first + e, 4)
        target = slice_of(a, second)
        own_sum[...] = jnp.zeros_like(own_sum)

        @pl.when(target <= ctx)
        def _():
            own_sum[...] = dkv_out[target].astype(f32)

        for k in range(1, 4):
            b = lax.rem(second + k, 4)

            @pl.when(target < slice_of(first, b))
            def _():
                remote(
                    dkv_in.at[b, a], dkv_in.at[b, a], r.ds1.at[0], r.dr1.at[b, a], axes.sibling
                ).wait_recv()
                own_sum[...] += dkv_in[b, a].astype(f32)

        if e:
            @pl.when(reach(first) > target)
            def _():
                mid[e - 1] = own_sum[...].astype(bf16)
                dkv_near(e).start()

    send_ob.wait()
    share_da.wait()
    part = gradient(gathered_rows(r.OB), DA[...]).astype(bf16)
    for p in range(4):
        r.og[p] = part[48 * p : 48 * p + 48]
    sum_o.start()
    send_n1.wait()
    share_dq.wait()
    n1_rows = gathered_rows(r.N1)
    part = gradient(n1_rows, DQ[...]).astype(bf16)
    for p in range(4):
        r.qg[p] = part[48 * p : 48 * p + 48]
    sum_q.start()
    for d in range(1, 4):
        @pl.when(reach(lax.rem(first + 4 - d, 4)) > ctx)
        def _():
            dkv_near(d).wait_recv()
            own_sum[...] += mid_in[d - 1].astype(f32)

    dkvT = own_sum[...].T
    dk = []
    for c in range(3):
        dk += rotated(dkvT[64 * c : 64 * c + 64], cosine, -sine)
    dkT = jnp.concatenate(dk, axis=0).astype(bf16)
    dvT = jnp.concatenate([dkvT[256:384], dkvT[192:256]], axis=0).astype(bf16)
    DKV[0:192, lanes_at(first)] = dkT
    DKV[192:384, lanes_at(first)] = dvT
    share_dkv.start()
    dn1_wide = dn1_wide + dot(K[0, :, :, 0:192].reshape(768, 192), dkT) + dot(
        K[1, :, :, 0:192].reshape(768, 192), dvT
    )
    high, low = two_part(dn1_wide)
    dn1T = dot(spread_in[...], high) + dot(spread_in[...], low)
    hat1 = r.hat1[...]
    gain_one = jnp.sum(dn1T * hat1, axis=1, keepdims=True)
    lane = lax.broadcasted_iota(jnp.int32, (576, 128), 1)
    columns = jnp.where(lane == 64, gain_one, jnp.where(lane == 65, gain_two, 0.0)).astype(bf16)
    grouped(r.gps, dot(spread_out[...], columns).astype(bf16))
    send_gain.start()
    shaped = dn1T * gain_cols[:, 64:65]
    mean = jnp.sum(shaped * hat1, axis=0, keepdims=True) * (1.0 / 576)
    r.ginT[...] = (r.dhT[...] + r1 * (shaped - hat1 * mean)).astype(bf16)

    sum_o.second_sum()
    sum_o.pair_sum()
    sum_q.second_sum()
    sum_q.pair_sum()
    pad_kv[0, 0:36, 192:256] = jnp.zeros((36, 64), f32)
    for m in range(2):
        pad_sq[m, 0:36, 0:576] = r.mom_square[:, m, :]
        pad_kv[m, 0:36, 0:192] = r.mom_kv[:, m, :]

    share_dkv.wait()
    part_k = gradient(n1_rows, DKV[0:192, :])
    part_v = gradient(n1_rows, DKV[192:384, :]).astype(bf16)
    send_gain.wait()
    gains_sum = r.gps[first].astype(f32)
    for d in range(1, 4):
        gains_sum = gains_sum + r.gpr[lax.rem(first + d, 4)].astype(f32)
    edge = (jnp.concatenate([part_k[:, 128:192], jnp.zeros((192, 64), f32)], axis=1) + gains_sum).astype(bf16)
    part_k = part_k.astype(bf16)
    kg = r.kg
    for p in range(4):
        rows = slice(48 * p, 48 * p + 48)
        kg[p, :, 0:128] = part_k[rows, 0:128]
        kg[p, :, 128:256] = edge[rows]
        kg[p, :, 256:448] = part_v[rows]
        kg[p, :, 448:512] = jnp.zeros((48, 64), bf16)
    sum_k.start()

    send_sq(1, sum_o)
    send_sq(0, sum_q)
    m_ff.begin()
    sum_k.second_sum()
    sum_k.pair_sum()
    m_ff.go_on(2)
    fin_k, gsend, gain_sums, gain_total = r.fin_k, r.gsend, r.gain_sums, r.gain_total

    @pl.when(sum_k.here)
    def _():
        sum_k.third_sum()
        for m in range(2):
            part = fin_k[:, 256 * m : 256 * m + 192].astype(f32)
            m_kv.u[m] = update_of(pad_kv[m, :, 0:192], part).astype(bf16)
            m_kv.send(m)

        gain_grads = fin_k[:, 128:256].astype(f32).T[64:66, 0:36]
        gain_next = momentum_decay * r.mom_gains[...] + gain_grads
        sums = jnp.sum(gain_next * gain_next, axis=1, keepdims=True)
        gsend[0:2, :] = jnp.broadcast_to(sums, (2, 128))
        gsend[2:8, :] = jnp.zeros((6, 128), f32)
        gain_sums[ctx] = gsend[...]
        for d in range(1, 16):
            remote(
                gsend, gain_sums.at[ctx], r.gs.at[0], r.gv.at[0], {"dp": dp, "ctx": lax.rem(ctx + d, 16)}
            ).start()

    send_out.start()
    m_sq.begin()
    m_sq.go_on(2)
    m_ff.go_on(NS_ITERS - 3)
    m_ff.end()
    m_kv.begin()
    m_kv.go_on(NS_ITERS - 1)
    m_kv.end()
    m_sq.go_on(NS_ITERS - 3)
    m_sq.end()
    came(gain_sums.at[0:15], r.gv.at[0], axes.sibling)
    total_gains = gain_sums[0]
    for k in range(1, 16):
        total_gains = total_gains + gain_sums[k]
    gain_total[...] = total_gains

    send_out.wait()
    total_out = r.h[...] + r.outs[first].astype(f32)
    for d in range(1, 4):
        total_out = total_out + r.outr[lax.rem(first + d, 4)].astype(f32)
    r.outT[...] = total_out.astype(bf16)
    for each in (*ff, sum_o, sum_q, sum_k):
        each.collect()
    m_ff.pass_on()
    m_sq.pass_on()
    m_kv.pass_on()
    m_sq.collect()
    m_kv.collect()
    m_ff.collect()

    sent(gain_sums.at[0:15], r.gs.at[0], axes.sibling)
    m_kv.settle()
    m_sq.settle()
    m_ff.settle()
    for d in range(1, 4):
        @pl.when(near_wanted(d))
        def _():
            kv_near(d).wait_send()

        @pl.when(reach(first) > slice_of(lax.rem(first + d, 4), second))
        def _():
            dkv_near(d).wait_send()

        for e in range(4):
            src = axes.slice_at(e, 0)
            held = True if e == 0 else reach(first) > src

            @pl.when(far_wanted(src, d) & held)
            def _():
                kv_far(src, e, d).wait_send()

    def dkv_gone(j, carry):
        y, z = lax.div(j, 4), lax.rem(j, 4)
        a, b = pick(core, z, y), pick(core, y, z)

        @pl.when(b != second)
        def _():
            dkv_far(j, a, b).wait_send()

        return carry

    lax.fori_loop(0, ctx, dkv_gone, 0)
    for each in (
        *ff, sum_o, sum_q, sum_k, gather_k, gather_qo, gather_w, share_n2, share_dy, share_da, share_dq,
        share_dkv, send_n1, send_ob, send_out, send_dn, send_gain,
    ):
        each.drain()


def whole(memory=pltpu.VMEM):
    return pl.BlockSpec(memory_space=memory)


def run_layer(inputs):
    outs = dict(
        outT=((576, 128), bf16),
        ginT=((576, 128), bf16),
        fin_f=((3, 2, 48, 576), bf16),
        fin_q=((48, 576), bf16),
        fin_o=((48, 576), bf16),
        fin_k=((48, 512), bf16),
        o_ff=((3, 96, 576), bf16),
        o_sq=((2, 48, 576), bf16),
        o_kv=((2, 48, 192), bf16),
        gain_total=((8, 128), f32),
    )
    dma = pltpu.SemaphoreType.DMA
    scratch = dict(
        K=pltpu.VMEM((2, 16, 48, 256), bf16),
        QO=pltpu.VMEM((2, 2, 16, 48, 384), bf16),
        W=pltpu.VMEM((3, 4, 96, 576), bf16),
        pad_sq=pltpu.VMEM((2, 48, 768), f32),
        pad_kv=pltpu.VMEM((2, 48, 256), f32),
        tile=pltpu.VMEM((128, 128), f32),
        E=pltpu.VMEM((576, 768), bf16),
        ET=pltpu.VMEM((768, 576), bf16),
        cos=pltpu.VMEM((32, 128), f32),
        sin=pltpu.VMEM((32, 128), f32),
        kv=pltpu.VMEM((16, 128, 384), bf16),
        kvT=pltpu.VMEM((4, 384, 512), bf16),
        QT=pltpu.VMEM((256, 1152), bf16),
        S=pltpu.VMEM((512, 1152), f32),
        eb=pltpu.VMEM((4, 512, 1152), bf16),
        tops=pltpu.VMEM((4, 1, 1152), f32),
        oT=pltpu.VMEM((256, 1152), f32),
        dO=pltpu.VMEM((256, 1152), bf16),
        dOg=pltpu.VMEM((256, 1152), bf16),
        dkv_out=pltpu.VMEM((16, 128, 384), bf16),
        dkv_in=pltpu.VMEM((4, 4, 128, 384), bf16),
        mid=pltpu.VMEM((3, 128, 384), bf16),
        mid_in=pltpu.VMEM((3, 128, 384), bf16),
        own_sum=pltpu.VMEM((128, 384), f32),
        dqT=pltpu.VMEM((576, 128), bf16),
        DKV=pltpu.VMEM((384, 512), bf16),
        fg=pltpu.VMEM((3, 4, 96, 576), bf16),
        qg=pltpu.VMEM((4, 48, 576), bf16),
        og=pltpu.VMEM((4, 48, 576), bf16),
        kg=pltpu.VMEM((4, 48, 512), bf16),
        gsend=pltpu.VMEM((8, 128), f32),
        nx=pltpu.VMEM((576, 1536), bf16),
        na=pltpu.VMEM((576, 576), bf16),
        np=pltpu.VMEM((576, 576), bf16),
        ka=pltpu.VMEM((192, 192), bf16),
        kp=pltpu.VMEM((192, 192), bf16),
        whole=pltpu.VMEM((16, 96, 576), bf16),
        kv_whole=pltpu.VMEM((16, 48, 192), bf16),
        gain_sums=pltpu.VMEM((16, 8, 128), f32),
        gs=dma((1,)),
        gv=dma((1,)),
        ks=dma((1,)),
        kr=dma((16,)),
        ds1=dma((1,)),
        dr1=dma((4, 4)),
        ds2=dma((1,)),
        dr2=dma((3,)),
        gk=Gather.scratch(),
        gqo=SideGather.scratch(),
        gw=SplitGather.scratch(),
        rf=[Reduce.scratch(96, 576, True) for _ in range(3)],
        rq=Reduce.scratch(48, 576, False),
        ro=Reduce.scratch(48, 576, False),
        rk=Reduce.scratch(48, 512, False),
        mf=Muon.scratch(3, 96, 576),
        ms=Muon.scratch(2, 48, 576),
        mk=Muon.scratch(2, 48, 192),
        top=pltpu.VMEM((1, 1152), f32),
        total=pltpu.VMEM((1, 1152), f32),
        fade=pltpu.VMEM((1, 1152), f32),
        delta=pltpu.VMEM((1, 1152), f32),
        hat1=pltpu.VMEM((576, 128), f32),
        hat2=pltpu.VMEM((576, 128), f32),
        h=pltpu.VMEM((576, 128), f32),
        o=pltpu.VMEM((576, 128), f32),
        dhT=pltpu.VMEM((576, 128), f32),
        N2=pltpu.VMEM((576, 512), bf16),
        DY=pltpu.VMEM((576, 512), bf16),
        DA=pltpu.VMEM((576, 512), bf16),
        DQ=pltpu.VMEM((576, 512), bf16),
        hid=pltpu.VMEM((384, 512), bf16),
        dgate=pltpu.VMEM((384, 512), bf16),
        dup=pltpu.VMEM((384, 512), bf16),
        outs=pltpu.VMEM((4, 576, 128), bf16),
        outr=pltpu.VMEM((4, 576, 128), bf16),
        dns=pltpu.VMEM((4, 576, 128), bf16),
        dnr=pltpu.VMEM((4, 576, 128), bf16),
        n1s=pltpu.VMEM((4, 192, 128), bf16),
        N1=pltpu.VMEM((4, 192, 128), bf16),
        obs=pltpu.VMEM((4, 192, 128), bf16),
        OB=pltpu.VMEM((4, 192, 128), bf16),
        gps=pltpu.VMEM((4, 192, 128), bf16),
        gpr=pltpu.VMEM((4, 192, 128), bf16),
        c_n2=Along.scratch(),
        c_dy=Along.scratch(),
        c_da=Along.scratch(),
        c_dq=Along.scratch(),
        c_dkv=Along.scratch(),
        c_n1=Along.scratch(),
        c_ob=Along.scratch(),
        c_out=Along.scratch(),
        c_dn=Along.scratch(),
        c_gain=Along.scratch(),
    )
    names = [*inputs, *outs, *scratch]
    scratch_list = list(scratch.values())

    def kernel(*refs):
        layer_kernel(names, *refs)

    return pl.pallas_call(
        kernel,
        out_shape=tuple(jax.ShapeDtypeStruct(*o) for o in outs.values()),
        in_specs=[whole()] * len(inputs),
        out_specs=[whole()] * len(outs),
        scratch_shapes=scratch_list,
        compiler_params=pltpu.CompilerParams(
            collective_id=3, has_side_effects=True, vmem_limit_bytes=VMEM_LIMIT
        ),
    )(*inputs.values())


VMEM_LIMIT = 63 * 2**20


def finish_kernel(
    outT, ginT, fin_f, fin_q, fin_o, fin_k, o_ff, o_sq, o_kv, gain_total, w_square, w_kv, w_gate_up, w_down, gains,
    mom_square, mom_kv, mom_gate_up, mom_down, mom_gains,
    out, gin, grad_square, grad_kv, grad_gate_up, grad_down, grad_gains,
    next_square, next_kv, next_gate_up, next_down, next_gains,
    new_square, new_kv, new_gate_up, new_down, new_gains,
):
    shrink = 1.0 - learn_rate * weight_decay
    out[...] = outT[...]
    gin[...] = ginT[...]

    def one(at, grad, width, weight, momentum, ortho, grad_out, next_out, new_out):
        grad_out[at] = grad
        next_out[at] = momentum_decay * momentum[at] + grad
        new_out[at] = shrink * weight[at] - learn_rate * (0.2 * math.sqrt(width)) * ortho

    everything = slice(None)
    for m, fin in enumerate((fin_q, fin_o)):
        one((everything, m, everything), fin[...].astype(f32)[0:36], 576, w_square, mom_square,
            o_sq[m].astype(f32)[0:36], grad_square, next_square, new_square)
    for m in range(2):
        one((everything, m, everything), fin_k[:, 256 * m : 256 * m + 192].astype(f32)[0:36], 576, w_kv, mom_kv,
            o_kv[m].astype(f32)[0:36], grad_kv, next_kv, new_kv)
    for half in range(2):
        rows = slice(48 * half, 48 * half + 48)
        for m in range(2):
            one((m, rows), fin_f[m, half].astype(f32), 1536, w_gate_up, mom_gate_up,
                o_ff[m, rows].astype(f32), grad_gate_up, next_gate_up, new_gate_up)
        one(rows, fin_f[2, half].astype(f32), 1536, w_down, mom_down,
            o_ff[2, rows].astype(f32), grad_down, next_down, new_down)
    gain_grads = fin_k[:, 128:256].astype(f32).T[64:66, 0:36]
    gain_next = momentum_decay * mom_gains[...] + gain_grads
    mean = gain_total[0:2, 0:1] * (1.0 / 576)
    grad_gains[...] = gain_grads
    next_gains[...] = gain_next
    new_gains[...] = gains[...] - gain_rate * gain_next / jnp.sqrt(mean + 1e-06)


def finish(packed, weights, momenta):
    shapes = [jax.ShapeDtypeStruct((576, 128), bf16)] * 2
    shapes += [jax.ShapeDtypeStruct(a.shape, f32) for a in weights] * 3
    return pl.pallas_call(
        finish_kernel,
        out_shape=tuple(shapes),
        in_specs=[whole()] * 20,
        out_specs=[whole()] * 17,
        compiler_params=pltpu.CompilerParams(vmem_limit_bytes=VMEM_LIMIT),
    )(*packed, *weights, *momenta)


def swapped(a):
    return jnp.transpose(a, (1, 0, 2))


def shards(
    tokens, positions, cotangent, w_square, w_kv, w_gate_up, w_down, gains,
    mom_square, mom_kv, mom_gate_up, mom_down, mom_gains,
):
    weights = (swapped(w_square), swapped(w_kv), w_gate_up, w_down, gains)
    momenta = (swapped(mom_square), swapped(mom_kv), mom_gate_up, mom_down, mom_gains)
    inputs = dict(
        tokens=tokens[0].T,
        positions=positions,
        cotangent=cotangent[0].T,
        w_square=weights[0],
        w_kv=weights[1],
        w_gate_up=weights[2],
        w_down=weights[3],
        gains=weights[4],
        mom_square=momenta[0],
        mom_kv=momenta[1],
        mom_gate_up=momenta[2],
        mom_down=momenta[3],
        mom_gains=momenta[4],
    )
    outs = list(finish(run_layer(inputs), weights, momenta))
    outs[0] = outs[0].T[None]
    outs[1] = outs[1].T[None]
    for i in (2, 3, 7, 8, 12, 13):
        outs[i] = swapped(outs[i])
    return tuple(outs)


def solution(mesh):
    return jax.shard_map(
        shards,
        mesh=mesh,
        in_specs=(
            P("dp", "ctx", None),
            P("dp", "ctx"),
            P("dp", "ctx", None),
            P(None, "ctx", None),
            P(None, "ctx", None),
            P(None, "ctx", None),
            P("ctx", None),
            P(None, "ctx"),
            P(None, "ctx", None),
            P(None, "ctx", None),
            P(None, "ctx", None),
            P("ctx", None),
            P(None, "ctx"),
        ),
        out_specs=(
            P("dp", "ctx", None),
            P("dp", "ctx", None),
            *(P(None, "ctx", None), P(None, "ctx", None), P(None, "ctx", None), P("ctx", None), P(None, "ctx")) * 3,
        ),
        check_vma=False,
    )
```

```python
import math
import types

import jax
import jax.numpy as jnp
from jax import lax
from jax.experimental import pallas as pl
from jax.experimental.pallas import tpu as pltpu
from jax.sharding import PartitionSpec as P

HEAD_WIDTH = 64
NS_ITERS = 5

norm_eps = 1e-05
rope_base = 100000.0
momentum_decay = 0.95
learn_rate = 0.2
weight_decay = 0.1
gain_rate = 0.25
poly_first = 3.4445
poly_second = -4.775
poly_third = 2.0315

MESH = pl.DeviceIdType.MESH
bf16 = jnp.bfloat16
f32 = jnp.float32
NT = (((1,), (1,)), ((), ()))
TN = (((0,), (0,)), ((), ()))
HIDDEN = -1e30

OWNERS_FF = ((0, 5, 10), (15, 2, 8))
OWNERS_SQ = ((3, 12), (7, 13))
OWNERS_KV = ((6, 9), (4, 1))
PLANES_FF = (1, 2, 0)
PLANES_SQ = (None, None)
PLANES_KV = (None, None)


def place():
    dp = lax.axis_index("dp")
    ctx = lax.axis_index("ctx")
    core = lax.rem(dp, 2)
    return dp, ctx, lax.div(dp, 2), core


def pick(core, first, second):
    return first + core * (second - first)


def remote(src, dst, send_sem, recv_sem, device):
    return pltpu.make_async_remote_copy(
        src_ref=src, dst_ref=dst, send_sem=send_sem, recv_sem=recv_sem, device_id=device, device_id_type=MESH
    )


def greet_all(dp, ctx):
    barrier = pltpu.get_barrier_semaphore()
    for d in range(1, 16):
        pl.semaphore_signal(
            barrier, inc=1, device_id={"dp": dp, "ctx": lax.rem(ctx + d, 16)}, device_id_type=MESH
        )
    for d in range(1, 4):
        pl.semaphore_signal(
            barrier, inc=1, device_id={"dp": lax.rem(dp + 2 * d, 8), "ctx": ctx}, device_id_type=MESH
        )
    pl.semaphore_signal(
        barrier, inc=1, device_id={"dp": dp + 1 - 2 * lax.rem(dp, 2), "ctx": ctx}, device_id_type=MESH
    )
    return barrier


def sent(bytes_like, sem, device):
    remote(bytes_like, bytes_like, sem, sem, device).wait_send()


def came(bytes_like, sem, device):
    remote(bytes_like, bytes_like, sem, sem, device).wait_recv()


class Axes:
    def __init__(self):
        self.dp, self.ctx, self.x, self.core = place()
        y, z = lax.div(self.ctx, 4), lax.rem(self.ctx, 4)
        self.first = pick(self.core, z, y)
        self.second = pick(self.core, y, z)
        self.sa = pick(self.core, 1, 4)
        self.sb = pick(self.core, 4, 1)
        self.sibling = {"dp": self.dp + 1 - 2 * self.core, "ctx": self.ctx}

    def near(self, d):
        a = lax.rem(self.first + d, 4)
        return {"dp": self.dp, "ctx": self.ctx + (a - self.first) * self.sa}

    def far(self, d):
        b = lax.rem(self.second + d, 4)
        return {"dp": self.dp, "ctx": self.ctx + (b - self.second) * self.sb}

    def beside(self, before):
        return {"dp": lax.rem(self.dp + pick(before, 2, 6), 8), "ctx": self.ctx}

    def slice_at(self, back_first, back_second):
        a = lax.rem(self.first + 4 - back_first, 4)
        b = lax.rem(self.second + 4 - back_second, 4)
        return a * self.sa + b * self.sb


class Gather:
    @staticmethod
    def scratch():
        dma = pltpu.SemaphoreType.DMA
        return [dma((2,)), dma((3,)), dma((4, 3)), dma((1,))]

    def __init__(self, axes, pack, refs):
        self.axes, self.pack = axes, pack
        self.s, self.v1, self.v2, self.vp = refs

    def move(self, s, ssem, vsem, device):
        part = self.pack.at[self.axes.core, s]
        return remote(part, part, self.s.at[ssem], vsem, device)

    def first_copy(self, d, s):
        return self.move(s, 0, self.v1.at[d - 1], self.axes.near(d))

    def second_copy(self, e, d, s):
        return self.move(s, 0, self.v2.at[e, d - 1], self.axes.far(d))

    def pair_copy(self, s):
        return self.move(s, 1, self.vp.at[0], self.axes.sibling)

    def start(self):
        for d in (2, 1, 3):
            self.first_copy(d, self.axes.ctx).start()

    def forward(self):
        for d in (2, 1, 3):
            self.second_copy(0, d, self.axes.ctx).start()
        for e in (1, 3, 2):
            s = self.axes.slice_at(e, 0)
            self.first_copy(e, s).wait_recv()
            for d in (2, 1, 3):
                self.second_copy(e, d, s).start()
            self.pair_copy(s).start()

    def swap(self):
        for e in (0, 1, 3, 2):
            for d in (1, 3, 2):
                s = self.axes.slice_at(e, d)
                self.second_copy(e, d, s).wait_recv()
                self.pair_copy(s).start()

    def finish(self):
        came(self.pack.at[0, 0:15], self.vp.at[0], self.axes.sibling)

    def drain(self):
        for i in range(2):
            sent(self.pack.at[0, 0:15], self.s.at[i], self.axes.sibling)


class SideGather:
    @staticmethod
    def scratch():
        dma = pltpu.SemaphoreType.DMA
        return [dma((4,)), dma((3,)), dma((4, 3)), dma((4,)), dma((2,))]

    def __init__(self, axes, pack, refs):
        self.axes, self.pack = axes, pack
        self.s, self.v1, self.v2, self.vx, self.vp = refs
        self.fetched = lax.rem(axes.x, 2)
        self.missing = 1 - self.fetched

    def move(self, m, s, ssem, vsem, device):
        part = self.pack.at[m, self.axes.core, s]
        return remote(part, part, self.s.at[ssem], vsem, device)

    def first_copy(self, d, s):
        return self.move(self.fetched, s, 0, self.v1.at[d - 1], self.axes.near(d))

    def second_copy(self, e, d, s):
        return self.move(self.fetched, s, 0, self.v2.at[e, d - 1], self.axes.far(d))

    def side_copy(self, s, d):
        return self.move(self.fetched, s, 1, self.vx.at[d], self.axes.beside(self.axes.core))

    def pair_copy(self, m, s):
        return self.move(m, s, 2 + m, self.vp.at[m], self.axes.sibling)

    def start(self):
        for d in (2, 1, 3):
            self.first_copy(d, self.axes.ctx).start()

    def arrived(self, s, d):
        self.side_copy(s, d).start()
        self.pair_copy(self.fetched, s).start()

    def forward(self):
        for d in (2, 1, 3):
            self.second_copy(0, d, self.axes.ctx).start()
        for e in (1, 3, 2):
            s = self.axes.slice_at(e, 0)
            self.first_copy(e, s).wait_recv()
            for d in (2, 1, 3):
                self.second_copy(e, d, s).start()
            self.arrived(s, 0)

    def swap(self):
        for e in (0, 1, 3, 2):
            for d in (1, 3, 2):
                s = self.axes.slice_at(e, d)
                self.second_copy(e, d, s).wait_recv()
                self.arrived(s, d)

    def side(self):
        for d in (0, 1, 3, 2):
            came(self.pack.at[0, 0, 0 : 4 if d else 3], self.vx.at[d], self.axes.sibling)
            for e in (1, 3, 2, 0):
                if d or e:
                    self.pair_copy(self.missing, self.axes.slice_at(e, d)).start()

    def finish(self):
        for m in range(2):
            came(self.pack.at[0, 0, 0:15], self.vp.at[m], self.axes.sibling)

    def drain(self):
        for i in range(4):
            sent(self.pack.at[0, 0, 0:15], self.s.at[i], self.axes.sibling)


class SplitGather:
    @staticmethod
    def scratch():
        dma = pltpu.SemaphoreType.DMA
        return [dma((2,)), dma((2, 3)), dma((2,)), dma((2,))]

    def __init__(self, axes, whole_ref, refs):
        self.axes, self.whole = axes, whole_ref
        self.s, self.v, self.sx, self.vx = refs
        self.odd = lax.rem(axes.x, 2)

    def region(self, k, odd, p):
        if k == 0:
            return self.whole.at[2 * odd, p]
        return self.whole.at[1, p, pl.ds(pl.multiple_of(48 * odd, 16), 48), :]

    def far_copy(self, k, d, p):
        part = self.region(k, self.odd, p)
        return remote(part, part, self.s.at[k], self.v.at[k, d - 1], self.axes.far(d))

    def side_copy(self, k, d, p, odd):
        part = self.region(k, odd, p)
        side = self.axes.core if k == 0 else 1 - self.axes.core
        return remote(part, part, self.sx.at[k], self.vx.at[k], self.axes.beside(side))

    def place(self, d):
        return lax.rem(self.axes.second + 4 - d, 4)

    def start(self, k):
        for d in (2, 1, 3):
            self.far_copy(k, d, self.axes.second).start()

    def forward(self):
        for k in (1, 0):
            for d in (1, 3, 2):
                p = self.place(d)
                self.far_copy(k, d, p).wait_recv()
                self.side_copy(k, d, p, self.odd).start()

    def three(self, k):
        return self.whole.at[0, 0:3] if k == 0 else self.whole.at[1, 0:3, 0:48]

    def wait(self):
        for k in range(2):
            came(self.three(k), self.vx.at[k], self.axes.sibling)

    def drain(self):
        for k in range(2):
            sent(self.three(k), self.s.at[k], self.axes.sibling)
            sent(self.three(k), self.sx.at[k], self.axes.sibling)


class Along:
    @staticmethod
    def scratch():
        return [pltpu.SemaphoreType.DMA((1,)), pltpu.SemaphoreType.DMA((1,))]

    def __init__(self, axes, axis, src, dst, three, refs):
        self.axes, self.src, self.dst, self.three = axes, src, dst, three
        self.ssem, self.vsem = refs
        self.me = axes.second if axis else axes.first
        self.peer = axes.far if axis else axes.near

    def start(self):
        for d in (2, 1, 3):
            remote(
                self.src(lax.rem(self.me + d, 4)), self.dst(self.me), self.ssem.at[0], self.vsem.at[0], self.peer(d)
            ).start()

    def wait(self):
        came(self.three, self.vsem.at[0], self.axes.sibling)

    def drain(self):
        sent(self.three, self.ssem.at[0], self.axes.sibling)


class Reduce:
    @staticmethod
    def scratch(rows, cols, halves):
        dma = pltpu.SemaphoreType.DMA
        part = (rows // 2, cols) if halves else (rows, cols)
        return [
            pltpu.VMEM((4, rows, cols), bf16),
            pltpu.VMEM((2, *part), bf16),
            pltpu.VMEM(part, bf16),
            pltpu.VMEM((4, *part), bf16),
            Along.scratch(),
            dma((4,)),
            dma((4,)),
        ]

    def __init__(self, axes, g, fin, halves, plane, refs):
        self.axes, self.g, self.fin, self.halves = axes, g, fin, halves
        self.plane, self.here = plane, True if plane is None else axes.x == plane
        self.r2, self.h, self.hx, self.x4, along, self.s, self.v = refs
        self.core, self.x = axes.core, axes.x
        self.second = Along(axes, 1, lambda p: g.at[p], lambda p: self.r2.at[p], self.r2.at[0:3], along)

    def pair_copy(self):
        other = 1 - self.core if self.halves else 0
        return remote(self.h.at[other], self.hx, self.s.at[0], self.v.at[0], self.axes.sibling)

    def third_copy(self, d=0):
        slot = self.x4.at[self.x]
        to = lax.rem(self.axes.dp + 2 * d, 8) if self.plane is None else 2 * self.plane + self.core
        return remote(slot, slot, self.s.at[1], self.v.at[1], {"dp": to, "ctx": self.axes.ctx})

    def tell_copy(self, d):
        part = self.fin.at[self.core] if self.halves else self.fin
        peer = {"dp": lax.rem(self.axes.dp + 2 * d, 8), "ctx": self.axes.ctx}
        return remote(part, part, self.s.at[3], self.v.at[3], peer)

    def last_copy(self, half):
        return remote(self.fin.at[half], self.fin.at[half], self.s.at[2], self.v.at[2], self.axes.sibling)

    def start(self):
        self.second.start()

    def second_sum(self):
        self.second.wait()
        me = self.axes.second
        total = self.g[me].astype(f32)
        for d in range(1, 4):
            total = total + self.r2[lax.rem(me + d, 4)].astype(f32)
        total = total.astype(bf16)
        rows = total.shape[0] // 2
        if self.halves:
            self.h[0] = total[0:rows]
            self.h[1] = total[rows:]
        else:
            self.h[0] = total
        self.pair_copy().start()

    def pair_sum(self):
        self.pair_copy().wait_recv()
        mine = self.h[self.core if self.halves else 0]
        self.x4[self.x] = (mine.astype(f32) + self.hx[...].astype(f32)).astype(bf16)

        if self.plane is None:
            for d in (2, 1, 3):
                self.third_copy(d).start()
        else:
            @pl.when(jnp.logical_not(self.here))
            def _():
                self.third_copy().start()

    def third_sum(self):
        came(self.x4.at[0:3], self.v.at[1], self.axes.sibling)
        total = self.x4[0].astype(f32)
        for k in range(1, 4):
            total = total + self.x4[k].astype(f32)
        if self.halves:
            self.fin[self.core] = total.astype(bf16)
            self.last_copy(self.core).start()
        else:
            self.fin[...] = total.astype(bf16)
        if self.plane is not None:
            for d in (2, 1, 3):
                self.tell_copy(d).start()

    def finish(self):
        if self.halves:
            self.last_copy(1 - self.core).wait_recv()

    def collect(self):
        if self.plane is None:
            return

        @pl.when(jnp.logical_not(self.here))
        def _():
            self.tell_copy(1).wait_recv()
            if self.halves:
                self.last_copy(self.core).start()

    def drain(self):
        self.second.drain()
        self.pair_copy().wait_send()
        if self.plane is None:
            sent(self.x4.at[0:3], self.s.at[1], self.axes.sibling)
            return

        @pl.when(self.here)
        def _():
            sent(self.x4.at[0:3], self.s.at[3], self.axes.sibling)

        @pl.when(jnp.logical_not(self.here))
        def _():
            self.third_copy().wait_send()
            if self.halves:
                self.last_copy(1 - self.core).wait_recv()

        if self.halves:
            self.last_copy(self.core).wait_send()


def blocks(size):
    return [(b, min(b + 256, size)) for b in range(0, size, 256)]


def mirror(dst, lows):
    size = dst.shape[0]
    for low, (b, e) in zip(lows, blocks(size)):
        dst[b:size, b:e] = low
        if e < size:
            dst[b:e, e:size] = low[e - b :].T


def diagonal(rows, cols):
    shape = (rows, cols)
    return lax.broadcasted_iota(jnp.int32, shape, 0) == lax.broadcasted_iota(jnp.int32, shape, 1)


def newton_schulz_step(x_ref, a_ref, p_ref, first):
    size, total = x_ref.shape
    parts = blocks(size)
    gram = [
        lax.dot_general(x_ref[b:size, :], x_ref[b:e, :], NT, preferred_element_type=f32) for b, e in parts
    ]
    if first:
        squares = 0.0
        for g, (b, e) in zip(gram, parts):
            squares = squares + jnp.sum(jnp.where(diagonal(e - b, e - b), g[0 : e - b], 0.0))
        scale = 1.0 / (jnp.sqrt(squares) + 1e-07)
        gram = [g * (scale * scale) for g in gram]
    mirror(a_ref, [g.astype(bf16) for g in gram])
    poly = []
    for g, (b, e) in zip(gram, parts):
        value = poly_second * g + poly_third * dot(a_ref[b:size, :], a_ref[:, b:e])
        value = value + jnp.where(diagonal(size - b, e - b), poly_first, 0.0)
        poly.append((value * scale if first else value).astype(bf16))
    mirror(p_ref, poly)
    for at in range(0, total, 512):
        end = min(at + 512, total)
        x_ref[:, at:end] = dot(p_ref[...], x_ref[:, at:end]).astype(bf16)


class Muon:
    @staticmethod
    def scratch(count, rows, cols):
        return [
            pltpu.VMEM((count, rows, cols), bf16),
            pltpu.SemaphoreType.DMA((count,)),
            pltpu.SemaphoreType.DMA((1,)),
            pltpu.SemaphoreType.DMA((1,)),
            pltpu.SemaphoreType.DMA((count,)),
            pltpu.SemaphoreType.DMA((1,)),
            pltpu.SemaphoreType.DMA((1,)),
            pltpu.SemaphoreType.DMA((1,)),
        ]

    def __init__(self, owners, planes, out, t, work, halves, refs):
        self.t, self.halves, self.planes = t, halves, planes
        self.u, self.us, self.uv, self.os, self.ov, self.bs, self.ps, self.pv = refs
        _, self.rows, self.cols = self.u.shape
        x, a, p = work
        self.x = x.at[0 : self.cols, 0 : 16 * self.rows]
        self.a, self.p = a, p
        self.out = out
        self.dp, self.ctx, at_x, self.core = place()
        self.sibling = {"dp": self.dp + 1 - 2 * self.core, "ctx": self.ctx}
        self.owners = [pick(self.core, a, b) for a, b in zip(*owners)]
        self.count = len(planes)
        self.everywhere = planes[0] is None
        self.here = [True if plane is None else at_x == plane for plane in planes]
        self.carries = [halves or self.core == m for m in range(self.count)]
        self.mine = False
        self.which = 0
        for m, owner in enumerate(self.owners):
            mine = self.here[m] & (self.ctx == owner) & self.carries[m]
            self.mine = self.mine | mine
            self.which = self.which + jnp.where(mine, m, 0)

    def up(self, m):
        return remote(
            self.u.at[m], self.t.at[self.ctx], self.us.at[m], self.uv.at[0],
            {"dp": self.dp, "ctx": self.owners[m]},
        )

    def send(self, m):
        @pl.when((self.ctx != self.owners[m]) & self.carries[m])
        def _():
            self.up(m).start()

        @pl.when((self.ctx == self.owners[m]) & self.carries[m])
        def _():
            self.t[self.ctx] = self.u[m]

    def part(self, ref, i, core):
        if self.halves:
            half = self.rows // 2
            return ref.at[i, pl.ds(pl.multiple_of(half * core, 16), half), :]
        return ref.at[i]

    def down(self, peer):
        return remote(
            self.part(self.t, peer, self.core), self.part(self.out, self.which, self.core),
            self.os.at[0], self.ov.at[self.which], {"dp": self.dp, "ctx": peer},
        )

    def pair_copy(self, m, core):
        part = self.part(self.out, m, core)
        return remote(part, part, self.ps.at[0], self.pv.at[0], self.sibling)

    def side_copy(self, m, d):
        part = self.part(self.out, m, self.core)
        peer = {"dp": lax.rem(self.dp + 2 * d, 8), "ctx": self.ctx}
        return remote(part, part, self.bs.at[0], self.ov.at[m], peer)

    def begin(self):
        @pl.when(self.mine)
        def _():
            came(self.t.at[0:15], self.uv.at[0], {"dp": self.dp, "ctx": self.ctx})
            self.x[...] = self.t[...].reshape(16 * self.rows, self.cols).T
            newton_schulz_step(self.x, self.a, self.p, True)

    def go_on(self, steps):
        @pl.when(self.mine)
        def _():
            def step(_, carry):
                newton_schulz_step(self.x, self.a, self.p, False)
                return carry

            lax.fori_loop(0, steps, step, 0)

    def end(self):
        @pl.when(self.mine)
        def _():
            self.t[...] = self.x[...].T.reshape(16, self.rows, self.cols)

            def leave(d, carry):
                self.down(lax.rem(self.ctx + d, 16)).start()
                return carry

            lax.fori_loop(1, 16, leave, 0)
            self.part(self.out, self.which, self.core)[...] = self.part(self.t, self.ctx, self.core)[...]


    def pass_on(self):
        for m, owner in enumerate(self.owners):
            @pl.when(self.here[m] & self.carries[m])
            def _():
                @pl.when(self.ctx != owner)
                def _():
                    self.side_copy(m, 1).wait_recv()

                if not self.everywhere:
                    for d in (2, 1, 3):
                        self.side_copy(m, d).start()
                self.pair_copy(m, self.core).start()

    def collect(self):
        if self.everywhere:
            return
        for m in range(self.count):
            @pl.when(jnp.logical_not(self.here[m]) & self.carries[m])
            def _():
                self.side_copy(m, 1).wait_recv()
                self.pair_copy(m, self.core).start()

    def settle(self):
        if self.halves:
            every = self.part(self.out, pl.ds(0, self.count), 0)
        else:
            every = self.out.at[0]
        came(every, self.pv.at[0], self.sibling)
        sent(every, self.ps.at[0], self.sibling)

        @pl.when(self.mine)
        def _():
            sent(self.part(self.t, pl.ds(0, 15), self.core), self.os.at[0], self.sibling)

        for m, owner in enumerate(self.owners):
            @pl.when(self.here[m] & self.carries[m])
            def _():
                @pl.when(self.ctx != owner)
                def _():
                    self.up(m).wait_send()

                if not self.everywhere:
                    for d in (1, 2, 3):
                        self.side_copy(m, d).wait_send()


def update_of(momentum, gradient):
    return gradient + momentum_decay * (momentum_decay * momentum + gradient)


def dot(a, b):
    return jnp.dot(a, b, preferred_element_type=f32)


def rotated(u, cosine, sine):
    first, second = u[0:32], u[32:64]
    return first * cosine - second * sine, second * cosine + first * sine


def two_part(value):
    high = value.astype(bf16)
    return high, (value - high.astype(f32)).astype(bf16)


VALUE_AT = (128, 192, 64)


def layer_kernel(names, *refs):
    r = types.SimpleNamespace(**dict(zip(names, refs)))
    dp, ctx, x, core = place()
    axes = Axes()
    first, second, sa, sb = axes.first, axes.second, axes.sa, axes.sb
    barrier = greet_all(dp, ctx)
    K, QO, W = r.K, r.QO, r.W
    Q, O = QO.at[0], QO.at[1]
    gather_k = Gather(axes, K, r.gk)
    gather_qo = SideGather(axes, QO, r.gqo)
    gather_w = SplitGather(axes, W, r.gw)

    def lanes_at(p):
        return pl.ds(pl.multiple_of(128 * p, 128), 128)

    def spread(buffer, refs):
        return Along(
            axes, 0, lambda p: buffer.at[:, lanes_at(first)], lambda p: buffer.at[:, lanes_at(p)],
            buffer.at[:, 0:384], refs,
        )

    def deliver(source, target, refs):
        return Along(axes, 0, lambda p: source.at[p], lambda p: target.at[p], target.at[0:3], refs)

    N2, DY, DA, DQ, DKV = r.N2, r.DY, r.DA, r.DQ, r.DKV
    share_n2, share_dy = spread(N2, r.c_n2), spread(DY, r.c_dy)
    share_da, share_dq, share_dkv = spread(DA, r.c_da), spread(DQ, r.c_dq), spread(DKV, r.c_dkv)
    send_n1 = deliver(r.n1s, r.N1, r.c_n1)
    send_ob = deliver(r.obs, r.OB, r.c_ob)
    send_out = deliver(r.outs, r.outr, r.c_out)
    send_dn = deliver(r.dns, r.dnr, r.c_dn)
    send_gain = deliver(r.gps, r.gpr, r.c_gain)

    fin_f = r.fin_f
    ff = [Reduce(axes, r.fg.at[m], fin_f.at[m], True, PLANES_FF[m], r.rf[m]) for m in range(3)]
    sum_q = Reduce(axes, r.qg, r.fin_q, False, None, r.rq)
    sum_o = Reduce(axes, r.og, r.fin_o, False, None, r.ro)
    sum_k = Reduce(axes, r.kg, r.fin_k, False, None, r.rk)
    work = (r.nx, r.na, r.np)
    m_ff = Muon(OWNERS_FF, PLANES_FF, r.o_ff, r.whole, work, True, r.mf)
    m_sq = Muon(OWNERS_SQ, PLANES_SQ, r.o_sq, r.whole.at[:, 0:48], work, False, r.ms)
    m_kv = Muon(OWNERS_KV, PLANES_KV, r.o_kv, r.kv_whole, (r.nx, r.ka, r.kp), False, r.mk)

    def grouped(buffer, value):
        for s in range(16):
            a, b = pick(core, s % 4, s // 4), pick(core, s // 4, s % 4)
            buffer[a, pl.ds(pl.multiple_of(48 * b, 16), 48), :] = value[48 * s : 48 * s + 48]

    pad_sq, pad_kv, tile = r.pad_sq, r.pad_kv, r.tile
    pad_sq[...] = jnp.zeros_like(pad_sq)
    pad_kv[...] = jnp.zeros_like(pad_kv)
    tile[...] = jnp.zeros_like(tile)
    tile[64:66, 0:36] = r.gains[...]
    pad_kv[0, 0:36, 128:256] = tile[...].T[0:36, :]
    for m in range(2):
        pad_sq[m, 0:36, 0:576] = r.w_square[:, m, :]
        pad_kv[m, 0:36, 0:192] = r.w_kv[:, m, :]
        K[m, ctx] = pad_kv[m].astype(bf16)
    for half in range(2):
        for m in range(2):
            QO[m, half, ctx] = pad_sq[m, :, 384 * half : 384 * half + 384].astype(bf16)
    W[0, second] = r.w_gate_up[0].astype(bf16)
    W[1, second] = r.w_gate_up[1].astype(bf16)
    W[2, second] = r.w_down[...].astype(bf16)
    pl.semaphore_wait(barrier, 19)
    gather_k.start()
    gather_qo.start()
    gather_w.start(1)
    DY[:, lanes_at(first)] = r.cotangent[...]

    spread_in, spread_out = r.E, r.ET
    row = lax.broadcasted_iota(jnp.int32, (768, 1), 0)
    step = jnp.zeros((768, 1), jnp.int32)
    for t in range(1, 16):
        step = step + (row >= 48 * t).astype(jnp.int32)
    home = jnp.where(row - 48 * step < 36, row - 12 * step, -1)
    col = lax.broadcasted_iota(jnp.int32, (768, 576), 1)
    spread_out[...] = (col == home).astype(f32).astype(bf16)

    xT = r.tokens[...].astype(f32)
    r1 = lax.rsqrt(jnp.sum(xT * xT, axis=0, keepdims=True) * (1.0 / 576) + norm_eps)
    hat1 = xT * r1
    r.hat1[...] = hat1
    high, low = two_part(hat1)
    hat1_wide = dot(spread_out[...], high) + dot(spread_out[...], low)
    gather_k.forward()
    gather_qo.forward()
    gather_w.start(0)
    row = lax.broadcasted_iota(jnp.int32, (576, 1), 0)
    step = jnp.zeros((576, 1), jnp.int32)
    for t in range(1, 16):
        step = step + (row >= 36 * t).astype(jnp.int32)
    col = lax.broadcasted_iota(jnp.int32, (576, 768), 1)
    spread_in[...] = (col == row + 12 * step).astype(f32).astype(bf16)
    pos = r.positions[...]
    row = lax.broadcasted_iota(jnp.int32, (32, 128), 0)
    freqs = jnp.zeros((32, 128), f32)
    for i in range(32):
        freqs = jnp.where(row == i, rope_base ** (-2.0 * i / HEAD_WIDTH), freqs)
    angle = freqs * pos.astype(f32)
    cosine, sine = jnp.cos(angle), jnp.sin(angle)
    r.cos[...] = cosine
    r.sin[...] = sine
    gather_k.swap()
    gather_k.finish()

    n1_wide = (hat1_wide * K[0, :, :, 192:193].reshape(768, 1).astype(f32)).astype(bf16)
    n1 = n1_wide.T
    kT = dot(n1, K[0].reshape(768, 256)).T
    vT = dot(n1, K[1].reshape(768, 256)).T
    kv, kvT, QT = r.kv, r.kvT, r.QT
    own = []
    for c in range(3):
        own += rotated(kT[64 * c : 64 * c + 64], cosine, sine)
    own += [vT[128:192], vT[0:128]]
    kv[ctx] = jnp.concatenate(own, axis=0).T.astype(bf16)

    def slice_of(a, b):
        return a * sa + b * sb

    def reach(a):
        return a * sa + 3 * sb

    def kv_near(d):
        return remote(kv.at[ctx], kv.at[ctx], r.ks.at[0], r.kr.at[ctx], axes.near(d))

    def kv_far(src, e, d):
        return remote(kv.at[src], kv.at[src], r.ks.at[0], r.kr.at[src], axes.far(d))

    def kv_arrive(src):
        remote(kv.at[src], kv.at[src], r.ks.at[0], r.kr.at[src], axes.sibling).wait_recv()

    def near_wanted(d):
        return reach(lax.rem(first + d, 4)) > ctx

    def far_wanted(src, d):
        return slice_of(first, lax.rem(second + d, 4)) > src

    for d in (2, 1, 3):
        @pl.when(near_wanted(d))
        def _():
            kv_near(d).start()

    for d in (2, 1, 3):
        @pl.when(far_wanted(ctx, d))
        def _():
            kv_far(ctx, 0, d).start()

    for i in range(1, 4):
        @pl.when((lax.rem(ctx, 4) + i < 4) & ((core == 1) | (ctx >= 12)))
        def _():
            kv[ctx + i] = jnp.zeros((128, 384), bf16)

    gather_qo.swap()
    for e in (1, 3, 2):
        src = axes.slice_at(e, 0)

        @pl.when(reach(first) > src)
        def _():
            kv_arrive(src)
            for d in (2, 1, 3):
                @pl.when(far_wanted(src, d))
                def _():
                    kv_far(src, e, d).start()

    gather_w.forward()
    gather_qo.side()
    gather_qo.finish()
    QT[...] = jnp.zeros_like(QT)
    qT = [dot(n1, Q[half].reshape(768, 384)).T for half in range(2)]
    for h in range(9):
        c = h // 3
        part = qT[h // 6][64 * (h % 6) : 64 * (h % 6) + 64]
        a, b = rotated(part, cosine, sine)
        lanes = slice(128 * h, 128 * h + 128)
        QT[64 * c : 64 * c + 32, lanes] = (a.astype(bf16).astype(f32) * 0.125).astype(bf16)
        QT[64 * c + 32 : 64 * c + 64, lanes] = (b.astype(bf16).astype(f32) * 0.125).astype(bf16)

    @pl.when(core == 0)
    def _():
        share_dy.start()

    S, eb, tops, top, total, fade, oT = r.S, r.eb, r.tops, r.top, r.total, r.fade, r.oT
    top[...] = jnp.full_like(top, HIDDEN)
    total[...] = jnp.zeros_like(total)
    oT[...] = jnp.zeros_like(oT)
    groups = lax.div(ctx, 4) + 1

    def attend(g, carry):
        for i in range(4):
            j = 4 * g + i

            @pl.when((j < ctx) & (pick(core, g, i) != second))
            def _():
                kv_arrive(j)

        block = kv[pl.ds(4 * g, 4)].reshape(512, 384)
        kvT[g] = block.T
        S[...] = dot(block[:, 0:256], QT[...])
        key = 512 * g + lax.broadcasted_iota(jnp.int32, (512, 128), 0)
        query = 128 * ctx + lax.broadcasted_iota(jnp.int32, (512, 128), 1)
        allowed = (key <= query) & (key >= query - pos)
        for h in range(9):
            lanes = slice(128 * h, 128 * h + 128)
            s = jnp.where(allowed, S[:, lanes], HIDDEN)
            before = top[:, lanes]
            now = jnp.maximum(before, jnp.max(s, axis=0, keepdims=True))
            weights = jnp.exp(s - now)
            damping = jnp.exp(before - now)
            total[:, lanes] = total[:, lanes] * damping + jnp.sum(weights, axis=0, keepdims=True)
            fade[:, lanes] = damping
            top[:, lanes] = now
            tops[g, :, lanes] = now
            eb[g, :, lanes] = weights.astype(bf16)
        oT[...] = oT[...] * fade[...] + dot(kvT[g, 128:384, :], eb[g])
        return carry

    lax.fori_loop(0, groups, attend, 0)
    @pl.when(core == 1)
    def _():
        share_dy.start()

    share = 1.0 / total[...]
    o = r.o
    for h in range(9):
        at_row = VALUE_AT[h // 3]
        lanes = slice(128 * h, 128 * h + 128)
        o[64 * h : 64 * h + 64, :] = oT[at_row : at_row + 64, lanes] * share[:, lanes]
    ob_wide = dot(spread_out[...], o[...].astype(bf16)).astype(bf16)
    ob = ob_wide.T
    mixed = [dot(ob, O[half].reshape(768, 384)).T for half in range(2)]
    hT = r.tokens[...].astype(f32) + jnp.concatenate([mixed[0], mixed[1][0:192]], axis=0)
    r2 = lax.rsqrt(jnp.sum(hT * hT, axis=0, keepdims=True) * (1.0 / 576) + norm_eps)
    hat2 = hT * r2
    gain_cols = dot(spread_in[...], K[0, :, :, 128:256].reshape(768, 128))
    N2[:, lanes_at(first)] = (hat2 * gain_cols[:, 65:66]).astype(bf16)
    share_n2.start()
    r.h[...] = hT
    r.hat2[...] = hat2
    grouped(r.obs, ob_wide)
    r.OB[first] = r.obs[first]
    grouped(r.n1s, n1_wide)
    r.N1[first] = r.n1s[first]
    gather_w.wait()
    share_dy.wait()
    dhid = dot(W[2].reshape(384, 576), DY[...])
    share_n2.wait()

    gate = dot(W[0].reshape(384, 576), N2[...])
    up = dot(W[1].reshape(384, 576), N2[...])
    sig = jax.nn.sigmoid(gate)
    silu = gate * sig
    hid, dgate, dup = r.hid, r.dgate, r.dup
    dgate[...] = (dhid * up * sig * (1.0 + gate * (1.0 - sig))).astype(bf16)
    dup[...] = (dhid * silu).astype(bf16)
    hid[...] = (silu * up).astype(bf16)
    part = lax.dot_general(W[0].reshape(384, 576), dgate[...], TN, preferred_element_type=f32)
    part = part + lax.dot_general(W[1].reshape(384, 576), dup[...], TN, preferred_element_type=f32)
    for p in range(4):
        r.dns[p] = part[:, 128 * p : 128 * p + 128].astype(bf16)
    send_dn.start()
    for m, left, right in ((2, hid, DY), (0, dgate, N2), (1, dup, N2)):
        part = lax.dot_general(left[...], right[...], NT, preferred_element_type=f32).astype(bf16)
        for p in range(4):
            r.fg[m, p] = part[96 * p : 96 * p + 96]
        ff[m].start()
    part = lax.dot_general(W[2].reshape(384, 576), hid[...], TN, preferred_element_type=f32)
    for p in range(4):
        r.outs[p] = part[:, 128 * p : 128 * p + 128].astype(bf16)

    send_dn.wait()
    dn2T = r.dns[first].astype(f32)
    for d in range(1, 4):
        dn2T = dn2T + r.dnr[lax.rem(first + d, 4)].astype(f32)
    hat2 = r.hat2[...]
    shaped = dn2T * gain_cols[:, 65:66]
    mean = jnp.sum(shaped * hat2, axis=0, keepdims=True) * (1.0 / 576)
    dhT = r.cotangent[...].astype(f32) + r2 * (shaped - hat2 * mean)
    r.dhT[...] = dhT
    gain_two = jnp.sum(dn2T * hat2, axis=1, keepdims=True)
    daT = dhT.astype(bf16)
    DA[:, lanes_at(first)] = daT
    send_ob.start()
    share_da.start()
    send_n1.start()
    dob_wide = dot(O[0].reshape(768, 384), daT[0:384]) + dot(O[1, :, :, 0:192].reshape(768, 192), daT[384:576])
    dobT = dot(spread_in[...], dob_wide.astype(bf16))
    dO, dQ, delta = r.dO, oT, r.delta
    dO[...] = jnp.zeros_like(dO)
    dQ[...] = jnp.zeros_like(dQ)
    for h in range(9):
        at_row = VALUE_AT[h // 3]
        lanes = slice(128 * h, 128 * h + 128)
        part = dobT[64 * h : 64 * h + 64]
        dO[at_row : at_row + 64, lanes] = part.astype(bf16)
        delta[:, lanes] = jnp.sum(part * o[64 * h : 64 * h + 64, :], axis=0, keepdims=True)

    dkv_out, dkv_in, dOg = r.dkv_out, r.dkv_in, r.dOg

    def dkv_far(j, a, b):
        device = {"dp": dp, "ctx": ctx + (b - second) * sb}
        return remote(dkv_out.at[j], dkv_in.at[second, a], r.ds1.at[0], r.dr1.at[second, a], device)

    def attend_back(g, carry):
        factor = jnp.exp(tops[g] - top[...]) / total[...]
        dOg[...] = (dO[...].astype(f32) * factor).astype(bf16)
        block = kv[pl.ds(4 * g, 4)].reshape(512, 384)
        S[...] = dot(block[:, 128:384], dOg[...])
        inner = delta[...] * factor
        dv = lax.dot_general(eb[g], dOg[...], NT, preferred_element_type=f32)
        for h in range(9):
            lanes = slice(128 * h, 128 * h + 128)
            eb[g, :, lanes] = (eb[g, :, lanes].astype(f32) * (S[:, lanes] - inner[:, lanes])).astype(bf16)
        dk = lax.dot_general(eb[g], QT[...], NT, preferred_element_type=f32)
        dQ[...] = dQ[...] + dot(kvT[g, 0:256, :], eb[g])
        out = jnp.concatenate([dk[:, 0:128], dk[:, 128:256] + dv[:, 0:128], dv[:, 128:256]], axis=1)
        dkv_out[pl.ds(4 * g, 4)] = out.astype(bf16).reshape(4, 128, 384)
        for i in range(4):
            j = 4 * g + i
            a, b = pick(core, i, g), pick(core, g, i)

            @pl.when((j < ctx) & (b != second))
            def _():
                dkv_far(j, a, b).start()

        return carry

    lax.fori_loop(0, groups, attend_back, 0)
    def gathered_rows(buffer):
        return jnp.concatenate([buffer[p] for p in range(4)], axis=1)

    def gradient(rows, columns):
        return lax.dot_general(rows, columns, NT, preferred_element_type=f32)

    def send_ff(m, momentum):
        @pl.when(ff[m].here)
        def _():
            ff[m].third_sum()
            ff[m].finish()
            for half in range(2):
                rows = slice(48 * half, 48 * half + 48)
                m_ff.u[m, rows] = update_of(momentum[rows, :], fin_f[m, half].astype(f32)).astype(bf16)
            m_ff.send(m)

    def send_sq(m, reduced):
        @pl.when(reduced.here)
        def _():
            reduced.third_sum()
            m_sq.u[m] = update_of(pad_sq[m, :, 0:576], reduced.fin[...].astype(f32)).astype(bf16)
            m_sq.send(m)

    cosine, sine = r.cos[...], r.sin[...]
    dqT = r.dqT
    for h in range(9):
        c = h // 3
        lanes = slice(128 * h, 128 * h + 128)
        a, b = rotated(dQ[64 * c : 64 * c + 64, lanes] * 0.125, cosine, -sine)
        dqT[64 * h : 64 * h + 32, :] = a.astype(bf16)
        dqT[64 * h + 32 : 64 * h + 64, :] = b.astype(bf16)
    DQ[:, lanes_at(first)] = dqT[...]
    share_dq.start()
    dn1_wide = dot(Q[0].reshape(768, 384), dqT[0:384]) + dot(Q[1, :, :, 0:192].reshape(768, 192), dqT[384:576])
    ff[2].second_sum()
    ff[0].second_sum()
    ff[2].pair_sum()
    ff[1].second_sum()
    ff[0].pair_sum()
    ff[1].pair_sum()
    send_ff(2, r.mom_down)
    send_ff(0, r.mom_gate_up.at[0])
    send_ff(1, r.mom_gate_up.at[1])
    mid, mid_in, own_sum = r.mid, r.mid_in, r.own_sum

    def dkv_near(d):
        return remote(mid.at[d - 1], mid_in.at[d - 1], r.ds2.at[0], r.dr2.at[d - 1], axes.near(d))

    for e in (2, 1, 3, 0):
        a = lax.rem(first + e, 4)
        target = slice_of(a, second)
        own_sum[...] = jnp.zeros_like(own_sum)

        @pl.when(target <= ctx)
        def _():
            own_sum[...] = dkv_out[target].astype(f32)

        for k in range(1, 4):
            b = lax.rem(second + k, 4)

            @pl.when(target < slice_of(first, b))
            def _():
                remote(
                    dkv_in.at[b, a], dkv_in.at[b, a], r.ds1.at[0], r.dr1.at[b, a], axes.sibling
                ).wait_recv()
                own_sum[...] += dkv_in[b, a].astype(f32)

        if e:
            @pl.when(reach(first) > target)
            def _():
                mid[e - 1] = own_sum[...].astype(bf16)
                dkv_near(e).start()

    send_ob.wait()
    share_da.wait()
    part = gradient(gathered_rows(r.OB), DA[...]).astype(bf16)
    for p in range(4):
        r.og[p] = part[48 * p : 48 * p + 48]
    sum_o.start()
    send_n1.wait()
    share_dq.wait()
    n1_rows = gathered_rows(r.N1)
    part = gradient(n1_rows, DQ[...]).astype(bf16)
    for p in range(4):
        r.qg[p] = part[48 * p : 48 * p + 48]
    sum_q.start()
    for d in range(1, 4):
        @pl.when(reach(lax.rem(first + 4 - d, 4)) > ctx)
        def _():
            dkv_near(d).wait_recv()
            own_sum[...] += mid_in[d - 1].astype(f32)

    dkvT = own_sum[...].T
    dk = []
    for c in range(3):
        dk += rotated(dkvT[64 * c : 64 * c + 64], cosine, -sine)
    dkT = jnp.concatenate(dk, axis=0).astype(bf16)
    dvT = jnp.concatenate([dkvT[256:384], dkvT[192:256]], axis=0).astype(bf16)
    DKV[0:192, lanes_at(first)] = dkT
    DKV[192:384, lanes_at(first)] = dvT
    share_dkv.start()
    dn1_wide = dn1_wide + dot(K[0, :, :, 0:192].reshape(768, 192), dkT) + dot(
        K[1, :, :, 0:192].reshape(768, 192), dvT
    )
    high, low = two_part(dn1_wide)
    dn1T = dot(spread_in[...], high) + dot(spread_in[...], low)
    hat1 = r.hat1[...]
    gain_one = jnp.sum(dn1T * hat1, axis=1, keepdims=True)
    lane = lax.broadcasted_iota(jnp.int32, (576, 128), 1)
    columns = jnp.where(lane == 64, gain_one, jnp.where(lane == 65, gain_two, 0.0)).astype(bf16)
    grouped(r.gps, dot(spread_out[...], columns).astype(bf16))
    send_gain.start()
    shaped = dn1T * gain_cols[:, 64:65]
    mean = jnp.sum(shaped * hat1, axis=0, keepdims=True) * (1.0 / 576)
    r.ginT[...] = (r.dhT[...] + r1 * (shaped - hat1 * mean)).astype(bf16)

    sum_o.second_sum()
    sum_o.pair_sum()
    sum_q.second_sum()
    sum_q.pair_sum()
    pad_kv[0, 0:36, 192:256] = jnp.zeros((36, 64), f32)
    for m in range(2):
        pad_sq[m, 0:36, 0:576] = r.mom_square[:, m, :]
        pad_kv[m, 0:36, 0:192] = r.mom_kv[:, m, :]

    share_dkv.wait()
    part_k = gradient(n1_rows, DKV[0:192, :])
    part_v = gradient(n1_rows, DKV[192:384, :]).astype(bf16)
    send_gain.wait()
    gains_sum = r.gps[first].astype(f32)
    for d in range(1, 4):
        gains_sum = gains_sum + r.gpr[lax.rem(first + d, 4)].astype(f32)
    edge = (jnp.concatenate([part_k[:, 128:192], jnp.zeros((192, 64), f32)], axis=1) + gains_sum).astype(bf16)
    part_k = part_k.astype(bf16)
    kg = r.kg
    for p in range(4):
        rows = slice(48 * p, 48 * p + 48)
        kg[p, :, 0:128] = part_k[rows, 0:128]
        kg[p, :, 128:256] = edge[rows]
        kg[p, :, 256:448] = part_v[rows]
        kg[p, :, 448:512] = jnp.zeros((48, 64), bf16)
    sum_k.start()

    send_sq(1, sum_o)
    send_sq(0, sum_q)
    m_ff.begin()
    sum_k.second_sum()
    sum_k.pair_sum()
    m_ff.go_on(3)
    fin_k, gsend, gain_sums, gain_total = r.fin_k, r.gsend, r.gain_sums, r.gain_total

    @pl.when(sum_k.here)
    def _():
        sum_k.third_sum()
        for m in range(2):
            part = fin_k[:, 256 * m : 256 * m + 192].astype(f32)
            m_kv.u[m] = update_of(pad_kv[m, :, 0:192], part).astype(bf16)
            m_kv.send(m)

        gain_grads = fin_k[:, 128:256].astype(f32).T[64:66, 0:36]
        gain_next = momentum_decay * r.mom_gains[...] + gain_grads
        sums = jnp.sum(gain_next * gain_next, axis=1, keepdims=True)
        gsend[0:2, :] = jnp.broadcast_to(sums, (2, 128))
        gsend[2:8, :] = jnp.zeros((6, 128), f32)
        gain_sums[ctx] = gsend[...]
        for d in range(1, 16):
            remote(
                gsend, gain_sums.at[ctx], r.gs.at[0], r.gv.at[0], {"dp": dp, "ctx": lax.rem(ctx + d, 16)}
            ).start()

    send_out.start()
    m_sq.begin()
    m_sq.go_on(2)
    m_ff.go_on(NS_ITERS - 4)
    m_ff.end()
    m_kv.begin()
    m_kv.go_on(NS_ITERS - 1)
    m_kv.end()
    m_sq.go_on(NS_ITERS - 3)
    m_sq.end()
    came(gain_sums.at[0:15], r.gv.at[0], axes.sibling)
    total_gains = gain_sums[0]
    for k in range(1, 16):
        total_gains = total_gains + gain_sums[k]
    gain_total[...] = total_gains

    send_out.wait()
    total_out = r.h[...] + r.outs[first].astype(f32)
    for d in range(1, 4):
        total_out = total_out + r.outr[lax.rem(first + d, 4)].astype(f32)
    r.outT[...] = total_out.astype(bf16)
    for each in (*ff, sum_o, sum_q, sum_k):
        each.collect()
    m_ff.pass_on()
    m_sq.pass_on()
    m_kv.pass_on()
    m_sq.collect()
    m_kv.collect()
    m_ff.collect()

    sent(gain_sums.at[0:15], r.gs.at[0], axes.sibling)
    m_kv.settle()
    m_sq.settle()
    m_ff.settle()
    for d in range(1, 4):
        @pl.when(near_wanted(d))
        def _():
            kv_near(d).wait_send()

        @pl.when(reach(first) > slice_of(lax.rem(first + d, 4), second))
        def _():
            dkv_near(d).wait_send()

        for e in range(4):
            src = axes.slice_at(e, 0)
            held = True if e == 0 else reach(first) > src

            @pl.when(far_wanted(src, d) & held)
            def _():
                kv_far(src, e, d).wait_send()

    def dkv_gone(j, carry):
        y, z = lax.div(j, 4), lax.rem(j, 4)
        a, b = pick(core, z, y), pick(core, y, z)

        @pl.when(b != second)
        def _():
            dkv_far(j, a, b).wait_send()

        return carry

    lax.fori_loop(0, ctx, dkv_gone, 0)
    for each in (
        *ff, sum_o, sum_q, sum_k, gather_k, gather_qo, gather_w, share_n2, share_dy, share_da, share_dq,
        share_dkv, send_n1, send_ob, send_out, send_dn, send_gain,
    ):
        each.drain()


def whole(memory=pltpu.VMEM):
    return pl.BlockSpec(memory_space=memory)


def run_layer(inputs):
    outs = dict(
        outT=((576, 128), bf16),
        ginT=((576, 128), bf16),
        fin_f=((3, 2, 48, 576), bf16),
        fin_q=((48, 576), bf16),
        fin_o=((48, 576), bf16),
        fin_k=((48, 512), bf16),
        o_ff=((3, 96, 576), bf16),
        o_sq=((2, 48, 576), bf16),
        o_kv=((2, 48, 192), bf16),
        gain_total=((8, 128), f32),
    )
    dma = pltpu.SemaphoreType.DMA
    scratch = dict(
        K=pltpu.VMEM((2, 16, 48, 256), bf16),
        QO=pltpu.VMEM((2, 2, 16, 48, 384), bf16),
        W=pltpu.VMEM((3, 4, 96, 576), bf16),
        pad_sq=pltpu.VMEM((2, 48, 768), f32),
        pad_kv=pltpu.VMEM((2, 48, 256), f32),
        tile=pltpu.VMEM((128, 128), f32),
        E=pltpu.VMEM((576, 768), bf16),
        ET=pltpu.VMEM((768, 576), bf16),
        cos=pltpu.VMEM((32, 128), f32),
        sin=pltpu.VMEM((32, 128), f32),
        kv=pltpu.VMEM((16, 128, 384), bf16),
        kvT=pltpu.VMEM((4, 384, 512), bf16),
        QT=pltpu.VMEM((256, 1152), bf16),
        S=pltpu.VMEM((512, 1152), f32),
        eb=pltpu.VMEM((4, 512, 1152), bf16),
        tops=pltpu.VMEM((4, 1, 1152), f32),
        oT=pltpu.VMEM((256, 1152), f32),
        dO=pltpu.VMEM((256, 1152), bf16),
        dOg=pltpu.VMEM((256, 1152), bf16),
        dkv_out=pltpu.VMEM((16, 128, 384), bf16),
        dkv_in=pltpu.VMEM((4, 4, 128, 384), bf16),
        mid=pltpu.VMEM((3, 128, 384), bf16),
        mid_in=pltpu.VMEM((3, 128, 384), bf16),
        own_sum=pltpu.VMEM((128, 384), f32),
        dqT=pltpu.VMEM((576, 128), bf16),
        DKV=pltpu.VMEM((384, 512), bf16),
        fg=pltpu.VMEM((3, 4, 96, 576), bf16),
        qg=pltpu.VMEM((4, 48, 576), bf16),
        og=pltpu.VMEM((4, 48, 576), bf16),
        kg=pltpu.VMEM((4, 48, 512), bf16),
        gsend=pltpu.VMEM((8, 128), f32),
        nx=pltpu.VMEM((576, 1536), bf16),
        na=pltpu.VMEM((576, 576), bf16),
        np=pltpu.VMEM((576, 576), bf16),
        ka=pltpu.VMEM((192, 192), bf16),
        kp=pltpu.VMEM((192, 192), bf16),
        whole=pltpu.VMEM((16, 96, 576), bf16),
        kv_whole=pltpu.VMEM((16, 48, 192), bf16),
        gain_sums=pltpu.VMEM((16, 8, 128), f32),
        gs=dma((1,)),
        gv=dma((1,)),
        ks=dma((1,)),
        kr=dma((16,)),
        ds1=dma((1,)),
        dr1=dma((4, 4)),
        ds2=dma((1,)),
        dr2=dma((3,)),
        gk=Gather.scratch(),
        gqo=SideGather.scratch(),
        gw=SplitGather.scratch(),
        rf=[Reduce.scratch(96, 576, True) for _ in range(3)],
        rq=Reduce.scratch(48, 576, False),
        ro=Reduce.scratch(48, 576, False),
        rk=Reduce.scratch(48, 512, False),
        mf=Muon.scratch(3, 96, 576),
        ms=Muon.scratch(2, 48, 576),
        mk=Muon.scratch(2, 48, 192),
        top=pltpu.VMEM((1, 1152), f32),
        total=pltpu.VMEM((1, 1152), f32),
        fade=pltpu.VMEM((1, 1152), f32),
        delta=pltpu.VMEM((1, 1152), f32),
        hat1=pltpu.VMEM((576, 128), f32),
        hat2=pltpu.VMEM((576, 128), f32),
        h=pltpu.VMEM((576, 128), f32),
        o=pltpu.VMEM((576, 128), f32),
        dhT=pltpu.VMEM((576, 128), f32),
        N2=pltpu.VMEM((576, 512), bf16),
        DY=pltpu.VMEM((576, 512), bf16),
        DA=pltpu.VMEM((576, 512), bf16),
        DQ=pltpu.VMEM((576, 512), bf16),
        hid=pltpu.VMEM((384, 512), bf16),
        dgate=pltpu.VMEM((384, 512), bf16),
        dup=pltpu.VMEM((384, 512), bf16),
        outs=pltpu.VMEM((4, 576, 128), bf16),
        outr=pltpu.VMEM((4, 576, 128), bf16),
        dns=pltpu.VMEM((4, 576, 128), bf16),
        dnr=pltpu.VMEM((4, 576, 128), bf16),
        n1s=pltpu.VMEM((4, 192, 128), bf16),
        N1=pltpu.VMEM((4, 192, 128), bf16),
        obs=pltpu.VMEM((4, 192, 128), bf16),
        OB=pltpu.VMEM((4, 192, 128), bf16),
        gps=pltpu.VMEM((4, 192, 128), bf16),
        gpr=pltpu.VMEM((4, 192, 128), bf16),
        c_n2=Along.scratch(),
        c_dy=Along.scratch(),
        c_da=Along.scratch(),
        c_dq=Along.scratch(),
        c_dkv=Along.scratch(),
        c_n1=Along.scratch(),
        c_ob=Along.scratch(),
        c_out=Along.scratch(),
        c_dn=Along.scratch(),
        c_gain=Along.scratch(),
    )
    names = [*inputs, *outs, *scratch]
    scratch_list = list(scratch.values())

    def kernel(*refs):
        layer_kernel(names, *refs)

    return pl.pallas_call(
        kernel,
        out_shape=tuple(jax.ShapeDtypeStruct(*o) for o in outs.values()),
        in_specs=[whole()] * len(inputs),
        out_specs=[whole()] * len(outs),
        scratch_shapes=scratch_list,
        compiler_params=pltpu.CompilerParams(
            collective_id=3, has_side_effects=True, vmem_limit_bytes=VMEM_LIMIT
        ),
    )(*inputs.values())


VMEM_LIMIT = 63 * 2**20


def finish_kernel(
    outT, ginT, fin_f, fin_q, fin_o, fin_k, o_ff, o_sq, o_kv, gain_total, w_square, w_kv, w_gate_up, w_down, gains,
    mom_square, mom_kv, mom_gate_up, mom_down, mom_gains,
    out, gin, grad_square, grad_kv, grad_gate_up, grad_down, grad_gains,
    next_square, next_kv, next_gate_up, next_down, next_gains,
    new_square, new_kv, new_gate_up, new_down, new_gains,
):
    shrink = 1.0 - learn_rate * weight_decay
    out[...] = outT[...]
    gin[...] = ginT[...]

    def one(at, grad, width, weight, momentum, ortho, grad_out, next_out, new_out):
        grad_out[at] = grad
        next_out[at] = momentum_decay * momentum[at] + grad
        new_out[at] = shrink * weight[at] - learn_rate * (0.2 * math.sqrt(width)) * ortho

    everything = slice(None)
    for m, fin in enumerate((fin_q, fin_o)):
        one((everything, m, everything), fin[...].astype(f32)[0:36], 576, w_square, mom_square,
            o_sq[m].astype(f32)[0:36], grad_square, next_square, new_square)
    for m in range(2):
        one((everything, m, everything), fin_k[:, 256 * m : 256 * m + 192].astype(f32)[0:36], 576, w_kv, mom_kv,
            o_kv[m].astype(f32)[0:36], grad_kv, next_kv, new_kv)
    for half in range(2):
        rows = slice(48 * half, 48 * half + 48)
        for m in range(2):
            one((m, rows), fin_f[m, half].astype(f32), 1536, w_gate_up, mom_gate_up,
                o_ff[m, rows].astype(f32), grad_gate_up, next_gate_up, new_gate_up)
        one(rows, fin_f[2, half].astype(f32), 1536, w_down, mom_down,
            o_ff[2, rows].astype(f32), grad_down, next_down, new_down)
    gain_grads = fin_k[:, 128:256].astype(f32).T[64:66, 0:36]
    gain_next = momentum_decay * mom_gains[...] + gain_grads
    mean = gain_total[0:2, 0:1] * (1.0 / 576)
    grad_gains[...] = gain_grads
    next_gains[...] = gain_next
    new_gains[...] = gains[...] - gain_rate * gain_next / jnp.sqrt(mean + 1e-06)


def finish(packed, weights, momenta):
    shapes = [jax.ShapeDtypeStruct((576, 128), bf16)] * 2
    shapes += [jax.ShapeDtypeStruct(a.shape, f32) for a in weights] * 3
    return pl.pallas_call(
        finish_kernel,
        out_shape=tuple(shapes),
        in_specs=[whole()] * 20,
        out_specs=[whole()] * 17,
        compiler_params=pltpu.CompilerParams(vmem_limit_bytes=VMEM_LIMIT),
    )(*packed, *weights, *momenta)


def swapped(a):
    return jnp.transpose(a, (1, 0, 2))


def shards(
    tokens, positions, cotangent, w_square, w_kv, w_gate_up, w_down, gains,
    mom_square, mom_kv, mom_gate_up, mom_down, mom_gains,
):
    weights = (swapped(w_square), swapped(w_kv), w_gate_up, w_down, gains)
    momenta = (swapped(mom_square), swapped(mom_kv), mom_gate_up, mom_down, mom_gains)
    inputs = dict(
        tokens=tokens[0].T,
        positions=positions,
        cotangent=cotangent[0].T,
        w_square=weights[0],
        w_kv=weights[1],
        w_gate_up=weights[2],
        w_down=weights[3],
        gains=weights[4],
        mom_square=momenta[0],
        mom_kv=momenta[1],
        mom_gate_up=momenta[2],
        mom_down=momenta[3],
        mom_gains=momenta[4],
    )
    outs = list(finish(run_layer(inputs), weights, momenta))
    outs[0] = outs[0].T[None]
    outs[1] = outs[1].T[None]
    for i in (2, 3, 7, 8, 12, 13):
        outs[i] = swapped(outs[i])
    return tuple(outs)


def solution(mesh):
    return jax.shard_map(
        shards,
        mesh=mesh,
        in_specs=(
            P("dp", "ctx", None),
            P("dp", "ctx"),
            P("dp", "ctx", None),
            P(None, "ctx", None),
            P(None, "ctx", None),
            P(None, "ctx", None),
            P("ctx", None),
            P(None, "ctx"),
            P(None, "ctx", None),
            P(None, "ctx", None),
            P(None, "ctx", None),
            P("ctx", None),
            P(None, "ctx"),
        ),
        out_specs=(
            P("dp", "ctx", None),
            P("dp", "ctx", None),
            *(P(None, "ctx", None), P(None, "ctx", None), P(None, "ctx", None), P("ctx", None), P(None, "ctx")) * 3,
        ),
        check_vma=False,
    )
```
